32 devices in a mesh: groups: 2 (over x), batch: 16 (over z, y, core), feat: 1.
Axes of the slice: x: 2, y: 2, z: 4, core: 2. Of those that a mesh axis runs over, the one named last changes fastest.
Arguments:
- view_one: bfloat16 [6144, 4096], P(('groups', 'batch'), 'feat'), parts along dimension 0, may hold values from -1000 to 1000, as said below
- view_two: bfloat16 [6144, 4096], P(('groups', 'batch'), 'feat'), parts along dimension 0, may hold values from -1000 to 1000
Outputs:
- grad_one: bfloat16 [6144, 4096], P(('groups', 'batch'), 'feat'), parts along dimension 0
- grad_two: bfloat16 [6144, 4096], P(('groups', 'batch'), 'feat'), parts along dimension 0
- loss_value: float32 [2], P('groups'), parts along dimension 0
The draws below stay inside these ranges and needn't reach their ends.
There are 2 independent parts, one for each index of `groups`. The reference program is written for one: setup_inputs(seed, part) draws one part's arguments, and reference() takes and returns one part's arrays. A program takes and returns all parts, laid end to end along the dimension named above; each array names one. Nothing has to cross between parts.
Inputs may be any that keep to these rules, and one draw needn't show every extreme that they name: `view_one`: the two views are projector outputs of the same samples.
All inputs are finite; a program needn't handle non-finite values.
Results may differ from the reference program's by a relative error of at most 0.013.
Values may be sent and summed in bfloat16 or wider, within the bound.
No kernel may reach another device: no remote copies, remote signals or barrier semaphores. Data moves between devices by JAX's collectives and lax.ppermute only.
A program may use at most 128 MiB of HBM per device.

```python
import math
import jax
import jax.numpy as jnp
from jax import lax

D = 4096
SAMPLES = 3072


factor_count = 4


def shared_base(key, loading):
    keys = jax.random.split(key, 6)
    rough = jax.random.normal(keys[0], (SAMPLES, D), jnp.float32)
    col_scale = jnp.exp(jax.random.uniform(keys[2], (1, D), jnp.float32) * math.log(10.0))
    lead = jax.random.normal(keys[3], (SAMPLES, factor_count), jnp.float32)
    load = jax.random.normal(keys[4], (factor_count, D), jnp.float32) * loading
    common = jnp.zeros((SAMPLES, D), jnp.float32)
    for index in range(factor_count):
        common = common + lead[:, index:index + 1] * load[index:index + 1, :]
    shifts = jax.random.normal(keys[5], (2, D), jnp.float32)
    trend = 1.0 + 2.0 * jnp.arange(SAMPLES, dtype=jnp.float32)[:, None] / SAMPLES
    base = col_scale * (rough + common + 2.0 * shifts[0][None, :] + 0.3 * trend * shifts[1][None, :])
    return (base, col_scale)


def noise_level(low, high):
    columns = jnp.arange(D, dtype=jnp.int32)
    half_width = D // 2
    within = (columns % half_width).astype(jnp.float32) / half_width
    whole = columns.astype(jnp.float32) / D
    position = 0.5 * (within + whole)
    return (low + (high - low) * position)[None, :]


def draw_view_one(key, part):
    base, col_scale = shared_base(key, 0.2)
    level = noise_level(0.25, 1.75)
    key = jax.random.fold_in(key, 11)
    noise = jax.random.normal(key, (SAMPLES, D), jnp.float32) * level
    return (base + col_scale * noise).astype(jnp.bfloat16)


def draw_view_two(key, part):
    base, col_scale = shared_base(key, 0.2)
    level = noise_level(0.25, 1.75)
    key = jax.random.fold_in(key, 23)
    noise = jax.random.normal(key, (SAMPLES, D), jnp.float32) * level
    return (base + col_scale * noise).astype(jnp.bfloat16)


def setup_inputs(seed: int = 0, part: int = 0) -> dict:
    streams_of = jax.random.split(jax.random.key(seed), 3)
    own_keys = jax.random.split(jax.random.fold_in(streams_of[2], part), 3)
    return {
        "view_one": draw_view_one(jax.random.fold_in(jax.random.fold_in(streams_of[2], part), 71), part),
        "view_two": draw_view_two(jax.random.fold_in(jax.random.fold_in(streams_of[2], part), 71), part),
    }


off_weight = 0.0051

def normalize(view):
    values = view.astype(jnp.float32)
    mean = lax.optimization_barrier(jnp.sum(values, axis=0)) / SAMPLES
    var = lax.optimization_barrier(jnp.sum(values * values, axis=0)) / SAMPLES - mean * mean
    inv = 1.0 / jnp.sqrt(var + 1e-05)
    return (((values - mean) * inv).astype(jnp.bfloat16), inv)

def finish(back, normed, inv):
    normal_f = normed.astype(jnp.float32)
    sum_back = lax.optimization_barrier(jnp.sum(back, axis=0))
    sum_prod = lax.optimization_barrier(jnp.sum(back * normal_f, axis=0))
    return (inv * (back - sum_back / SAMPLES - normal_f * sum_prod / SAMPLES)).astype(jnp.bfloat16)

def reference(view_one, view_two):
    norm_one, inv_one = normalize(view_one)
    norm_two, inv_two = normalize(view_two)
    summed = lax.dot_general(norm_one, norm_two, (((0,), (0,)), ((), ())), preferred_element_type=jnp.float32)
    corr = summed / SAMPLES
    diag = lax.broadcasted_iota(jnp.int32, (D, D), 0) == lax.broadcasted_iota(jnp.int32, (D, D), 1)
    grad_corr = jnp.where(diag, -2.0 * (1.0 - corr), 2.0 * off_weight * corr).astype(jnp.bfloat16)
    loss = jnp.sum(jnp.where(diag, (1.0 - corr) ** 2, off_weight * corr * corr)) / D
    back_one = jnp.dot(norm_two, grad_corr.T, preferred_element_type=jnp.float32)
    back_two = jnp.dot(norm_one, grad_corr, preferred_element_type=jnp.float32)
    grad_one = finish(back_one, norm_one, inv_one)
    grad_two = finish(back_two, norm_two, inv_two)
    return (grad_one, grad_two, jnp.reshape(loss, (1,)).astype(jnp.float32))
```

```python
import jax
import jax.numpy as jnp
from jax import lax
from jax.sharding import PartitionSpec as P

off_weight = 0.0051
chunks = 8


def local_term(columns, full_two):
    return lax.dot_general(
        columns, full_two, (((0,), (0,)), ((), ())), preferred_element_type=jnp.float32
    )


def tile_grad(summed, row_base, samples):
    corr = summed / samples
    row_ids = row_base + lax.broadcasted_iota(jnp.int32, corr.shape, 0)
    col_ids = lax.broadcasted_iota(jnp.int32, corr.shape, 1)
    diag = row_ids == col_ids
    grad = jnp.where(diag, -2.0 * (1.0 - corr), 2.0 * off_weight * corr).astype(jnp.bfloat16)
    part_loss = jnp.sum(jnp.where(diag, (1.0 - corr) ** 2, off_weight * corr * corr))
    return (grad, part_loss)


def fold_step(columns, full_two, piece):
    contrib = lax.dot_general(
        full_two, piece, (((1,), (1,)), ((), ())), preferred_element_type=jnp.float32
    )
    back_mix = jnp.dot(columns, piece, preferred_element_type=jnp.float32)
    return (contrib, back_mix)


def finish(back, normed, inv, sum_back, sum_prod, samples):
    normal_f = normed.astype(jnp.float32)
    return (inv * (back - sum_back / samples - normal_f * sum_prod / samples)).astype(jnp.bfloat16)


def shards(view_one, view_two):
    rows, half_feat = view_one.shape
    batches = lax.axis_size("batch")
    samples = rows * batches
    values_one = view_one.astype(jnp.float32)
    values_two = view_two.astype(jnp.float32)
    sums = lax.psum(
        (
            jnp.sum(values_one, axis=0),
            jnp.sum(values_one * values_one, axis=0),
            jnp.sum(values_two, axis=0),
            jnp.sum(values_two * values_two, axis=0),
        ),
        "batch",
    )
    mean_one = sums[0] / samples
    mean_two = sums[2] / samples
    inv_one = 1.0 / jnp.sqrt(sums[1] / samples - mean_one * mean_one + 1e-05)
    inv_two = 1.0 / jnp.sqrt(sums[3] / samples - mean_two * mean_two + 1e-05)
    norm_one = ((values_one - mean_one) * inv_one).astype(jnp.bfloat16)
    norm_two = ((values_two - mean_two) * inv_two).astype(jnp.bfloat16)
    full_two = lax.all_gather(norm_two, "feat", axis=1, tiled=True)
    width = full_two.shape[1]
    tile = half_feat // batches
    row_base = lax.axis_index("feat") * half_feat + lax.axis_index("batch") * tile
    summed = lax.psum_scatter(
        local_term(norm_one, full_two), "batch", scatter_dimension=0, tiled=True
    )
    grad, part_loss = tile_grad(summed, row_base, samples)
    back_one, back_mix = fold_step(
        norm_one, full_two, lax.all_gather(grad, "batch", axis=0, tiled=True)
    )
    back_two = lax.psum_scatter(back_mix, "feat", scatter_dimension=1, tiled=True)
    loss = lax.psum(part_loss, ("batch", "feat")) / width
    norm_one_f = norm_one.astype(jnp.float32)
    norm_two_f = norm_two.astype(jnp.float32)
    stats = (
        lax.psum(jnp.sum(back_one, axis=0).astype(jnp.bfloat16), "batch").astype(jnp.float32),
        lax.psum(jnp.sum(back_one * norm_one_f, axis=0).astype(jnp.bfloat16), "batch").astype(
            jnp.float32
        ),
        lax.psum(jnp.sum(back_two, axis=0).astype(jnp.bfloat16), "batch").astype(jnp.float32),
        lax.psum(jnp.sum(back_two * norm_two_f, axis=0).astype(jnp.bfloat16), "batch").astype(
            jnp.float32
        ),
    )
    grad_one = finish(back_one, norm_one, inv_one, stats[0], stats[1], samples)
    grad_two = finish(back_two, norm_two, inv_two, stats[2], stats[3], samples)
    return (grad_one, grad_two, jnp.reshape(loss, (1,)))


def normalize(raw, samples):
    values = raw.astype(jnp.float32)
    mean = jnp.sum(values, axis=0) / samples
    var = jnp.sum(values * values, axis=0) / samples - mean * mean
    inv = 1.0 / jnp.sqrt(var + 1e-05)
    return (((values - mean) * inv).astype(jnp.bfloat16), inv)


def corr_chunk(normed_one, normed_two, row_base, col_base, samples):
    summed = local_term(normed_one, normed_two)
    corr = summed / samples
    row_ids = row_base + lax.broadcasted_iota(jnp.int32, corr.shape, 0)
    col_ids = col_base + lax.broadcasted_iota(jnp.int32, corr.shape, 1)
    diag = row_ids == col_ids
    grad = jnp.where(diag, -2.0 * (1.0 - corr), 2.0 * off_weight * corr).astype(jnp.bfloat16)
    loss = jnp.sum(jnp.where(diag, (1.0 - corr) ** 2, off_weight * corr * corr))
    grad_f = grad.astype(jnp.float32)
    total_one = jnp.sum(normed_one.astype(jnp.float32), axis=0)
    total_two = jnp.sum(normed_two.astype(jnp.float32), axis=0)
    prod = grad_f * summed
    return (
        grad,
        loss,
        jnp.sum(grad_f * total_two[None, :], axis=1),
        jnp.sum(prod, axis=1),
        jnp.sum(grad_f * total_one[:, None], axis=0),
        jnp.sum(prod, axis=0),
    )


def pair_shards(view_one, view_two):
    rows, width = view_one.shape
    batches = lax.axis_size("batch")
    samples = rows * batches
    half = width // 2
    place = lax.axis_index("batch")
    side = place % 2
    first_row = (place // 2) * 2 * rows
    swap = [(i, i ^ 1) for i in range(batches)]

    def mine(both):
        return lax.dynamic_slice_in_dim(both, side * rows, rows, axis=0)

    def theirs(both):
        return lax.dynamic_slice_in_dim(both, (1 - side) * rows, rows, axis=0)

    def pair_rows(full):
        return lax.dynamic_slice_in_dim(full, first_row, 2 * rows, axis=0)

    gathered_one = lax.all_gather(view_one, "batch", axis=0, tiled=True)
    raw_one = lax.dynamic_slice_in_dim(gathered_one, side * half, half, axis=1)
    norm_one, inv_one = normalize(raw_one, samples)
    pair_one = pair_rows(norm_one)
    step = width // chunks
    back_one = jnp.zeros((2 * rows, half), jnp.float32)
    sum_back = jnp.zeros((half,), jnp.float32)
    sum_prod = jnp.zeros((half,), jnp.float32)
    loss = jnp.zeros((), jnp.float32)
    grad_two = []
    for index in range(chunks):
        base = index * step
        raw_two = lax.all_gather(view_two[:, base : base + step], "batch", axis=0, tiled=True)
        norm_two, inv_two = normalize(raw_two, samples)
        pair_two = pair_rows(norm_two)
        grad, part_loss, back_row, prod_row, back_col, prod_col = corr_chunk(
            norm_one, norm_two, side * half, base, samples
        )
        loss = loss + part_loss
        sum_back = sum_back + back_row
        sum_prod = sum_prod + prod_row
        back_one = back_one + lax.dot_general(
            pair_two, grad, (((1,), (1,)), ((), ())), preferred_element_type=jnp.float32
        )
        back_two = jnp.dot(pair_one, grad, preferred_element_type=jnp.float32)
        done_two = inv_two * (
            back_two - back_col / samples - pair_two.astype(jnp.float32) * prod_col / samples
        )
        other = lax.ppermute(theirs(done_two), "batch", swap)
        grad_two.append((mine(done_two) + other).astype(jnp.bfloat16))
    done_one = finish(back_one, pair_one, inv_one, sum_back, sum_prod, samples)
    own = mine(done_one)
    other = lax.ppermute(theirs(done_one), "batch", swap)
    grad_one = jnp.where(
        side == 0,
        jnp.concatenate([own, other], axis=1),
        jnp.concatenate([other, own], axis=1),
    )
    loss = (loss + lax.ppermute(loss, "batch", swap)) / width
    return (grad_one, jnp.concatenate(grad_two, axis=1), jnp.reshape(loss, (1,)))


def solution(mesh):
    placed = (P(("groups", "batch"), "feat"), P(("groups", "batch"), "feat"))
    paired = mesh.shape["feat"] == 1 and mesh.shape["batch"] % 2 == 0
    return jax.shard_map(
        pair_shards if paired else shards,
        mesh=mesh,
        in_specs=placed,
        out_specs=(P(("groups", "batch"), "feat"), P(("groups", "batch"), "feat"), P("groups")),
        check_vma=False,
    )
```

```python
import jax
import jax.numpy as jnp
from jax import lax
from jax.sharding import PartitionSpec as P

off_weight = 0.0051
chunks = 4


def local_term(columns, full_two):
    return lax.dot_general(
        columns, full_two, (((0,), (0,)), ((), ())), preferred_element_type=jnp.float32
    )


def tile_grad(summed, row_base, samples):
    corr = summed / samples
    row_ids = row_base + lax.broadcasted_iota(jnp.int32, corr.shape, 0)
    col_ids = lax.broadcasted_iota(jnp.int32, corr.shape, 1)
    diag = row_ids == col_ids
    grad = jnp.where(diag, -2.0 * (1.0 - corr), 2.0 * off_weight * corr).astype(jnp.bfloat16)
    part_loss = jnp.sum(jnp.where(diag, (1.0 - corr) ** 2, off_weight * corr * corr))
    return (grad, part_loss)


def fold_step(columns, full_two, piece):
    contrib = lax.dot_general(
        full_two, piece, (((1,), (1,)), ((), ())), preferred_element_type=jnp.float32
    )
    back_mix = jnp.dot(columns, piece, preferred_element_type=jnp.float32)
    return (contrib, back_mix)


def finish(back, normed, inv, sum_back, sum_prod, samples):
    normal_f = normed.astype(jnp.float32)
    return (inv * (back - sum_back / samples - normal_f * sum_prod / samples)).astype(jnp.bfloat16)


def shards(view_one, view_two):
    rows, half_feat = view_one.shape
    batches = lax.axis_size("batch")
    samples = rows * batches
    values_one = view_one.astype(jnp.float32)
    values_two = view_two.astype(jnp.float32)
    sums = lax.psum(
        (
            jnp.sum(values_one, axis=0),
            jnp.sum(values_one * values_one, axis=0),
            jnp.sum(values_two, axis=0),
            jnp.sum(values_two * values_two, axis=0),
        ),
        "batch",
    )
    mean_one = sums[0] / samples
    mean_two = sums[2] / samples
    inv_one = 1.0 / jnp.sqrt(sums[1] / samples - mean_one * mean_one + 1e-05)
    inv_two = 1.0 / jnp.sqrt(sums[3] / samples - mean_two * mean_two + 1e-05)
    norm_one = ((values_one - mean_one) * inv_one).astype(jnp.bfloat16)
    norm_two = ((values_two - mean_two) * inv_two).astype(jnp.bfloat16)
    full_two = lax.all_gather(norm_two, "feat", axis=1, tiled=True)
    width = full_two.shape[1]
    tile = half_feat // batches
    row_base = lax.axis_index("feat") * half_feat + lax.axis_index("batch") * tile
    summed = lax.psum_scatter(
        local_term(norm_one, full_two), "batch", scatter_dimension=0, tiled=True
    )
    grad, part_loss = tile_grad(summed, row_base, samples)
    back_one, back_mix = fold_step(
        norm_one, full_two, lax.all_gather(grad, "batch", axis=0, tiled=True)
    )
    back_two = lax.psum_scatter(back_mix, "feat", scatter_dimension=1, tiled=True)
    loss = lax.psum(part_loss, ("batch", "feat")) / width
    norm_one_f = norm_one.astype(jnp.float32)
    norm_two_f = norm_two.astype(jnp.float32)
    stats = (
        lax.psum(jnp.sum(back_one, axis=0).astype(jnp.bfloat16), "batch").astype(jnp.float32),
        lax.psum(jnp.sum(back_one * norm_one_f, axis=0).astype(jnp.bfloat16), "batch").astype(
            jnp.float32
        ),
        lax.psum(jnp.sum(back_two, axis=0).astype(jnp.bfloat16), "batch").astype(jnp.float32),
        lax.psum(jnp.sum(back_two * norm_two_f, axis=0).astype(jnp.bfloat16), "batch").astype(
            jnp.float32
        ),
    )
    grad_one = finish(back_one, norm_one, inv_one, stats[0], stats[1], samples)
    grad_two = finish(back_two, norm_two, inv_two, stats[2], stats[3], samples)
    return (grad_one, grad_two, jnp.reshape(loss, (1,)))


def normalize(raw, samples):
    values = raw.astype(jnp.float32)
    mean = jnp.sum(values, axis=0) / samples
    var = jnp.sum(values * values, axis=0) / samples - mean * mean
    inv = 1.0 / jnp.sqrt(var + 1e-05)
    return (((values - mean) * inv).astype(jnp.bfloat16), inv)


def corr_chunk(normed_one, normed_two, row_base, col_base, samples):
    summed = local_term(normed_one, normed_two)
    corr = summed / samples
    row_ids = row_base + lax.broadcasted_iota(jnp.int32, corr.shape, 0)
    col_ids = col_base + lax.broadcasted_iota(jnp.int32, corr.shape, 1)
    diag = row_ids == col_ids
    grad = jnp.where(diag, -2.0 * (1.0 - corr), 2.0 * off_weight * corr).astype(jnp.bfloat16)
    loss = jnp.sum(jnp.where(diag, (1.0 - corr) ** 2, off_weight * corr * corr))
    grad_f = grad.astype(jnp.float32)
    total_one = jnp.sum(normed_one.astype(jnp.float32), axis=0)
    total_two = jnp.sum(normed_two.astype(jnp.float32), axis=0)
    prod = grad_f * summed
    return (
        grad,
        loss,
        jnp.sum(grad_f * total_two[None, :], axis=1),
        jnp.sum(prod, axis=1),
        jnp.sum(grad_f * total_one[:, None], axis=0),
        jnp.sum(prod, axis=0),
    )


def pair_shards(view_one, view_two):
    rows, width = view_one.shape
    batches = lax.axis_size("batch")
    samples = rows * batches
    half = width // 2
    step = half // chunks
    chips = batches // 2
    side = lax.axis_index("batch") % 2
    swap = [(i, i ^ 1) for i in range(batches)]
    line = chips // 2
    order = [2 * r for r in range(line)] + [2 * r + 1 for r in reversed(range(line))]
    ahead = [
        (2 * order[r] + c, 2 * order[(r + 1) % chips] + c) for r in range(chips) for c in range(2)
    ]
    behind = [(there, here) for here, there in ahead]

    def mine(both, axis=0):
        size = both.shape[axis] // 2
        return lax.dynamic_slice_in_dim(both, side * size, size, axis=axis)

    def theirs(both, axis=0):
        size = both.shape[axis] // 2
        return lax.dynamic_slice_in_dim(both, (1 - side) * size, size, axis=axis)

    def in_order(own, other, axis):
        return jnp.where(
            side == 0,
            jnp.concatenate([own, other], axis=axis),
            jnp.concatenate([other, own], axis=axis),
        )

    def chip_rows(view):
        other = lax.ppermute(theirs(view, 1), "batch", swap)
        return in_order(mine(view, 1), other, 0)

    def ring(block, after):
        if after is not None:
            block, _ = lax.optimization_barrier((block, after))
        up = down = block
        parts = [block]
        for hop in range(1, chips // 2):
            up = lax.ppermute(up, "batch", ahead)
            down = lax.ppermute(down, "batch", behind)
            parts += [up, down]
        parts.append(lax.ppermute(up[:rows], "batch", ahead))
        parts.append(lax.ppermute(down[rows:], "batch", behind))
        return (parts, (parts[3], parts[4]))

    block_one = chip_rows(view_one)
    block_two = chip_rows(view_two)
    after = None
    norms, invs = [], []
    for index in range(chunks):
        piece = block_one[:, index * step : (index + 1) * step]
        parts, after = ring(piece, after)
        norm, inv = normalize(jnp.concatenate(parts, axis=0), samples)
        norms.append(norm)
        invs.append(inv)
    norm_one = jnp.concatenate(norms, axis=1)
    inv_one = jnp.concatenate(invs)
    pair_one = norm_one[: 2 * rows]
    back_one = jnp.zeros((2 * rows, half), jnp.float32)
    sum_back = jnp.zeros((half,), jnp.float32)
    sum_prod = jnp.zeros((half,), jnp.float32)
    loss = jnp.zeros((), jnp.float32)
    grad_own, grad_far = [], []
    for index in range(chunks):
        piece = block_two[:, index * step : (index + 1) * step]
        parts, after = ring(piece, after)
        own_norm, own_inv = normalize(jnp.concatenate(parts, axis=0), samples)
        far_norm = lax.ppermute(own_norm, "batch", swap)
        far_inv = lax.ppermute(own_inv, "batch", swap)
        for norm_two, inv_two, column_half, grads in (
            (own_norm, own_inv, side, grad_own),
            (far_norm, far_inv, 1 - side, grad_far),
        ):
            base = column_half * half + index * step
            pair_two = norm_two[: 2 * rows]
            grad, part_loss, back_row, prod_row, back_col, prod_col = corr_chunk(
                norm_one, norm_two, side * half, base, samples
            )
            loss = loss + part_loss
            sum_back = sum_back + back_row
            sum_prod = sum_prod + prod_row
            back_one = back_one + lax.dot_general(
                pair_two, grad, (((1,), (1,)), ((), ())), preferred_element_type=jnp.float32
            )
            back_two = jnp.dot(pair_one, grad, preferred_element_type=jnp.float32)
            grads.append(
                inv_two
                * (back_two - back_col / samples - pair_two.astype(jnp.float32) * prod_col / samples)
            )
    done_one = finish(back_one, pair_one, inv_one, sum_back, sum_prod, samples)
    grad_one = in_order(mine(done_one), lax.ppermute(theirs(done_one), "batch", swap), 1)
    columns_own, columns_far = [], []
    for index in range(chunks):
        sent_far = lax.ppermute(theirs(grad_far[index]), "batch", swap)
        sent_own = lax.ppermute(theirs(grad_own[index]), "batch", swap)
        columns_own.append((mine(grad_own[index]) + sent_far).astype(jnp.bfloat16))
        columns_far.append((mine(grad_far[index]) + sent_own).astype(jnp.bfloat16))
    grad_two = in_order(
        jnp.concatenate(columns_own, axis=1), jnp.concatenate(columns_far, axis=1), 1
    )
    loss = (loss + lax.ppermute(loss, "batch", swap)) / width
    return (grad_one, grad_two, jnp.reshape(loss, (1,)))


def solution(mesh):
    placed = (P(("groups", "batch"), "feat"), P(("groups", "batch"), "feat"))
    paired = mesh.shape["feat"] == 1 and mesh.shape["batch"] % 4 == 0
    return jax.shard_map(
        pair_shards if paired else shards,
        mesh=mesh,
        in_specs=placed,
        out_specs=(P(("groups", "batch"), "feat"), P(("groups", "batch"), "feat"), P("groups")),
        check_vma=False,
    )
```

```python
import functools

import jax
import jax.numpy as jnp
from jax import lax
from jax.experimental import pallas as pl
from jax.experimental.pallas import tpu as pltpu
from jax.sharding import PartitionSpec as P

off_weight = 0.0051
chunks = 4
lanes = 256
tile_rows = 512
spare = 16
vmem = 44 * 1024 * 1024


def local_term(columns, full_two):
    return lax.dot_general(
        columns, full_two, (((0,), (0,)), ((), ())), preferred_element_type=jnp.float32
    )


def tile_grad(summed, row_base, samples):
    corr = summed / samples
    row_ids = row_base + lax.broadcasted_iota(jnp.int32, corr.shape, 0)
    col_ids = lax.broadcasted_iota(jnp.int32, corr.shape, 1)
    diag = row_ids == col_ids
    grad = jnp.where(diag, -2.0 * (1.0 - corr), 2.0 * off_weight * corr).astype(jnp.bfloat16)
    part_loss = jnp.sum(jnp.where(diag, (1.0 - corr) ** 2, off_weight * corr * corr))
    return (grad, part_loss)


def fold_step(columns, full_two, piece):
    contrib = lax.dot_general(
        full_two, piece, (((1,), (1,)), ((), ())), preferred_element_type=jnp.float32
    )
    back_mix = jnp.dot(columns, piece, preferred_element_type=jnp.float32)
    return (contrib, back_mix)


def finish(back, normed, inv, sum_back, sum_prod, samples):
    normal_f = normed.astype(jnp.float32)
    return (inv * (back - sum_back / samples - normal_f * sum_prod / samples)).astype(jnp.bfloat16)


def shards(view_one, view_two):
    rows, half_feat = view_one.shape
    batches = lax.axis_size("batch")
    samples = rows * batches
    values_one = view_one.astype(jnp.float32)
    values_two = view_two.astype(jnp.float32)
    sums = lax.psum(
        (
            jnp.sum(values_one, axis=0),
            jnp.sum(values_one * values_one, axis=0),
            jnp.sum(values_two, axis=0),
            jnp.sum(values_two * values_two, axis=0),
        ),
        "batch",
    )
    mean_one = sums[0] / samples
    mean_two = sums[2] / samples
    inv_one = 1.0 / jnp.sqrt(sums[1] / samples - mean_one * mean_one + 1e-05)
    inv_two = 1.0 / jnp.sqrt(sums[3] / samples - mean_two * mean_two + 1e-05)
    norm_one = ((values_one - mean_one) * inv_one).astype(jnp.bfloat16)
    norm_two = ((values_two - mean_two) * inv_two).astype(jnp.bfloat16)
    full_two = lax.all_gather(norm_two, "feat", axis=1, tiled=True)
    width = full_two.shape[1]
    tile = half_feat // batches
    row_base = lax.axis_index("feat") * half_feat + lax.axis_index("batch") * tile
    summed = lax.psum_scatter(
        local_term(norm_one, full_two), "batch", scatter_dimension=0, tiled=True
    )
    grad, part_loss = tile_grad(summed, row_base, samples)
    back_one, back_mix = fold_step(
        norm_one, full_two, lax.all_gather(grad, "batch", axis=0, tiled=True)
    )
    back_two = lax.psum_scatter(back_mix, "feat", scatter_dimension=1, tiled=True)
    loss = lax.psum(part_loss, ("batch", "feat")) / width
    norm_one_f = norm_one.astype(jnp.float32)
    norm_two_f = norm_two.astype(jnp.float32)
    stats = (
        lax.psum(jnp.sum(back_one, axis=0).astype(jnp.bfloat16), "batch").astype(jnp.float32),
        lax.psum(jnp.sum(back_one * norm_one_f, axis=0).astype(jnp.bfloat16), "batch").astype(
            jnp.float32
        ),
        lax.psum(jnp.sum(back_two, axis=0).astype(jnp.bfloat16), "batch").astype(jnp.float32),
        lax.psum(jnp.sum(back_two * norm_two_f, axis=0).astype(jnp.bfloat16), "batch").astype(
            jnp.float32
        ),
    )
    grad_one = finish(back_one, norm_one, inv_one, stats[0], stats[1], samples)
    grad_two = finish(back_two, norm_two, inv_two, stats[2], stats[3], samples)
    return (grad_one, grad_two, jnp.reshape(loss, (1,)))


def norm_kernel(samples, turned, count, *refs):
    parts = refs[:count]
    if turned:
        norm_ref, pair_ref, stat_ref = refs[-3:]
    else:
        norm_ref, stat_ref = refs[-2:]
    total = jnp.zeros((1, lanes), jnp.float32)
    square = jnp.zeros((1, lanes), jnp.float32)
    for part in parts:
        values = part[...].astype(jnp.float32)
        total += jnp.sum(values, axis=0, keepdims=True)
        square += jnp.sum(values * values, axis=0, keepdims=True)
    mean = total / samples
    inv = 1.0 / jnp.sqrt(square / samples - mean * mean + 1e-05)
    norm_total = jnp.zeros((1, lanes), jnp.float32)
    start = 0
    late = []
    for place, part in enumerate(parts):
        norm = ((part[...].astype(jnp.float32) - mean) * inv).astype(jnp.bfloat16)
        norm_total += jnp.sum(norm.astype(jnp.float32), axis=0, keepdims=True)
        if not turned:
            norm_ref[start : start + part.shape[0], :] = norm
            start += part.shape[0]
            continue
        if place == 0:
            pair_ref[: part.shape[0], :] = norm
        if place >= count - 2:
            late.append(norm)
            if place < count - 1:
                continue
            norm = jnp.concatenate(late, axis=0)
        norm_ref[:, start : start + norm.shape[0]] = norm.T
        start += norm.shape[0]
    row = lax.broadcasted_iota(jnp.int32, (8, lanes), 0)
    stat_ref[...] = jnp.where(row == 0, inv, jnp.where(row == 1, norm_total, 0.0))
    if turned:
        pair_ref[parts[0].shape[0] :, :] = total_rows(norm_total)


def total_rows(total):
    high = total.astype(jnp.bfloat16).astype(jnp.float32)
    row = lax.broadcasted_iota(jnp.int32, (spare, total.shape[1]), 0)
    both = jnp.where(row == 0, high, jnp.where(row == 1, total - high, 0.0))
    return both.astype(jnp.bfloat16)


def norm_one_chunk(parts, held, index, half, samples):
    step = parts[0].shape[1]
    rows = parts[0].shape[0]
    tiles = step // lanes
    place = lambda tile: (0, index * tiles + tile)
    any_spec = pl.BlockSpec(memory_space=pl.ANY)
    count = len(parts)
    return pl.pallas_call(
        functools.partial(norm_kernel, samples, True, count),
        grid=(tiles,),
        in_specs=[pl.BlockSpec((part.shape[0], lanes), lambda tile: (0, tile)) for part in parts]
        + [any_spec] * len(held),
        out_specs=[
            pl.BlockSpec((lanes, samples), lambda tile: (index * tiles + tile, 0)),
            pl.BlockSpec((rows + spare, lanes), place),
            pl.BlockSpec((8, lanes), place),
        ],
        out_shape=[
            jax.ShapeDtypeStruct((half, samples), jnp.bfloat16),
            jax.ShapeDtypeStruct((rows + spare, half), jnp.bfloat16),
            jax.ShapeDtypeStruct((8, half), jnp.float32),
        ],
        input_output_aliases={count + k: k for k in range(len(held))},
        compiler_params=pltpu.CompilerParams(vmem_limit_bytes=vmem),
        cost_estimate=pl.CostEstimate(
            flops=10 * samples * step, bytes_accessed=4 * samples * step, transcendentals=0
        ),
        name="norm_one_chunk",
    )(*parts, *held)


def norm_two_chunk(parts, samples):
    step = parts[0].shape[1]
    return pl.pallas_call(
        functools.partial(norm_kernel, samples, False, len(parts)),
        grid=(step // lanes,),
        in_specs=[pl.BlockSpec((part.shape[0], lanes), lambda tile: (0, tile)) for part in parts],
        out_specs=[
            pl.BlockSpec((samples, lanes), lambda tile: (0, tile)),
            pl.BlockSpec((8, lanes), lambda tile: (0, tile)),
        ],
        out_shape=[
            jax.ShapeDtypeStruct((samples, step), jnp.bfloat16),
            jax.ShapeDtypeStruct((8, step), jnp.float32),
        ],
        compiler_params=pltpu.CompilerParams(vmem_limit_bytes=vmem),
        cost_estimate=pl.CostEstimate(
            flops=10 * samples * step, bytes_accessed=4 * samples * step, transcendentals=0
        ),
        name="norm_two_chunk",
    )(*parts)


def corr_kernel(samples, diag_at, begins, fresh, opens, closes, *refs):
    one_ref, pair_ref, two_ref, stat_ref = refs[:4]
    rest = list(refs[4:])
    acc_in = None if begins else rest.pop(0)
    loss_in = None if begins else rest.pop(0)
    back_in = None if opens else rest.pop(0)
    acc_out, loss_out, back_out, ext_ref, back_ref = rest
    rows = pair_ref.shape[0] - spare
    tile = pl.program_id(0)

    @pl.when(tile == 0)
    def _():
        ext_ref[:rows, :] = two_ref[:rows, :]
        ext_ref[rows:, :] = total_rows(stat_ref[1:2, :])
        back_ref[...] = jnp.zeros_like(back_ref) if opens else back_in[...]
        loss_out[...] = jnp.zeros_like(loss_out) if begins else loss_in[...]

    summed = jnp.dot(one_ref[...], two_ref[...], preferred_element_type=jnp.float32)
    corr = summed * (1.0 / samples)
    grad = (2.0 * off_weight) * corr
    loss = off_weight * corr * corr
    if diag_at is not None:
        ahead = lax.broadcasted_iota(jnp.int32, corr.shape, 1) - lax.broadcasted_iota(
            jnp.int32, corr.shape, 0
        )
        diag = ahead == tile * corr.shape[0] - diag_at
        grad = jnp.where(diag, 2.0 * corr - 2.0, grad)
        loss = jnp.where(diag, (1.0 - corr) ** 2, loss)
    grad = grad.astype(jnp.bfloat16)
    prod = grad.astype(jnp.float32) * summed
    height, width = summed.shape
    loss_out[...] += jnp.sum(loss.reshape(height // 8, 8, width), axis=0)
    folded = prod[:, :128]
    for start in range(128, width, 128):
        folded += prod[:, start : start + 128]
    prod_row = jnp.sum(folded.T, axis=0, keepdims=True)
    back = lax.dot_general(
        ext_ref[...], grad, (((1,), (1,)), ((), ())), preferred_element_type=jnp.float32
    )
    acc_out[...] = back if fresh else acc_in[...] + back
    row = lax.broadcasted_iota(jnp.int32, (8, height), 0)
    acc_out[rows + 8 :, :] += jnp.where(row == 0, prod_row, 0.0)
    back_ref[...] += jnp.dot(pair_ref[...], grad, preferred_element_type=jnp.float32)
    back_ref[rows + 8 :, :] += jnp.sum(prod.reshape(height // 8, 8, width), axis=0)

    @pl.when(tile == pl.num_programs(0) - 1)
    def _():
        if not closes:
            back_out[...] = back_ref[...]
        else:
            sum_back = (back_ref[rows : rows + 1, :] + back_ref[rows + 1 : rows + 2, :]) / samples
            sum_prod = jnp.sum(back_ref[rows + 8 :, :], axis=0, keepdims=True) / samples
            normal = two_ref[:rows, :].astype(jnp.float32)
            back_out[...] = stat_ref[0:1, :] * (back_ref[:rows, :] - sum_back - normal * sum_prod)


def corr_piece(norm_one, pair_one, norm_two, stat_two, acc, back, fresh, piece, pieces, diag_at):
    half, samples = norm_one.shape
    width = norm_two.shape[1]
    ext = pair_one.shape[0]
    rows = ext - spare
    tiles = half // pieces // tile_rows
    first = piece * tiles
    opens, closes = piece == 0, piece == pieces - 1
    whole = lambda shape: pl.BlockSpec(shape, lambda tile: (0, 0))
    acc_spec = pl.BlockSpec((ext, tile_rows), lambda tile: (0, first + tile))
    operands = [norm_one, pair_one, norm_two, stat_two]
    in_specs = [
        pl.BlockSpec((tile_rows, samples), lambda tile: (first + tile, 0)),
        acc_spec,
        whole((samples, width)),
        whole((8, width)),
    ]
    aliases = {}
    if acc is not None:
        aliases = {4: 0, 5: 1}
        operands += list(acc)
        in_specs += [acc_spec, whole((8, width))]
    if not opens:
        operands.append(back)
        in_specs.append(whole((ext, width)))
    back_shape = (rows if closes else ext, width)
    if diag_at is not None:
        diag_at = diag_at - piece * tiles * tile_rows
    return pl.pallas_call(
        functools.partial(corr_kernel, samples, diag_at, acc is None, fresh, opens, closes),
        grid=(tiles,),
        in_specs=in_specs,
        out_specs=[acc_spec, whole((8, width)), whole(back_shape)],
        out_shape=[
            jax.ShapeDtypeStruct((ext, half), jnp.float32),
            jax.ShapeDtypeStruct((8, width), jnp.float32),
            jax.ShapeDtypeStruct(back_shape, jnp.float32),
        ],
        scratch_shapes=[
            pltpu.VMEM((ext, width), jnp.bfloat16),
            pltpu.VMEM((ext, width), jnp.float32),
        ],
        input_output_aliases=aliases,
        compiler_params=pltpu.CompilerParams(vmem_limit_bytes=vmem),
        cost_estimate=pl.CostEstimate(
            flops=2 * tiles * tile_rows * width * (samples + 2 * ext),
            bytes_accessed=2 * samples * (tiles * tile_rows + width),
            transcendentals=0,
        ),
        name="corr_piece",
    )(*operands)


def pair_shards(view_one, view_two):
    rows, width = view_one.shape
    batches = lax.axis_size("batch")
    samples = rows * batches
    half = width // 2
    step = half // chunks
    chips = batches // 2
    side = lax.axis_index("batch") % 2
    swap = [(i, i ^ 1) for i in range(batches)]
    line = chips // 2
    order = [2 * r for r in range(line)] + [2 * r + 1 for r in reversed(range(line))]
    ahead = [
        (2 * order[r] + c, 2 * order[(r + 1) % chips] + c) for r in range(chips) for c in range(2)
    ]
    behind = [(there, here) for here, there in ahead]

    def mine(both, axis=0):
        size = both.shape[axis] // 2
        return lax.dynamic_slice_in_dim(both, side * size, size, axis=axis)

    def theirs(both, axis=0):
        size = both.shape[axis] // 2
        return lax.dynamic_slice_in_dim(both, (1 - side) * size, size, axis=axis)

    def swapped(value):
        return lax.ppermute(value, "batch", swap)

    def in_order(own, other, axis):
        return jnp.where(
            side == 0,
            jnp.concatenate([own, other], axis=axis),
            jnp.concatenate([other, own], axis=axis),
        )

    def chip_rows(view):
        return in_order(mine(view, 1), swapped(theirs(view, 1)), 0)

    blocks = (chip_rows(view_one), chip_rows(view_two))
    hops = chips // 2
    flows = [(view, index) for view in range(2) for index in range(chunks)]
    slots = {}
    for flow in range(len(flows)):
        for hop in range(hops):
            slots[hops * flow + flow % 2 + 2 * hop] = (flow, hop)
    last_hop = {hops * flow + flow % 2 + 2 * (hops - 1): flow for flow in range(len(flows))}
    ends = {}
    arrived = {}
    held = []
    state = {"acc": None, "back": None, "token": None}
    grad_own, grad_far = [], []
    work = []
    pieces = 2

    def run_piece(norm, stat, piece, diag_at, grads):
        acc, loss, back = corr_piece(
            held[0],
            held[1],
            norm,
            stat,
            state["acc"],
            state["back"],
            not grads and diag_at == 0,
            piece,
            pieces,
            diag_at,
        )
        state["acc"], state["back"], state["token"] = (acc, loss), back, loss
        if piece == pieces - 1:
            grads.append(back)

    def take(flow):
        view, index = flows[flow]
        if view == 0:
            held[:] = norm_one_chunk(arrived[flow], held, index, half, samples)
            state["token"] = held[2]
            return
        norm, stat = norm_two_chunk(arrived[flow], samples)
        state["token"] = stat
        far_norm, far_stat = swapped(norm), swapped(stat)
        for piece in range(pieces):
            work.append(functools.partial(run_piece, norm, stat, piece, index * step, grad_own))
        for piece in range(pieces):
            work.append(functools.partial(run_piece, far_norm, far_stat, piece, None, grad_far))

    for slot in range(max(slots) + 2):
        if slot in slots:
            flow, hop = slots[slot]
            view, index = flows[flow]
            if hop == 0:
                block = blocks[view][:, index * step : (index + 1) * step]
                ends[flow] = (block, block)
                arrived[flow] = [block]
            up, down = ends[flow]
            if hop == hops - 1:
                up, down = up[:rows], down[rows:]
            if state["token"] is not None:
                up, down, _ = lax.optimization_barrier((up, down, state["token"]))
            up = lax.ppermute(up, "batch", ahead)
            down = lax.ppermute(down, "batch", behind)
            ends[flow] = (up, down)
            arrived[flow] += [up, down]
        if slot - 1 in last_hop:
            take(last_hop[slot - 1])
        if work:
            work.pop(0)()
    while work:
        work.pop(0)()

    acc, loss = state["acc"]
    pair_f = held[1][: 2 * rows].astype(jnp.float32)
    sum_back = acc[2 * rows] + acc[2 * rows + 1]
    sum_prod = acc[2 * rows + 8]
    done_one = (
        held[2][0] * (acc[: 2 * rows] - sum_back / samples - pair_f * sum_prod / samples)
    ).astype(jnp.bfloat16)
    grad_one = in_order(mine(done_one), swapped(theirs(done_one)), 1)
    columns_own, columns_far = [], []
    for own, far in zip(grad_own, grad_far):
        columns_own.append((mine(own) + swapped(theirs(far))).astype(jnp.bfloat16))
        columns_far.append((mine(far) + swapped(theirs(own))).astype(jnp.bfloat16))
    grad_two = in_order(
        jnp.concatenate(columns_own, axis=1), jnp.concatenate(columns_far, axis=1), 1
    )
    loss = jnp.sum(loss)
    loss = (loss + swapped(loss)) / width
    return (grad_one, grad_two, jnp.reshape(loss, (1,)))


def solution(mesh):
    placed = (P(("groups", "batch"), "feat"), P(("groups", "batch"), "feat"))
    paired = mesh.shape["feat"] == 1 and mesh.shape["batch"] % 4 == 0
    return jax.shard_map(
        pair_shards if paired else shards,
        mesh=mesh,
        in_specs=placed,
        out_specs=(P(("groups", "batch"), "feat"), P(("groups", "batch"), "feat"), P("groups")),
        check_vma=False,
    )
```

```python
import functools

import jax
import jax.numpy as jnp
from jax import lax
from jax.experimental import pallas as pl
from jax.experimental.pallas import tpu as pltpu
from jax.sharding import PartitionSpec as P

off_weight = 0.0051
parts = (3, 3, 2)
lanes = 256
tile_rows = 512
spare = 16
vmem = 40 * 1024 * 1024


def local_term(columns, full_two):
    return lax.dot_general(
        columns, full_two, (((0,), (0,)), ((), ())), preferred_element_type=jnp.float32
    )


def tile_grad(summed, row_base, samples):
    corr = summed / samples
    row_ids = row_base + lax.broadcasted_iota(jnp.int32, corr.shape, 0)
    col_ids = lax.broadcasted_iota(jnp.int32, corr.shape, 1)
    diag = row_ids == col_ids
    grad = jnp.where(diag, -2.0 * (1.0 - corr), 2.0 * off_weight * corr).astype(jnp.bfloat16)
    part_loss = jnp.sum(jnp.where(diag, (1.0 - corr) ** 2, off_weight * corr * corr))
    return (grad, part_loss)


def fold_step(columns, full_two, piece):
    contrib = lax.dot_general(
        full_two, piece, (((1,), (1,)), ((), ())), preferred_element_type=jnp.float32
    )
    back_mix = jnp.dot(columns, piece, preferred_element_type=jnp.float32)
    return (contrib, back_mix)


def finish(back, normed, inv, sum_back, sum_prod, samples):
    normal_f = normed.astype(jnp.float32)
    return (inv * (back - sum_back / samples - normal_f * sum_prod / samples)).astype(jnp.bfloat16)


def shards(view_one, view_two):
    rows, half_feat = view_one.shape
    batches = lax.axis_size("batch")
    samples = rows * batches
    values_one = view_one.astype(jnp.float32)
    values_two = view_two.astype(jnp.float32)
    sums = lax.psum(
        (
            jnp.sum(values_one, axis=0),
            jnp.sum(values_one * values_one, axis=0),
            jnp.sum(values_two, axis=0),
            jnp.sum(values_two * values_two, axis=0),
        ),
        "batch",
    )
    mean_one = sums[0] / samples
    mean_two = sums[2] / samples
    inv_one = 1.0 / jnp.sqrt(sums[1] / samples - mean_one * mean_one + 1e-05)
    inv_two = 1.0 / jnp.sqrt(sums[3] / samples - mean_two * mean_two + 1e-05)
    norm_one = ((values_one - mean_one) * inv_one).astype(jnp.bfloat16)
    norm_two = ((values_two - mean_two) * inv_two).astype(jnp.bfloat16)
    full_two = lax.all_gather(norm_two, "feat", axis=1, tiled=True)
    width = full_two.shape[1]
    tile = half_feat // batches
    row_base = lax.axis_index("feat") * half_feat + lax.axis_index("batch") * tile
    summed = lax.psum_scatter(
        local_term(norm_one, full_two), "batch", scatter_dimension=0, tiled=True
    )
    grad, part_loss = tile_grad(summed, row_base, samples)
    back_one, back_mix = fold_step(
        norm_one, full_two, lax.all_gather(grad, "batch", axis=0, tiled=True)
    )
    back_two = lax.psum_scatter(back_mix, "feat", scatter_dimension=1, tiled=True)
    loss = lax.psum(part_loss, ("batch", "feat")) / width
    norm_one_f = norm_one.astype(jnp.float32)
    norm_two_f = norm_two.astype(jnp.float32)
    stats = (
        lax.psum(jnp.sum(back_one, axis=0).astype(jnp.bfloat16), "batch").astype(jnp.float32),
        lax.psum(jnp.sum(back_one * norm_one_f, axis=0).astype(jnp.bfloat16), "batch").astype(
            jnp.float32
        ),
        lax.psum(jnp.sum(back_two, axis=0).astype(jnp.bfloat16), "batch").astype(jnp.float32),
        lax.psum(jnp.sum(back_two * norm_two_f, axis=0).astype(jnp.bfloat16), "batch").astype(
            jnp.float32
        ),
    )
    grad_one = finish(back_one, norm_one, inv_one, stats[0], stats[1], samples)
    grad_two = finish(back_two, norm_two, inv_two, stats[2], stats[3], samples)
    return (grad_one, grad_two, jnp.reshape(loss, (1,)))


def total_rows(total):
    high = total.astype(jnp.bfloat16).astype(jnp.float32)
    row = lax.broadcasted_iota(jnp.int32, (spare, total.shape[1]), 0)
    both = jnp.where(row == 0, high, jnp.where(row == 1, total - high, 0.0))
    return both.astype(jnp.bfloat16)


def norm_kernel(rows, turned, place_ref, raw_ref, norm_ref, *rest):
    samples = raw_ref.shape[0]
    starts = range(0, samples, rows)
    total = jnp.zeros((1, lanes), jnp.float32)
    square = jnp.zeros((1, lanes), jnp.float32)
    for start in starts:
        values = raw_ref[start : start + rows, :].astype(jnp.float32)
        total += jnp.sum(values, axis=0, keepdims=True)
        square += jnp.sum(values * values, axis=0, keepdims=True)
    mean = total / samples
    inv = 1.0 / jnp.sqrt(square / samples - mean * mean + 1e-05)
    norm_total = jnp.zeros((1, lanes), jnp.float32)

    def normed(values):
        return ((values.astype(jnp.float32) - mean) * inv).astype(jnp.bfloat16)

    for start in starts:
        norm = normed(raw_ref[start : start + rows, :])
        norm_total += jnp.sum(norm.astype(jnp.float32), axis=0, keepdims=True)
        if turned:
            norm_ref[:, start : start + rows] = norm.T
        else:
            norm_ref[start : start + rows, :] = norm
    stat_ref = rest[-1]
    row = lax.broadcasted_iota(jnp.int32, (8, lanes), 0)
    stat_ref[...] = jnp.where(row == 0, inv, jnp.where(row == 1, norm_total, 0.0))
    if turned:
        pair_ref = rest[0]
        first = pl.multiple_of(place_ref[1] * rows, 16)
        pair_ref[:rows, :] = normed(raw_ref[pl.ds(first, rows), :])
        pair_ref[rows:, :] = total_rows(norm_total)


def norm_half(place, raw, rows, turned):
    samples, width = raw.shape
    half = width // 2
    tiles = half // lanes
    column = lambda tile, place_ref: (0, tile)
    if turned:
        norm_spec = pl.BlockSpec((lanes, samples), lambda tile, place_ref: (tile, 0))
        pair_specs = [pl.BlockSpec((rows + spare, lanes), column)]
        norm_shape = (half, samples)
        pair_shapes = [jax.ShapeDtypeStruct((rows + spare, half), jnp.bfloat16)]
    else:
        norm_spec = pl.BlockSpec((samples, lanes), column)
        pair_specs, pair_shapes = [], []
        norm_shape = (samples, half)
    return pl.pallas_call(
        functools.partial(norm_kernel, rows, turned),
        grid_spec=pltpu.PrefetchScalarGridSpec(
            num_scalar_prefetch=1,
            grid=(tiles,),
            in_specs=[
                pl.BlockSpec(
                    (samples, lanes), lambda tile, place_ref: (0, place_ref[0] * tiles + tile)
                )
            ],
            out_specs=[norm_spec] + pair_specs + [pl.BlockSpec((8, lanes), column)],
        ),
        out_shape=[jax.ShapeDtypeStruct(norm_shape, jnp.bfloat16)]
        + pair_shapes
        + [jax.ShapeDtypeStruct((8, half), jnp.float32)],
        compiler_params=pltpu.CompilerParams(vmem_limit_bytes=vmem),
        cost_estimate=pl.CostEstimate(
            flops=10 * samples * half, bytes_accessed=4 * samples * half, transcendentals=0
        ),
        name="norm_one" if turned else "norm_two",
    )(place, raw)


def corr_kernel(samples, diag_at, begins, *refs):
    place_ref, one_ref, pair_ref, two_ref, stat_ref = refs[:5]
    rest = list(refs[5:])
    acc_in = None if begins else rest.pop(0)
    loss_in = None if begins else rest.pop(0)
    acc_out, loss_out, keep_out, send_out, ext_ref, grad_ref, prod_ref, back_ref = rest
    ext = pair_ref.shape[0]
    rows = ext - spare
    tile = pl.program_id(0)
    first = pl.multiple_of(place_ref[1] * rows, 16)

    @pl.when(tile == 0)
    def _():
        ext_ref[:rows, :] = two_ref[pl.ds(first, rows), :]
        ext_ref[rows:, :] = total_rows(stat_ref[1:2, :])
        prod_ref[...] = jnp.zeros_like(prod_ref)
        loss_out[...] = jnp.zeros_like(loss_out) if begins else loss_in[...]

    summed = jnp.dot(one_ref[...], two_ref[...], preferred_element_type=jnp.float32)
    height, width = summed.shape
    grad = summed * (2.0 * off_weight / samples)
    loss = summed * summed
    if diag_at is not None:
        ahead = lax.broadcasted_iota(jnp.int32, summed.shape, 1) - lax.broadcasted_iota(
            jnp.int32, summed.shape, 0
        )
        diag = ahead == tile * height - diag_at
        grad = jnp.where(diag, summed * (2.0 / samples) - 2.0, grad)
        loss = jnp.where(diag, (samples - summed) ** 2 * (1.0 / off_weight), loss)
    grad = grad.astype(jnp.bfloat16)
    grad_ref[pl.ds(tile * height, height), :] = grad
    prod = grad.astype(jnp.float32) * summed

    def fold(value):
        folded = value[:, :128]
        for start in range(128, width, 128):
            folded += value[:, start : start + 128]
        return folded

    loss_out[...] += fold(jnp.sum(loss.reshape(height // 8, 8, width), axis=0))
    prod_ref[...] += jnp.sum(prod.reshape(height // 8, 8, width), axis=0)
    prod_row = jnp.sum(fold(prod).T, axis=0, keepdims=True)
    back = lax.dot_general(
        ext_ref[...], grad, (((1,), (1,)), ((), ())), preferred_element_type=jnp.float32
    )
    acc_out[...] = back if begins else acc_in[...] + back
    row = lax.broadcasted_iota(jnp.int32, (8, height), 0)
    acc_out[rows + 8 :, :] += jnp.where(row == 0, prod_row, 0.0)

    @pl.when(tile == pl.num_programs(0) - 1)
    def _():
        back_two = jnp.dot(pair_ref[...], grad_ref[...], preferred_element_type=jnp.float32)
        sum_back = (back_two[rows : rows + 1, :] + back_two[rows + 1 : rows + 2, :]) / samples
        sum_prod = jnp.sum(prod_ref[...], axis=0, keepdims=True) / samples
        normal = ext_ref[:rows, :].astype(jnp.float32)
        back_ref[...] = stat_ref[0:1, :] * (back_two[:rows, :] - sum_back - normal * sum_prod)
        side = place_ref[0]
        keep_out[...] = back_ref[pl.ds(pl.multiple_of(side * (rows // 2), 8), rows // 2), :]
        send_out[...] = back_ref[pl.ds(pl.multiple_of((1 - side) * (rows // 2), 8), rows // 2), :]


def corr_half(place, norm_one, pair_one, norm_two, stat_two, acc, diag_at):
    half, samples = norm_one.shape
    width = norm_two.shape[1]
    ext = pair_one.shape[0]
    rows = ext - spare
    tiles = half // tile_rows

    def whole(shape):
        return pl.BlockSpec(shape, lambda tile: (0, 0), pipeline_mode=pl.Buffered(1))

    def kept(shape):
        return pl.BlockSpec(shape, lambda tile: (0, 0))

    acc_spec = pl.BlockSpec((ext, tile_rows), lambda tile: (0, tile))
    operands = [place, norm_one, pair_one, norm_two, stat_two]
    in_specs = [
        pl.BlockSpec(memory_space=pltpu.SMEM),
        pl.BlockSpec((tile_rows, samples), lambda tile: (tile, 0)),
        whole((ext, half)),
        whole((samples, width)),
        whole((8, width)),
    ]
    aliases = {}
    if acc is not None:
        aliases = {5: 0, 6: 1}
        operands += list(acc)
        in_specs += [acc_spec, kept((8, 128))]
    return pl.pallas_call(
        functools.partial(corr_kernel, samples, diag_at, acc is None),
        grid=(tiles,),
        in_specs=in_specs,
        out_specs=[acc_spec, kept((8, 128)), kept((rows // 2, width)), kept((rows // 2, width))],
        out_shape=[
            jax.ShapeDtypeStruct((ext, half), jnp.float32),
            jax.ShapeDtypeStruct((8, 128), jnp.float32),
            jax.ShapeDtypeStruct((rows // 2, width), jnp.float32),
            jax.ShapeDtypeStruct((rows // 2, width), jnp.float32),
        ],
        scratch_shapes=[
            pltpu.VMEM((ext, width), jnp.bfloat16),
            pltpu.VMEM((half, width), jnp.bfloat16),
            pltpu.VMEM((8, width), jnp.float32),
            pltpu.VMEM((rows, width), jnp.float32),
        ],
        input_output_aliases=aliases,
        compiler_params=pltpu.CompilerParams(vmem_limit_bytes=vmem),
        cost_estimate=pl.CostEstimate(
            flops=2 * half * width * (samples + 2 * ext),
            bytes_accessed=2 * samples * (half + width),
            transcendentals=0,
        ),
        name="corr_half",
    )(*operands)


def place_kernel(side_ref, keep_ref, get_ref, *refs):
    refs[-1][...] = (keep_ref[...] + get_ref[...]).astype(jnp.bfloat16)


def place_two(side, keep, get, placed, far, first, width):
    rows, step = keep.shape
    half = width // 2

    def column(tile, side_ref):
        side = 1 - side_ref[0] if far else side_ref[0]
        return (0, (side * half + first) // lanes + tile)

    block = pl.BlockSpec((rows, lanes), lambda tile, side_ref: (0, tile))
    held = [] if placed is None else [placed]
    return pl.pallas_call(
        place_kernel,
        grid_spec=pltpu.PrefetchScalarGridSpec(
            num_scalar_prefetch=1,
            grid=(step // lanes,),
            in_specs=[block, block] + [pl.BlockSpec(memory_space=pl.ANY)] * len(held),
            out_specs=pl.BlockSpec((rows, lanes), column),
        ),
        out_shape=jax.ShapeDtypeStruct((rows, width), jnp.bfloat16),
        input_output_aliases={3: 0} if held else {},
        cost_estimate=pl.CostEstimate(
            flops=rows * step, bytes_accessed=10 * rows * step, transcendentals=0
        ),
        name="place_two",
    )(side, keep, get, *held)


def finish_kernel(samples, side_ref, acc_ref, pair_ref, stat_ref, keep_out, send_out, done_ref):
    rows = done_ref.shape[0]
    sum_back = (acc_ref[rows : rows + 1, :] + acc_ref[rows + 1 : rows + 2, :]) / samples
    sum_prod = acc_ref[rows + 8 : rows + 9, :] / samples
    normal = pair_ref[:rows, :].astype(jnp.float32)
    done_ref[...] = stat_ref[0:1, :] * (acc_ref[:rows, :] - sum_back - normal * sum_prod)
    side = side_ref[0]
    keep = done_ref[pl.ds(pl.multiple_of(side * (rows // 2), 8), rows // 2), :]
    send = done_ref[pl.ds(pl.multiple_of((1 - side) * (rows // 2), 8), rows // 2), :]
    keep_out[...] = keep.astype(jnp.bfloat16)
    send_out[...] = send.astype(jnp.bfloat16)


def finish_one(side, acc, pair, stat, samples):
    ext, half = acc.shape
    rows = ext - spare
    block = lambda height: pl.BlockSpec((height, tile_rows), lambda tile: (0, tile))
    return pl.pallas_call(
        functools.partial(finish_kernel, samples),
        grid=(half // tile_rows,),
        in_specs=[pl.BlockSpec(memory_space=pltpu.SMEM), block(ext), block(ext), block(8)],
        out_specs=[block(rows // 2), block(rows // 2)],
        out_shape=[jax.ShapeDtypeStruct((rows // 2, half), jnp.bfloat16)] * 2,
        scratch_shapes=[pltpu.VMEM((rows, tile_rows), jnp.float32)],
        cost_estimate=pl.CostEstimate(
            flops=5 * rows * half, bytes_accessed=8 * rows * half, transcendentals=0
        ),
        name="finish_one",
    )(side, acc, pair, stat)


def join_kernel(side_ref, keep_ref, get_ref, out_ref):
    @pl.when(pl.program_id(0) == 0)
    def _():
        out_ref[...] = keep_ref[...]

    @pl.when(pl.program_id(0) == 1)
    def _():
        out_ref[...] = get_ref[...]


def join_one(side, keep, get):
    rows, half = keep.shape
    block = pl.BlockSpec((rows, half), lambda tile, side_ref: (0, 0))
    column = lambda tile, side_ref: (0, side_ref[0] + tile - 2 * side_ref[0] * tile)
    return pl.pallas_call(
        join_kernel,
        grid_spec=pltpu.PrefetchScalarGridSpec(
            num_scalar_prefetch=1,
            grid=(2,),
            in_specs=[block, block],
            out_specs=pl.BlockSpec((rows, half), column),
        ),
        out_shape=jax.ShapeDtypeStruct((rows, 2 * half), jnp.bfloat16),
        cost_estimate=pl.CostEstimate(
            flops=0, bytes_accessed=8 * rows * half, transcendentals=0
        ),
        name="join_one",
    )(side, keep, get)


def pair_shards(view_one, view_two):
    rows, width = view_one.shape
    batches = lax.axis_size("batch")
    samples = rows * batches
    half = width // 2
    index = lax.axis_index("batch")
    place = jnp.stack([index % 2, index // 2]).astype(jnp.int32)
    swap = [(i, i ^ 1) for i in range(batches)]

    def swapped(value):
        return lax.ppermute(value, "batch", swap)

    def gathered(block):
        return lax.all_gather(block, "batch", axis=0, tiled=True)

    steps = [half * part // sum(parts) for part in parts]
    firsts = [sum(steps[:count]) for count in range(len(parts))]

    def columns(count):
        first, last = firsts[count], firsts[count] + steps[count]
        return jnp.concatenate(
            [view_two[:, side * half + first : side * half + last] for side in range(2)], axis=1
        )

    raw_one = gathered(view_one)
    block, raw_one = lax.optimization_barrier((columns(0), raw_one))
    raw_two = gathered(block)
    one = norm_half(place, raw_one, 2 * rows, True)
    acc = None
    grad_two = None
    for count, (step, first) in enumerate(zip(steps, firsts)):
        if count + 1 < len(parts):
            block = columns(count + 1)
            if acc is None:
                block, raw_two, *one = lax.optimization_barrier((block, raw_two, *one))
            else:
                block, raw_two, *acc = lax.optimization_barrier((block, raw_two, *acc))
            raw_next = gathered(block)
        else:
            raw_two, grad_two, *acc = lax.optimization_barrier((raw_two, grad_two, *acc))
        norm_one, pair_one, stat_one = one
        norm, stat = norm_half(place, raw_two, 2 * rows, False)
        far_norm, far_stat = swapped(norm), swapped(stat)
        *acc, keep_own, send_own = corr_half(place, norm_one, pair_one, norm, stat, acc, first)
        *acc, keep_far, send_far = corr_half(
            place, norm_one, pair_one, far_norm, far_stat, acc, None
        )
        get_own, get_far = swapped(send_far), swapped(send_own)
        grad_two = place_two(place, keep_own, get_own, grad_two, False, first, width)
        grad_two = place_two(place, keep_far, get_far, grad_two, True, first, width)
        raw_two = raw_next
    acc, loss = acc
    keep, send = finish_one(place, acc, pair_one, stat_one, samples)
    grad_one = join_one(place, keep, swapped(send))
    loss = jnp.sum(loss) * (off_weight / (samples * samples))
    loss = (loss + swapped(loss)) / width
    return (grad_one, grad_two, jnp.reshape(loss, (1,)))


def solution(mesh):
    placed = (P(("groups", "batch"), "feat"), P(("groups", "batch"), "feat"))
    paired = mesh.shape["feat"] == 1 and mesh.shape["batch"] % 4 == 0
    return jax.shard_map(
        pair_shards if paired else shards,
        mesh=mesh,
        in_specs=placed,
        out_specs=(P(("groups", "batch"), "feat"), P(("groups", "batch"), "feat"), P("groups")),
        check_vma=False,
    )
```

```python
import functools

import jax
import jax.numpy as jnp
from jax import lax
from jax.experimental import pallas as pl
from jax.experimental.pallas import tpu as pltpu
from jax.sharding import PartitionSpec as P

off_weight = 0.0051
chunks = 4
lanes = 256
tile_rows = 512
strip = 32
spare = 16
vmem = 44 * 1024 * 1024


def local_term(columns, full_two):
    return lax.dot_general(
        columns, full_two, (((0,), (0,)), ((), ())), preferred_element_type=jnp.float32
    )


def tile_grad(summed, row_base, samples):
    corr = summed / samples
    row_ids = row_base + lax.broadcasted_iota(jnp.int32, corr.shape, 0)
    col_ids = lax.broadcasted_iota(jnp.int32, corr.shape, 1)
    diag = row_ids == col_ids
    grad = jnp.where(diag, -2.0 * (1.0 - corr), 2.0 * off_weight * corr).astype(jnp.bfloat16)
    part_loss = jnp.sum(jnp.where(diag, (1.0 - corr) ** 2, off_weight * corr * corr))
    return (grad, part_loss)


def fold_step(columns, full_two, piece):
    contrib = lax.dot_general(
        full_two, piece, (((1,), (1,)), ((), ())), preferred_element_type=jnp.float32
    )
    back_mix = jnp.dot(columns, piece, preferred_element_type=jnp.float32)
    return (contrib, back_mix)


def finish(back, normed, inv, sum_back, sum_prod, samples):
    normal_f = normed.astype(jnp.float32)
    return (inv * (back - sum_back / samples - normal_f * sum_prod / samples)).astype(jnp.bfloat16)


def shards(view_one, view_two):
    rows, half_feat = view_one.shape
    batches = lax.axis_size("batch")
    samples = rows * batches
    values_one = view_one.astype(jnp.float32)
    values_two = view_two.astype(jnp.float32)
    sums = lax.psum(
        (
            jnp.sum(values_one, axis=0),
            jnp.sum(values_one * values_one, axis=0),
            jnp.sum(values_two, axis=0),
            jnp.sum(values_two * values_two, axis=0),
        ),
        "batch",
    )
    mean_one = sums[0] / samples
    mean_two = sums[2] / samples
    inv_one = 1.0 / jnp.sqrt(sums[1] / samples - mean_one * mean_one + 1e-05)
    inv_two = 1.0 / jnp.sqrt(sums[3] / samples - mean_two * mean_two + 1e-05)
    norm_one = ((values_one - mean_one) * inv_one).astype(jnp.bfloat16)
    norm_two = ((values_two - mean_two) * inv_two).astype(jnp.bfloat16)
    full_two = lax.all_gather(norm_two, "feat", axis=1, tiled=True)
    width = full_two.shape[1]
    tile = half_feat // batches
    row_base = lax.axis_index("feat") * half_feat + lax.axis_index("batch") * tile
    summed = lax.psum_scatter(
        local_term(norm_one, full_two), "batch", scatter_dimension=0, tiled=True
    )
    grad, part_loss = tile_grad(summed, row_base, samples)
    back_one, back_mix = fold_step(
        norm_one, full_two, lax.all_gather(grad, "batch", axis=0, tiled=True)
    )
    back_two = lax.psum_scatter(back_mix, "feat", scatter_dimension=1, tiled=True)
    loss = lax.psum(part_loss, ("batch", "feat")) / width
    norm_one_f = norm_one.astype(jnp.float32)
    norm_two_f = norm_two.astype(jnp.float32)
    stats = (
        lax.psum(jnp.sum(back_one, axis=0).astype(jnp.bfloat16), "batch").astype(jnp.float32),
        lax.psum(jnp.sum(back_one * norm_one_f, axis=0).astype(jnp.bfloat16), "batch").astype(
            jnp.float32
        ),
        lax.psum(jnp.sum(back_two, axis=0).astype(jnp.bfloat16), "batch").astype(jnp.float32),
        lax.psum(jnp.sum(back_two * norm_two_f, axis=0).astype(jnp.bfloat16), "batch").astype(
            jnp.float32
        ),
    )
    grad_one = finish(back_one, norm_one, inv_one, stats[0], stats[1], samples)
    grad_two = finish(back_two, norm_two, inv_two, stats[2], stats[3], samples)
    return (grad_one, grad_two, jnp.reshape(loss, (1,)))


def norm_kernel(samples, turned, count, *refs):
    parts = refs[:count]
    if turned:
        norm_ref, pair_ref, stat_ref = refs[-4:-1]
    else:
        norm_ref, stat_ref = refs[-3:-1]
    total = jnp.zeros((1, lanes), jnp.float32)
    square = jnp.zeros((1, lanes), jnp.float32)
    for part in parts:
        values = part[...].astype(jnp.float32)
        total += jnp.sum(values, axis=0, keepdims=True)
        square += jnp.sum(values * values, axis=0, keepdims=True)
    mean = total / samples
    inv = 1.0 / jnp.sqrt(square / samples - mean * mean + 1e-05)
    norm_total = jnp.zeros((1, lanes), jnp.float32)
    start = 0
    late = []
    for place, part in enumerate(parts):
        norm = ((part[...].astype(jnp.float32) - mean) * inv).astype(jnp.bfloat16)
        norm_total += jnp.sum(norm.astype(jnp.float32), axis=0, keepdims=True)
        if not turned:
            norm_ref[start : start + part.shape[0], :] = norm
            start += part.shape[0]
            continue
        if place == 0:
            pair_ref[: part.shape[0], :] = norm
        if place >= count - 2:
            late.append(norm)
            if place < count - 1:
                continue
            norm = jnp.concatenate(late, axis=0)
        norm_ref[:, start : start + norm.shape[0]] = norm.T
        start += norm.shape[0]
    row = lax.broadcasted_iota(jnp.int32, (8, lanes), 0)
    stat_ref[...] = jnp.where(row == 0, inv, jnp.where(row == 1, norm_total, 0.0))
    if turned:
        pair_ref[parts[0].shape[0] :, :] = total_rows(norm_total)


def total_rows(total):
    high = total.astype(jnp.bfloat16).astype(jnp.float32)
    row = lax.broadcasted_iota(jnp.int32, (spare, total.shape[1]), 0)
    both = jnp.where(row == 0, high, jnp.where(row == 1, total - high, 0.0))
    return both.astype(jnp.bfloat16)


def norm_one_chunk(parts, held, token, index, half, samples):
    step = parts[0].shape[1]
    rows = parts[0].shape[0]
    tiles = step // lanes
    place = lambda tile: (0, index * tiles + tile)
    any_spec = pl.BlockSpec(memory_space=pl.ANY)
    count = len(parts)
    return pl.pallas_call(
        functools.partial(norm_kernel, samples, True, count),
        grid=(tiles,),
        in_specs=[pl.BlockSpec((part.shape[0], lanes), lambda tile: (0, tile)) for part in parts]
        + [any_spec] * (len(held) + 1),
        out_specs=[
            pl.BlockSpec((lanes, samples), lambda tile: (index * tiles + tile, 0)),
            pl.BlockSpec((rows + spare, lanes), place),
            pl.BlockSpec((8, lanes), place),
            any_spec,
        ],
        out_shape=[
            jax.ShapeDtypeStruct((half, samples), jnp.bfloat16),
            jax.ShapeDtypeStruct((rows + spare, half), jnp.bfloat16),
            jax.ShapeDtypeStruct((8, half), jnp.float32),
            jax.ShapeDtypeStruct(token.shape, token.dtype),
        ],
        input_output_aliases={
            **{count + k: k for k in range(len(held))},
            count + len(held): 3,
        },
        compiler_params=pltpu.CompilerParams(vmem_limit_bytes=vmem),
        cost_estimate=pl.CostEstimate(
            flops=step, bytes_accessed=step, transcendentals=0
        ),
        name="norm_one_chunk",
    )(*parts, *held, token)


def norm_two_chunk(parts, token, samples):
    step = parts[0].shape[1]
    return pl.pallas_call(
        functools.partial(norm_kernel, samples, False, len(parts)),
        grid=(step // lanes,),
        in_specs=[pl.BlockSpec((part.shape[0], lanes), lambda tile: (0, tile)) for part in parts]
        + [pl.BlockSpec(memory_space=pl.ANY)],
        out_specs=[
            pl.BlockSpec((samples, lanes), lambda tile: (0, tile)),
            pl.BlockSpec((8, lanes), lambda tile: (0, tile)),
            pl.BlockSpec(memory_space=pl.ANY),
        ],
        out_shape=[
            jax.ShapeDtypeStruct((samples, step), jnp.bfloat16),
            jax.ShapeDtypeStruct((8, step), jnp.float32),
            jax.ShapeDtypeStruct(token.shape, token.dtype),
        ],
        input_output_aliases={len(parts): 2},
        compiler_params=pltpu.CompilerParams(vmem_limit_bytes=vmem),
        cost_estimate=pl.CostEstimate(
            flops=step, bytes_accessed=step, transcendentals=0
        ),
        name="norm_two_chunk",
    )(*parts, token)


def corr_kernel(samples, diag_at, begins, ends, *refs):
    side_ref, one_ref, pair_ref, two_ref, stat_ref, loss_in = refs[:6]
    rest = list(refs[6:])
    acc_in = None if begins else rest.pop(0)
    stat_one_ref = rest.pop(0) if ends else None
    loss_out, keep_out, send_out = rest[:3]
    ext_ref, grad_ref, prod_ref, back_ref, sum_ref, fold_ref = rest[-6:]
    ext = pair_ref.shape[0]
    rows = ext - spare
    share = rows // 2
    tile = pl.program_id(0)
    side = side_ref[0]
    mine = pl.ds(pl.multiple_of(side * share, 8), share)
    theirs = pl.ds(pl.multiple_of((1 - side) * share, 8), share)

    @pl.when(tile == 0)
    def _():
        ext_ref[:rows, :] = two_ref[:rows, :]
        ext_ref[rows:, :] = total_rows(stat_ref[1:2, :])
        prod_ref[...] = jnp.zeros_like(prod_ref)
        loss_out[...] = loss_in[...]

    sum_ref[...] = jnp.dot(one_ref[...], two_ref[...], preferred_element_type=jnp.float32)
    height, width = sum_ref.shape

    def fold(value):
        folded = value[:, :128]
        for start in range(128, width, 128):
            folded += value[:, start : start + 128]
        return folded

    def strip_sum(value):
        return jnp.sum(value.reshape(strip // 8, 8, width), axis=0)

    loss_sum = jnp.zeros((8, 128), jnp.float32)
    prod_sum = jnp.zeros((8, width), jnp.float32)
    if diag_at is not None:
        ahead = lax.broadcasted_iota(jnp.int32, (strip, width), 1) - lax.broadcasted_iota(
            jnp.int32, (strip, width), 0
        )
    for start in range(0, height, strip):
        summed = sum_ref[start : start + strip, :]
        grad = summed * (2.0 * off_weight / samples)
        loss = summed * summed
        if diag_at is not None:
            diag = ahead == tile * height + start - diag_at
            grad = jnp.where(diag, summed * (2.0 / samples) - 2.0, grad)
            loss = jnp.where(diag, (samples - summed) ** 2 * (1.0 / off_weight), loss)
        grad = grad.astype(jnp.bfloat16)
        grad_ref[pl.ds(pl.multiple_of(tile * height + start, strip), strip), :] = grad
        prod = grad.astype(jnp.float32) * summed
        loss_sum += fold(strip_sum(loss))
        prod_sum += strip_sum(prod)
        fold_ref[start : start + strip, :] = fold(prod)
    loss_out[...] += loss_sum
    prod_ref[...] += prod_sum
    prod_row = jnp.sum(fold_ref[...].T, axis=0, keepdims=True)
    here = pl.ds(pl.multiple_of(tile * height, height), height)
    back = lax.dot_general(
        ext_ref[...], grad_ref[here, :], (((1,), (1,)), ((), ())), preferred_element_type=jnp.float32
    )
    row = lax.broadcasted_iota(jnp.int32, (8, height), 0)
    added = jnp.where(row == 0, prod_row, 0.0)
    if not ends:
        acc_out = rest[3]
        acc_out[...] = back if begins else acc_in[...] + back
        acc_out[rows + 8 :, :] += added
    else:
        keep_one, send_one, total_ref = rest[3], rest[4], rest[5]
        total_ref[...] = acc_in[...] + back
        total_ref[rows + 8 :, :] += added
        sum_back = (total_ref[rows : rows + 1, :] + total_ref[rows + 1 : rows + 2, :]) / samples
        sum_prod = total_ref[rows + 8 : rows + 9, :] / samples
        normal = pair_ref[:rows, here].astype(jnp.float32)
        total_ref[:rows, :] = stat_one_ref[0:1, :] * (
            total_ref[:rows, :] - sum_back - normal * sum_prod
        )
        keep_one[...] = total_ref[mine, :].astype(jnp.bfloat16)
        send_one[...] = total_ref[theirs, :].astype(jnp.bfloat16)

    @pl.when(tile == pl.num_programs(0) - 1)
    def _():
        back_two = jnp.dot(pair_ref[...], grad_ref[...], preferred_element_type=jnp.float32)
        sum_back = (back_two[rows : rows + 1, :] + back_two[rows + 1 : rows + 2, :]) / samples
        sum_prod = jnp.sum(prod_ref[...], axis=0, keepdims=True) / samples
        normal = two_ref[:rows, :].astype(jnp.float32)
        back_ref[...] = stat_ref[0:1, :] * (back_two[:rows, :] - sum_back - normal * sum_prod)
        keep_out[...] = back_ref[mine, :]
        send_out[...] = back_ref[theirs, :]


def corr_half(side, norm_one, pair_one, norm_two, stat_two, loss, acc, stat_one, diag_at, ends):
    half, samples = norm_one.shape
    width = norm_two.shape[1]
    ext = pair_one.shape[0]
    rows = ext - spare
    share = rows // 2
    tiles = half // tile_rows
    begins = acc is None

    def whole(shape):
        return pl.BlockSpec(shape, lambda tile: (0, 0), pipeline_mode=pl.Buffered(1))

    def kept(shape):
        return pl.BlockSpec(shape, lambda tile: (0, 0))

    def tiled(height):
        return pl.BlockSpec((height, tile_rows), lambda tile: (0, tile))

    operands = [side, norm_one, pair_one, norm_two, stat_two, loss]
    in_specs = [
        pl.BlockSpec(memory_space=pltpu.SMEM),
        pl.BlockSpec((tile_rows, samples), lambda tile: (tile, 0)),
        whole((ext, half)),
        whole((samples, width)),
        whole((8, width)),
        kept((8, 128)),
    ]
    out_specs = [kept((8, 128)), kept((share, width)), kept((share, width))]
    out_shape = [jax.ShapeDtypeStruct((8, 128), jnp.float32)]
    out_shape += [jax.ShapeDtypeStruct((share, width), jnp.float32)] * 2
    aliases = {5: 0}
    if not begins:
        operands.append(acc)
        in_specs.append(tiled(ext))
    if ends:
        operands.append(stat_one)
        in_specs.append(tiled(8))
        out_specs += [tiled(share)] * 2
        out_shape += [jax.ShapeDtypeStruct((share, half), jnp.bfloat16)] * 2
    else:
        if not begins:
            aliases[6] = 3
        out_specs.append(tiled(ext))
        out_shape.append(jax.ShapeDtypeStruct((ext, half), jnp.float32))
    return pl.pallas_call(
        functools.partial(corr_kernel, samples, diag_at, begins, ends),
        grid=(tiles,),
        in_specs=in_specs,
        out_specs=out_specs,
        out_shape=out_shape,
        scratch_shapes=([pltpu.VMEM((ext, tile_rows), jnp.float32)] if ends else [])
        + [
            pltpu.VMEM((ext, width), jnp.bfloat16),
            pltpu.VMEM((half, width), jnp.bfloat16),
            pltpu.VMEM((8, width), jnp.float32),
            pltpu.VMEM((rows, width), jnp.float32),
            pltpu.VMEM((tile_rows, width), jnp.float32),
            pltpu.VMEM((tile_rows, 128), jnp.float32),
        ],
        input_output_aliases=aliases,
        compiler_params=pltpu.CompilerParams(vmem_limit_bytes=vmem),
        cost_estimate=pl.CostEstimate(
            flops=width, bytes_accessed=width, transcendentals=0
        ),
        name="corr_half",
    )(*operands)


def place_kernel(side_ref, keep_ref, get_ref, *refs):
    refs[-1][...] = (keep_ref[...] + get_ref[...]).astype(jnp.bfloat16)


def place_two(side, keep, get, placed, far, index, width):
    rows, step = keep.shape
    steps = width // 2 // step

    def column(tile, side_ref):
        half = 1 - side_ref[0] if far else side_ref[0]
        return (0, half * steps + index)

    block = pl.BlockSpec((rows, step), lambda tile, side_ref: (0, 0))
    held = [] if placed is None else [placed]
    return pl.pallas_call(
        place_kernel,
        grid_spec=pltpu.PrefetchScalarGridSpec(
            num_scalar_prefetch=1,
            grid=(1,),
            in_specs=[block, block] + [pl.BlockSpec(memory_space=pl.ANY)] * len(held),
            out_specs=pl.BlockSpec((rows, step), column),
        ),
        out_shape=jax.ShapeDtypeStruct((rows, width), jnp.bfloat16),
        input_output_aliases={3: 0} if held else {},
        cost_estimate=pl.CostEstimate(
            flops=rows * step, bytes_accessed=10 * rows * step, transcendentals=0
        ),
        name="place_two",
    )(side, keep, get, *held)


def join_kernel(side_ref, keep_ref, get_ref, out_ref):
    @pl.when(pl.program_id(0) == 0)
    def _():
        out_ref[...] = keep_ref[...]

    @pl.when(pl.program_id(0) == 1)
    def _():
        out_ref[...] = get_ref[...]


def join_one(side, keep, get):
    rows, half = keep.shape
    block = pl.BlockSpec((rows, half), lambda tile, side_ref: (0, 0))
    column = lambda tile, side_ref: (0, side_ref[0] + tile - 2 * side_ref[0] * tile)
    return pl.pallas_call(
        join_kernel,
        grid_spec=pltpu.PrefetchScalarGridSpec(
            num_scalar_prefetch=1,
            grid=(2,),
            in_specs=[block, block],
            out_specs=pl.BlockSpec((rows, half), column),
        ),
        out_shape=jax.ShapeDtypeStruct((rows, 2 * half), jnp.bfloat16),
        cost_estimate=pl.CostEstimate(
            flops=0, bytes_accessed=8 * rows * half, transcendentals=0
        ),
        name="join_one",
    )(side, keep, get)


def pair_shards(view_one, view_two):
    rows, width = view_one.shape
    batches = lax.axis_size("batch")
    samples = rows * batches
    half = width // 2
    step = half // chunks
    chips = batches // 2
    side = lax.axis_index("batch") % 2
    swap = [(i, i ^ 1) for i in range(batches)]
    line = chips // 2
    order = [2 * r for r in range(line)] + [2 * r + 1 for r in reversed(range(line))]
    ahead = [
        (2 * order[r] + c, 2 * order[(r + 1) % chips] + c) for r in range(chips) for c in range(2)
    ]
    behind = [(there, here) for here, there in ahead]

    def mine(both, axis=0):
        size = both.shape[axis] // 2
        return lax.dynamic_slice_in_dim(both, side * size, size, axis=axis)

    def theirs(both, axis=0):
        size = both.shape[axis] // 2
        return lax.dynamic_slice_in_dim(both, (1 - side) * size, size, axis=axis)

    def swapped(value):
        return lax.ppermute(value, "batch", swap)

    def in_order(own, other, axis):
        return jnp.where(
            side == 0,
            jnp.concatenate([own, other], axis=axis),
            jnp.concatenate([other, own], axis=axis),
        )

    def chip_rows(view):
        return in_order(mine(view, 1), swapped(theirs(view, 1)), 0)

    blocks = (chip_rows(view_one), chip_rows(view_two))
    hops = chips // 2
    flows = [(view, index) for view in range(2) for index in range(chunks)]
    slots = {}
    for flow in range(len(flows)):
        for hop in range(hops):
            slots[hops * flow + flow % 2 + 2 * hop] = (flow, hop)
    last_hop = {hops * flow + flow % 2 + 2 * (hops - 1): flow for flow in range(len(flows))}
    ends = {}
    arrived = {}
    held = []
    state = {"loss": jnp.zeros((8, 128), jnp.float32), "acc": None, "grad": None}
    place = jnp.reshape(side, (1,)).astype(jnp.int32)
    work = []

    def run_half(norm, stat, diag_at, last, kept):
        state["loss"], keep, send, *rest = corr_half(
            place,
            held[0],
            held[1],
            norm,
            stat,
            state["loss"],
            state["acc"],
            held[2],
            diag_at,
            last,
        )
        if last:
            state["one"] = rest
        else:
            state["acc"] = rest[0]
        kept.append((keep, send))

    def put(kept, index):
        (keep_own, send_own), (keep_far, send_far) = kept
        get_own, get_far = swapped(send_far), swapped(send_own)
        grad = place_two(place, keep_own, get_own, state["grad"], False, index, width)
        state["grad"] = place_two(place, keep_far, get_far, grad, True, index, width)

    def take(flow):
        view, index = flows[flow]
        if view == 0:
            *held[:], state["loss"] = norm_one_chunk(
                arrived[flow], held, state["loss"], index, half, samples
            )
            return
        norm, stat, state["loss"] = norm_two_chunk(arrived[flow], state["loss"], samples)
        far_norm, far_stat = swapped(norm), swapped(stat)
        kept = []
        last = flow == len(flows) - 1
        work.append(functools.partial(run_half, norm, stat, index * step, False, kept))
        if not last:
            work.append(lambda: None)
        work.append(functools.partial(run_half, far_norm, far_stat, None, last, kept))
        puts.append((kept, index))

    puts = []
    for slot in range(max(slots) + 3):
        if slot in slots:
            flow, hop = slots[slot]
            view, index = flows[flow]
            if hop == 0:
                block = blocks[view][:, index * step : (index + 1) * step]
                ends[flow] = (block, block)
                arrived[flow] = [block]
            up, down = ends[flow]
            up, down, state["loss"] = lax.optimization_barrier((up, down, state["loss"]))
            if hop > 0:
                arrived[flow][-2:] = [up, down]
            if hop == hops - 1:
                up, down = up[:rows], down[rows:]
            up = lax.ppermute(up, "batch", ahead)
            down = lax.ppermute(down, "batch", behind)
            ends[flow] = (up, down)
            arrived[flow] += [up, down]
        if slot - 2 in last_hop:
            take(last_hop[slot - 2])
        elif work:
            work.pop(0)()
    while work:
        work.pop(0)()
    for kept, index in puts:
        put(kept, index)

    keep, send = state["one"]
    grad_one = join_one(place, keep, swapped(send))
    loss = jnp.sum(state["loss"]) * (off_weight / (samples * samples))
    loss = (loss + swapped(loss)) / width
    return (grad_one, state["grad"], jnp.reshape(loss, (1,)))


def solution(mesh):
    placed = (P(("groups", "batch"), "feat"), P(("groups", "batch"), "feat"))
    paired = mesh.shape["feat"] == 1 and mesh.shape["batch"] % 4 == 0
    return jax.shard_map(
        pair_shards if paired else shards,
        mesh=mesh,
        in_specs=placed,
        out_specs=(P(("groups", "batch"), "feat"), P(("groups", "batch"), "feat"), P("groups")),
        check_vma=False,
    )
```

```python
import functools

import jax
import jax.numpy as jnp
from jax import lax
from jax.experimental import pallas as pl
from jax.experimental.pallas import tpu as pltpu
from jax.sharding import PartitionSpec as P

off_weight = 0.0051
parts = (1, 2, 1)
lanes = 256
tile_rows = 512
high = 128
wide = 256
spare = 16
vmem = 44 * 1024 * 1024


def local_term(columns, full_two):
    return lax.dot_general(
        columns, full_two, (((0,), (0,)), ((), ())), preferred_element_type=jnp.float32
    )


def tile_grad(summed, row_base, samples):
    corr = summed / samples
    row_ids = row_base + lax.broadcasted_iota(jnp.int32, corr.shape, 0)
    col_ids = lax.broadcasted_iota(jnp.int32, corr.shape, 1)
    diag = row_ids == col_ids
    grad = jnp.where(diag, -2.0 * (1.0 - corr), 2.0 * off_weight * corr).astype(jnp.bfloat16)
    part_loss = jnp.sum(jnp.where(diag, (1.0 - corr) ** 2, off_weight * corr * corr))
    return (grad, part_loss)


def fold_step(columns, full_two, piece):
    contrib = lax.dot_general(
        full_two, piece, (((1,), (1,)), ((), ())), preferred_element_type=jnp.float32
    )
    back_mix = jnp.dot(columns, piece, preferred_element_type=jnp.float32)
    return (contrib, back_mix)


def finish(back, normed, inv, sum_back, sum_prod, samples):
    normal_f = normed.astype(jnp.float32)
    return (inv * (back - sum_back / samples - normal_f * sum_prod / samples)).astype(jnp.bfloat16)


def shards(view_one, view_two):
    rows, half_feat = view_one.shape
    batches = lax.axis_size("batch")
    samples = rows * batches
    values_one = view_one.astype(jnp.float32)
    values_two = view_two.astype(jnp.float32)
    sums = lax.psum(
        (
            jnp.sum(values_one, axis=0),
            jnp.sum(values_one * values_one, axis=0),
            jnp.sum(values_two, axis=0),
            jnp.sum(values_two * values_two, axis=0),
        ),
        "batch",
    )
    mean_one = sums[0] / samples
    mean_two = sums[2] / samples
    inv_one = 1.0 / jnp.sqrt(sums[1] / samples - mean_one * mean_one + 1e-05)
    inv_two = 1.0 / jnp.sqrt(sums[3] / samples - mean_two * mean_two + 1e-05)
    norm_one = ((values_one - mean_one) * inv_one).astype(jnp.bfloat16)
    norm_two = ((values_two - mean_two) * inv_two).astype(jnp.bfloat16)
    full_two = lax.all_gather(norm_two, "feat", axis=1, tiled=True)
    width = full_two.shape[1]
    tile = half_feat // batches
    row_base = lax.axis_index("feat") * half_feat + lax.axis_index("batch") * tile
    summed = lax.psum_scatter(
        local_term(norm_one, full_two), "batch", scatter_dimension=0, tiled=True
    )
    grad, part_loss = tile_grad(summed, row_base, samples)
    back_one, back_mix = fold_step(
        norm_one, full_two, lax.all_gather(grad, "batch", axis=0, tiled=True)
    )
    back_two = lax.psum_scatter(back_mix, "feat", scatter_dimension=1, tiled=True)
    loss = lax.psum(part_loss, ("batch", "feat")) / width
    norm_one_f = norm_one.astype(jnp.float32)
    norm_two_f = norm_two.astype(jnp.float32)
    stats = (
        lax.psum(jnp.sum(back_one, axis=0).astype(jnp.bfloat16), "batch").astype(jnp.float32),
        lax.psum(jnp.sum(back_one * norm_one_f, axis=0).astype(jnp.bfloat16), "batch").astype(
            jnp.float32
        ),
        lax.psum(jnp.sum(back_two, axis=0).astype(jnp.bfloat16), "batch").astype(jnp.float32),
        lax.psum(jnp.sum(back_two * norm_two_f, axis=0).astype(jnp.bfloat16), "batch").astype(
            jnp.float32
        ),
    )
    grad_one = finish(back_one, norm_one, inv_one, stats[0], stats[1], samples)
    grad_two = finish(back_two, norm_two, inv_two, stats[2], stats[3], samples)
    return (grad_one, grad_two, jnp.reshape(loss, (1,)))


def total_rows(total):
    high = total.astype(jnp.bfloat16).astype(jnp.float32)
    row = lax.broadcasted_iota(jnp.int32, (spare, total.shape[1]), 0)
    both = jnp.where(row == 0, high, jnp.where(row == 1, total - high, 0.0))
    return both.astype(jnp.bfloat16)


def norm_one_kernel(rows, place_ref, raw_ref, norm_ref, pair_ref, stat_ref):
    samples = raw_ref.shape[0]
    starts = range(0, samples, rows)
    total = jnp.zeros((1, lanes), jnp.float32)
    square = jnp.zeros((1, lanes), jnp.float32)
    for start in starts:
        values = raw_ref[start : start + rows, :].astype(jnp.float32)
        total += jnp.sum(values, axis=0, keepdims=True)
        square += jnp.sum(values * values, axis=0, keepdims=True)
    mean = total / samples
    inv = 1.0 / jnp.sqrt(square / samples - mean * mean + 1e-05)
    norm_total = jnp.zeros((1, lanes), jnp.float32)

    def normed(values):
        return ((values.astype(jnp.float32) - mean) * inv).astype(jnp.bfloat16)

    for start in starts:
        norm = normed(raw_ref[start : start + rows, :])
        norm_total += jnp.sum(norm.astype(jnp.float32), axis=0, keepdims=True)
        norm_ref[:, start : start + rows] = norm.T
    row = lax.broadcasted_iota(jnp.int32, (8, lanes), 0)
    stat_ref[...] = jnp.where(row == 0, inv, jnp.where(row == 1, norm_total, 0.0))
    first = pl.multiple_of(place_ref[1] * rows, 16)
    pair_ref[:rows, :] = normed(raw_ref[pl.ds(first, rows), :])
    pair_ref[rows:, :] = total_rows(norm_total)


def norm_one_half(place, raw, rows):
    samples, width = raw.shape
    half = width // 2
    tiles = half // lanes
    column = lambda tile, place_ref: (0, tile)
    return pl.pallas_call(
        functools.partial(norm_one_kernel, rows),
        grid_spec=pltpu.PrefetchScalarGridSpec(
            num_scalar_prefetch=1,
            grid=(tiles,),
            in_specs=[
                pl.BlockSpec(
                    (samples, lanes), lambda tile, place_ref: (0, place_ref[0] * tiles + tile)
                )
            ],
            out_specs=[
                pl.BlockSpec((lanes, samples), lambda tile, place_ref: (tile, 0)),
                pl.BlockSpec((rows + spare, lanes), column),
                pl.BlockSpec((8, lanes), column),
            ],
        ),
        out_shape=[
            jax.ShapeDtypeStruct((half, samples), jnp.bfloat16),
            jax.ShapeDtypeStruct((rows + spare, half), jnp.bfloat16),
            jax.ShapeDtypeStruct((8, half), jnp.float32),
        ],
        compiler_params=pltpu.CompilerParams(vmem_limit_bytes=vmem),
        cost_estimate=pl.CostEstimate(flops=half, bytes_accessed=half, transcendentals=0),
        name="norm_one",
    )(place, raw)


def norm_two_kernel(samples, count, spots_ref, *refs):
    parts = refs[:count]
    norm_ref, stat_ref = refs[-3:-1]
    total = jnp.zeros((1, lanes), jnp.float32)
    square = jnp.zeros((1, lanes), jnp.float32)
    for part in parts:
        values = part[...].astype(jnp.float32)
        total += jnp.sum(values, axis=0, keepdims=True)
        square += jnp.sum(values * values, axis=0, keepdims=True)
    mean = total / samples
    inv = 1.0 / jnp.sqrt(square / samples - mean * mean + 1e-05)
    norm_total = jnp.zeros((1, lanes), jnp.float32)
    for index, part in enumerate(parts):
        norm = ((part[...].astype(jnp.float32) - mean) * inv).astype(jnp.bfloat16)
        norm_total += jnp.sum(norm.astype(jnp.float32), axis=0, keepdims=True)
        first = pl.multiple_of(spots_ref[index], 64)
        norm_ref[pl.ds(first, part.shape[0]), :] = norm
    row = lax.broadcasted_iota(jnp.int32, (8, lanes), 0)
    stat_ref[...] = jnp.where(row == 0, inv, jnp.where(row == 1, norm_total, 0.0))


def norm_two_chunk(spots, parts, token, samples):
    step = parts[0].shape[1]
    any_spec = pl.BlockSpec(memory_space=pl.ANY)
    return pl.pallas_call(
        functools.partial(norm_two_kernel, samples, len(parts)),
        grid=(step // lanes,),
        in_specs=[pl.BlockSpec(memory_space=pltpu.SMEM)]
        + [pl.BlockSpec((part.shape[0], lanes), lambda tile: (0, tile)) for part in parts]
        + [any_spec],
        out_specs=[
            pl.BlockSpec((samples, lanes), lambda tile: (0, tile)),
            pl.BlockSpec((8, lanes), lambda tile: (0, tile)),
            any_spec,
        ],
        out_shape=[
            jax.ShapeDtypeStruct((samples, step), jnp.bfloat16),
            jax.ShapeDtypeStruct((8, step), jnp.float32),
            jax.ShapeDtypeStruct(token.shape, token.dtype),
        ],
        input_output_aliases={len(parts) + 1: 2},
        compiler_params=pltpu.CompilerParams(vmem_limit_bytes=vmem),
        cost_estimate=pl.CostEstimate(flops=step, bytes_accessed=step, transcendentals=0),
        name="norm_two",
    )(spots, *parts, token)


def corr_kernel(samples, diag_at, begins, ends, *refs):
    side_ref, one_ref, pair_ref, two_ref, stat_ref, loss_in = refs[:6]
    rest = list(refs[6:])
    acc_in = None if begins else rest.pop(0)
    stat_one_ref = rest.pop(0) if ends else None
    loss_out, keep_out, send_out = rest[:3]
    ext_ref, grad_ref, prod_ref, back_ref, fold_ref = rest[-5:]
    ext = pair_ref.shape[0]
    rows = ext - spare
    share = rows // 2
    tile = pl.program_id(0)
    side = side_ref[0]
    own = pl.ds(pl.multiple_of(side_ref[1] * rows, 64), rows)
    mine = pl.ds(pl.multiple_of(side * share, 8), share)
    theirs = pl.ds(pl.multiple_of((1 - side) * share, 8), share)

    @pl.when(tile == 0)
    def _():
        ext_ref[:rows, :] = two_ref[own, :]
        ext_ref[rows:, :] = total_rows(stat_ref[1:2, :])
        prod_ref[...] = jnp.zeros_like(prod_ref)
        loss_out[...] = loss_in[...]

    height = one_ref.shape[0]
    width = two_ref.shape[1]

    def fold(value):
        folded = value[:, :128]
        for start in range(128, value.shape[1], 128):
            folded += value[:, start : start + 128]
        return folded

    def down(value):
        return jnp.sum(value.reshape(high // 8, 8, wide), axis=0)

    for top in range(0, height, high):
        across = jnp.zeros((high, 128), jnp.float32)
        here = pl.ds(pl.multiple_of(tile * height + top, high), high)
        for left in range(0, width, wide):
            summed = jnp.dot(
                one_ref[top : top + high, :],
                two_ref[:, left : left + wide],
                preferred_element_type=jnp.float32,
            )
            grad = summed * (2.0 * off_weight / samples)
            loss = summed * summed
            if diag_at is not None:
                ahead = lax.broadcasted_iota(jnp.int32, (high, wide), 1) - lax.broadcasted_iota(
                    jnp.int32, (high, wide), 0
                )
                diag = ahead == tile * height + top - left - diag_at
                grad = jnp.where(diag, summed * (2.0 / samples) - 2.0, grad)
                loss = jnp.where(diag, (samples - summed) ** 2 * (1.0 / off_weight), loss)
            grad = grad.astype(jnp.bfloat16)
            grad_ref[here, left : left + wide] = grad
            prod = grad.astype(jnp.float32) * summed
            loss_out[...] += fold(down(loss))
            prod_ref[:, left : left + wide] += down(prod)
            across += fold(prod)
        fold_ref[top : top + high, :] = across
    prod_row = jnp.sum(fold_ref[...].T, axis=0, keepdims=True)
    here = pl.ds(pl.multiple_of(tile * height, height), height)
    back = lax.dot_general(
        ext_ref[...], grad_ref[here, :], (((1,), (1,)), ((), ())), preferred_element_type=jnp.float32
    )
    row = lax.broadcasted_iota(jnp.int32, (8, height), 0)
    added = jnp.where(row == 0, prod_row, 0.0)
    if not ends:
        acc_out = rest[3]
        acc_out[...] = back if begins else acc_in[...] + back
        acc_out[rows + 8 :, :] += added
    else:
        keep_one, send_one, total_ref = rest[3], rest[4], rest[5]
        total_ref[...] = acc_in[...] + back
        total_ref[rows + 8 :, :] += added
        sum_back = (total_ref[rows : rows + 1, :] + total_ref[rows + 1 : rows + 2, :]) / samples
        sum_prod = total_ref[rows + 8 : rows + 9, :] / samples
        normal = pair_ref[:rows, here].astype(jnp.float32)
        total_ref[:rows, :] = stat_one_ref[0:1, :] * (
            total_ref[:rows, :] - sum_back - normal * sum_prod
        )
        keep_one[...] = total_ref[mine, :].astype(jnp.bfloat16)
        send_one[...] = total_ref[theirs, :].astype(jnp.bfloat16)

    @pl.when(tile == pl.num_programs(0) - 1)
    def _():
        back_two = jnp.dot(pair_ref[...], grad_ref[...], preferred_element_type=jnp.float32)
        sum_back = (back_two[rows : rows + 1, :] + back_two[rows + 1 : rows + 2, :]) / samples
        sum_prod = jnp.sum(prod_ref[...], axis=0, keepdims=True) / samples
        normal = ext_ref[:rows, :].astype(jnp.float32)
        back_ref[...] = stat_ref[0:1, :] * (back_two[:rows, :] - sum_back - normal * sum_prod)
        keep_out[...] = back_ref[mine, :]
        send_out[...] = back_ref[theirs, :]


def corr_half(side, norm_one, pair_one, norm_two, stat_two, loss, acc, stat_one, diag_at, ends):
    half, samples = norm_one.shape
    width = norm_two.shape[1]
    ext = pair_one.shape[0]
    rows = ext - spare
    share = rows // 2
    tiles = half // tile_rows
    begins = acc is None

    def whole(shape):
        return pl.BlockSpec(shape, lambda tile: (0, 0), pipeline_mode=pl.Buffered(1))

    def kept(shape):
        return pl.BlockSpec(shape, lambda tile: (0, 0))

    def tiled(height):
        return pl.BlockSpec((height, tile_rows), lambda tile: (0, tile))

    operands = [side, norm_one, pair_one, norm_two, stat_two, loss]
    in_specs = [
        pl.BlockSpec(memory_space=pltpu.SMEM),
        pl.BlockSpec((tile_rows, samples), lambda tile: (tile, 0)),
        whole((ext, half)),
        whole((samples, width)),
        whole((8, width)),
        kept((8, 128)),
    ]
    out_specs = [kept((8, 128)), kept((share, width)), kept((share, width))]
    out_shape = [jax.ShapeDtypeStruct((8, 128), jnp.float32)]
    out_shape += [jax.ShapeDtypeStruct((share, width), jnp.float32)] * 2
    aliases = {5: 0}
    if not begins:
        operands.append(acc)
        in_specs.append(tiled(ext))
    if ends:
        operands.append(stat_one)
        in_specs.append(tiled(8))
        out_specs += [tiled(share)] * 2
        out_shape += [jax.ShapeDtypeStruct((share, half), jnp.bfloat16)] * 2
    else:
        if not begins:
            aliases[6] = 3
        out_specs.append(tiled(ext))
        out_shape.append(jax.ShapeDtypeStruct((ext, half), jnp.float32))
    return pl.pallas_call(
        functools.partial(corr_kernel, samples, diag_at, begins, ends),
        grid=(tiles,),
        in_specs=in_specs,
        out_specs=out_specs,
        out_shape=out_shape,
        scratch_shapes=([pltpu.VMEM((ext, tile_rows), jnp.float32)] if ends else [])
        + [
            pltpu.VMEM((ext, width), jnp.bfloat16),
            pltpu.VMEM((half, width), jnp.bfloat16),
            pltpu.VMEM((8, width), jnp.float32),
            pltpu.VMEM((rows, width), jnp.float32),
            pltpu.VMEM((tile_rows, 128), jnp.float32),
        ],
        input_output_aliases=aliases,
        compiler_params=pltpu.CompilerParams(vmem_limit_bytes=vmem),
        cost_estimate=pl.CostEstimate(
            flops=width, bytes_accessed=width, transcendentals=0
        ),
        name="corr_half",
    )(*operands)


def place_kernel(side_ref, keep_own, get_own, keep_far, get_far, *refs):
    @pl.when(pl.program_id(0) == 0)
    def _():
        refs[-1][...] = (keep_own[...] + get_own[...]).astype(jnp.bfloat16)

    @pl.when(pl.program_id(0) == 1)
    def _():
        refs[-1][...] = (keep_far[...] + get_far[...]).astype(jnp.bfloat16)


def place_two(side, own, far, placed, first, width):
    rows, step = own[0].shape
    half = width // 2
    piece = min(step, 512)

    def column(turn, tile, side_ref):
        side = side_ref[0] + turn - 2 * side_ref[0] * turn
        return (0, (side * half + first) // piece + tile)

    block = pl.BlockSpec((rows, piece), lambda turn, tile, side_ref: (0, tile))
    held = [] if placed is None else [placed]
    return pl.pallas_call(
        place_kernel,
        grid_spec=pltpu.PrefetchScalarGridSpec(
            num_scalar_prefetch=1,
            grid=(2, step // piece),
            in_specs=[block] * 4 + [pl.BlockSpec(memory_space=pl.ANY)] * len(held),
            out_specs=pl.BlockSpec((rows, piece), column),
        ),
        out_shape=jax.ShapeDtypeStruct((rows, width), jnp.bfloat16),
        input_output_aliases={5: 0} if held else {},
        cost_estimate=pl.CostEstimate(flops=step, bytes_accessed=step, transcendentals=0),
        name="place_two",
    )(side, *own, *far, *held)


def join_kernel(side_ref, keep_ref, get_ref, out_ref):
    @pl.when(pl.program_id(0) == 0)
    def _():
        out_ref[...] = keep_ref[...]

    @pl.when(pl.program_id(0) == 1)
    def _():
        out_ref[...] = get_ref[...]


def join_one(side, keep, get):
    rows, half = keep.shape
    block = pl.BlockSpec((rows, half), lambda tile, side_ref: (0, 0))
    column = lambda tile, side_ref: (0, side_ref[0] + tile - 2 * side_ref[0] * tile)
    return pl.pallas_call(
        join_kernel,
        grid_spec=pltpu.PrefetchScalarGridSpec(
            num_scalar_prefetch=1,
            grid=(2,),
            in_specs=[block, block],
            out_specs=pl.BlockSpec((rows, half), column),
        ),
        out_shape=jax.ShapeDtypeStruct((rows, 2 * half), jnp.bfloat16),
        cost_estimate=pl.CostEstimate(
            flops=0, bytes_accessed=8 * rows * half, transcendentals=0
        ),
        name="join_one",
    )(side, keep, get)


def pair_shards(view_one, view_two):
    rows, width = view_one.shape
    batches = lax.axis_size("batch")
    samples = rows * batches
    half = width // 2
    chips = batches // 2
    index = lax.axis_index("batch")
    side, chip = index % 2, index // 2
    place = jnp.stack([side, chip]).astype(jnp.int32)
    swap = [(i, i ^ 1) for i in range(batches)]
    line = chips // 2
    order = [2 * r for r in range(line)] + [2 * r + 1 for r in reversed(range(line))]
    ahead = [
        (2 * order[r] + c, 2 * order[(r + 1) % chips] + c) for r in range(chips) for c in range(2)
    ]
    behind = [(there, here) for here, there in ahead]
    hops = chips // 2
    spots = [None] * chips
    for r in range(chips):
        far = 2 * rows * order[(r + hops) % chips]
        spots[order[r]] = [2 * rows * order[r]]
        for hop in range(1, hops):
            spots[order[r]] += [2 * rows * order[(r + turn * hop) % chips] for turn in (-1, 1)]
        spots[order[r]] += [far, far + rows]
    spots = jnp.asarray(spots, jnp.int32)[chip]

    def swapped(value):
        return lax.ppermute(value, "batch", swap)

    def chip_rows(view):
        own = lax.dynamic_slice_in_dim(view, side * half, half, axis=1)
        other = swapped(lax.dynamic_slice_in_dim(view, (1 - side) * half, half, axis=1))
        return jnp.where(
            side == 0,
            jnp.concatenate([own, other], axis=0),
            jnp.concatenate([other, own], axis=0),
        )

    raw_one = lax.all_gather(view_one, "batch", axis=0, tiled=True)
    block_two = chip_rows(view_two)
    steps = [half * part // sum(parts) for part in parts]
    firsts = [sum(steps[:flow]) for flow in range(len(parts))]
    flows = len(parts)
    slots = {}
    for flow in range(flows):
        for hop in range(hops):
            slots[hops * flow + flow % 2 + 2 * hop] = (flow, hop)
    last_hop = {hops * flow + flow % 2 + 2 * (hops - 1): flow for flow in range(flows)}
    ends, arrived = {}, {}
    loss = jnp.zeros((8, 128), jnp.float32)
    raw_one, loss = lax.optimization_barrier((raw_one, loss))
    held = norm_one_half(place, raw_one, 2 * rows)
    state = {"loss": loss, "acc": None, "grad": None}
    work = []

    def run_half(norm, stat, diag_at, last, kept):
        state["loss"], keep, send, *rest = corr_half(
            place, *held[:2], norm, stat, state["loss"], state["acc"], held[2], diag_at, last
        )
        if last:
            state["one"] = rest
        else:
            state["acc"] = rest[0]
        kept.append((keep, send))

    def put(kept, first):
        (keep_own, send_own), (keep_far, send_far) = kept
        own, far = (keep_own, swapped(send_far)), (keep_far, swapped(send_own))
        state["grad"] = place_two(place, own, far, state["grad"], first, width)

    def put_early(kept, first):
        put(kept, first)
        state["loss"], state["grad"] = lax.optimization_barrier((state["loss"], state["grad"]))

    def take(flow):
        norm, stat, state["loss"] = norm_two_chunk(spots, arrived[flow], state["loss"], samples)
        far_norm, far_stat = swapped(norm), swapped(stat)
        kept = []
        last = flow == flows - 1
        first = firsts[flow]
        work.append(functools.partial(run_half, norm, stat, first, False, kept))
        if not last:
            work.append(lambda: None)
        work.append(functools.partial(run_half, far_norm, far_stat, None, last, kept))
        work.append(functools.partial(put if last else put_early, kept, first))

    for slot in range(max(slots) + 3):
        if slot in slots:
            flow, hop = slots[slot]
            if hop == 0:
                block = block_two[:, firsts[flow] : firsts[flow] + steps[flow]]
                ends[flow] = (block, block)
                arrived[flow] = [block]
            up, down = ends[flow]
            if flow > 0:
                up, down, state["loss"] = lax.optimization_barrier((up, down, state["loss"]))
                if hop > 0:
                    arrived[flow][-2:] = [up, down]
            if hop == hops - 1:
                up, down = up[:rows], down[rows:]
            up = lax.ppermute(up, "batch", ahead)
            down = lax.ppermute(down, "batch", behind)
            ends[flow] = (up, down)
            arrived[flow] += [up, down]
        if slot - 2 in last_hop:
            take(last_hop[slot - 2])
        elif work:
            work.pop(0)()
    while work:
        work.pop(0)()

    keep, send = state["one"]
    grad_one = join_one(place, keep, swapped(send))
    loss = jnp.sum(state["loss"]) * (off_weight / (samples * samples))
    loss = (loss + swapped(loss)) / width
    return (grad_one, state["grad"], jnp.reshape(loss, (1,)))


def solution(mesh):
    placed = (P(("groups", "batch"), "feat"), P(("groups", "batch"), "feat"))
    paired = mesh.shape["feat"] == 1 and mesh.shape["batch"] % 4 == 0
    return jax.shard_map(
        pair_shards if paired else shards,
        mesh=mesh,
        in_specs=placed,
        out_specs=(P(("groups", "batch"), "feat"), P(("groups", "batch"), "feat"), P("groups")),
        check_vma=False,
    )
```

```python
import functools

import jax
import jax.numpy as jnp
from jax import lax
from jax.experimental import pallas as pl
from jax.experimental.pallas import tpu as pltpu
from jax.sharding import PartitionSpec as P

off_weight = 0.0051
tiles = 4
vmem = 56 * 1024 * 1024


def local_term(columns, full_two):
    return lax.dot_general(
        columns, full_two, (((0,), (0,)), ((), ())), preferred_element_type=jnp.float32
    )


def tile_grad(summed, row_base, samples):
    corr = summed / samples
    row_ids = row_base + lax.broadcasted_iota(jnp.int32, corr.shape, 0)
    col_ids = lax.broadcasted_iota(jnp.int32, corr.shape, 1)
    diag = row_ids == col_ids
    grad = jnp.where(diag, -2.0 * (1.0 - corr), 2.0 * off_weight * corr).astype(jnp.bfloat16)
    part_loss = jnp.sum(jnp.where(diag, (1.0 - corr) ** 2, off_weight * corr * corr))
    return (grad, part_loss)


def fold_step(columns, full_two, piece):
    contrib = lax.dot_general(
        full_two, piece, (((1,), (1,)), ((), ())), preferred_element_type=jnp.float32
    )
    back_mix = jnp.dot(columns, piece, preferred_element_type=jnp.float32)
    return (contrib, back_mix)


def finish(back, normed, inv, sum_back, sum_prod, samples):
    normal_f = normed.astype(jnp.float32)
    return (inv * (back - sum_back / samples - normal_f * sum_prod / samples)).astype(jnp.bfloat16)


def shards(view_one, view_two):
    rows, half_feat = view_one.shape
    batches = lax.axis_size("batch")
    samples = rows * batches
    values_one = view_one.astype(jnp.float32)
    values_two = view_two.astype(jnp.float32)
    sums = lax.psum(
        (
            jnp.sum(values_one, axis=0),
            jnp.sum(values_one * values_one, axis=0),
            jnp.sum(values_two, axis=0),
            jnp.sum(values_two * values_two, axis=0),
        ),
        "batch",
    )
    mean_one = sums[0] / samples
    mean_two = sums[2] / samples
    inv_one = 1.0 / jnp.sqrt(sums[1] / samples - mean_one * mean_one + 1e-05)
    inv_two = 1.0 / jnp.sqrt(sums[3] / samples - mean_two * mean_two + 1e-05)
    norm_one = ((values_one - mean_one) * inv_one).astype(jnp.bfloat16)
    norm_two = ((values_two - mean_two) * inv_two).astype(jnp.bfloat16)
    full_two = lax.all_gather(norm_two, "feat", axis=1, tiled=True)
    width = full_two.shape[1]
    tile = half_feat // batches
    row_base = lax.axis_index("feat") * half_feat + lax.axis_index("batch") * tile
    summed = lax.psum_scatter(
        local_term(norm_one, full_two), "batch", scatter_dimension=0, tiled=True
    )
    grad, part_loss = tile_grad(summed, row_base, samples)
    back_one, back_mix = fold_step(
        norm_one, full_two, lax.all_gather(grad, "batch", axis=0, tiled=True)
    )
    back_two = lax.psum_scatter(back_mix, "feat", scatter_dimension=1, tiled=True)
    loss = lax.psum(part_loss, ("batch", "feat")) / width
    norm_one_f = norm_one.astype(jnp.float32)
    norm_two_f = norm_two.astype(jnp.float32)
    stats = (
        lax.psum(jnp.sum(back_one, axis=0).astype(jnp.bfloat16), "batch").astype(jnp.float32),
        lax.psum(jnp.sum(back_one * norm_one_f, axis=0).astype(jnp.bfloat16), "batch").astype(
            jnp.float32
        ),
        lax.psum(jnp.sum(back_two, axis=0).astype(jnp.bfloat16), "batch").astype(jnp.float32),
        lax.psum(jnp.sum(back_two * norm_two_f, axis=0).astype(jnp.bfloat16), "batch").astype(
            jnp.float32
        ),
    )
    grad_one = finish(back_one, norm_one, inv_one, stats[0], stats[1], samples)
    grad_two = finish(back_two, norm_two, inv_two, stats[2], stats[3], samples)
    return (grad_one, grad_two, jnp.reshape(loss, (1,)))


def attend_kernel(count, begins, ends, *refs):
    q_one, q_two, stat_ref = refs[:3]
    blocks_one = refs[3 : 3 + count]
    blocks_two = refs[3 + count : 3 + 2 * count]
    rest = list(refs[3 + 2 * count :])
    loss_in = rest.pop(0)
    acc_in = None if begins else (rest.pop(0), rest.pop(0))
    held_one, held_two, gram_one, gram_two, round_one, round_two = rest[-6:]
    loss_out, *outs = rest[:-6]
    step = pl.program_id(0)
    tile = lax.rem(step, tiles)

    @pl.when(step == 0)
    def _():
        gram_one[...] = jnp.zeros_like(gram_one)
        gram_two[...] = jnp.zeros_like(gram_two)

    @pl.when(step < tiles)
    def _():
        for blocks, held, mean in ((blocks_one, held_one, 0), (blocks_two, held_two, 2)):
            start = 0
            for block in blocks:
                size = block.shape[0]
                normal = (block[...].astype(jnp.float32) - stat_ref[mean : mean + 1, :]) * stat_ref[
                    mean + 1 : mean + 2, :
                ]
                held[tile, start : start + size, :] = normal.astype(jnp.bfloat16)
                start += size
        for gram, queries, held in ((gram_one, q_one, held_one), (gram_two, q_two, held_two)):
            gram[...] += lax.dot_general(
                queries[...], held[tile], (((1,), (1,)), ((), ())), preferred_element_type=jnp.float32
            )

    @pl.when(step == tiles)
    def _():
        both = gram_one[...] * gram_two[...]
        height, width = both.shape
        folded = jnp.sum(both.reshape(height // 8, 8, width), axis=0)
        loss_out[...] = loss_in[...]
        for start in range(0, width, 128):
            loss_out[...] += folded[:, start : start + 128]
        round_one[...] = gram_one[...].astype(jnp.bfloat16)
        round_two[...] = gram_two[...].astype(jnp.bfloat16)

    @pl.when(step >= tiles)
    def _():
        for index, (gram, held) in enumerate(((round_two, held_one), (round_one, held_two))):
            total = jnp.dot(gram[...], held[tile], preferred_element_type=jnp.float32)
            if not begins:
                total += acc_in[index][...]
            if ends:
                share = total.shape[0] // 2
                outs[2 * index][...] = total[:share]
                outs[2 * index + 1][...] = total[share:].astype(jnp.bfloat16)
            else:
                outs[index][...] = total


def attend(q_one, q_two, stat, blocks_one, blocks_two, loss, acc, ends):
    rows, width = q_one.shape
    lanes = width // tiles
    keys = sum(block.shape[0] for block in blocks_one)
    count = len(blocks_one)
    begins = acc is None
    early = lambda step: (0, jnp.minimum(step, tiles - 1))
    late = lambda step: (0, jnp.maximum(step - tiles, 0))
    fixed = pl.BlockSpec((8, 128), lambda step: (0, 0))
    operands = [q_one, q_two, stat, *blocks_one, *blocks_two, loss]
    in_specs = [pl.BlockSpec((rows, lanes), early)] * 2 + [pl.BlockSpec((4, lanes), early)]
    in_specs += [pl.BlockSpec((block.shape[0], lanes), early) for block in blocks_one] * 2
    in_specs.append(fixed)
    out_specs = [fixed]
    out_shape = [jax.ShapeDtypeStruct((8, 128), jnp.float32)]
    aliases = {3 + 2 * count: 0}
    if not begins:
        operands += list(acc)
        in_specs += [pl.BlockSpec((rows, lanes), late)] * 2
    if ends:
        out_specs += [pl.BlockSpec((rows // 2, lanes), late)] * 4
        out_shape += [
            jax.ShapeDtypeStruct((rows // 2, width), jnp.float32),
            jax.ShapeDtypeStruct((rows // 2, width), jnp.bfloat16),
        ] * 2
    else:
        if not begins:
            aliases.update({4 + 2 * count: 1, 5 + 2 * count: 2})
        out_specs += [pl.BlockSpec((rows, lanes), late)] * 2
        out_shape += [jax.ShapeDtypeStruct((rows, width), jnp.float32)] * 2
    return pl.pallas_call(
        functools.partial(attend_kernel, count, begins, ends),
        grid=(2 * tiles,),
        in_specs=in_specs,
        out_specs=out_specs,
        out_shape=out_shape,
        scratch_shapes=[pltpu.VMEM((tiles, keys, lanes), jnp.bfloat16)] * 2
        + [pltpu.VMEM((rows, keys), jnp.float32)] * 2
        + [pltpu.VMEM((rows, keys), jnp.bfloat16)] * 2,
        input_output_aliases=aliases,
        compiler_params=pltpu.CompilerParams(vmem_limit_bytes=vmem),
        cost_estimate=pl.CostEstimate(flops=width, bytes_accessed=width, transcendentals=0),
        name="attend",
    )(*operands)


def totals_kernel(own_one, get_one, own_two, get_two, norm_one, norm_two, loss_ref, out_ref):
    acc_one = own_one[...] + get_one[...].astype(jnp.float32)
    acc_two = own_two[...] + get_two[...].astype(jnp.float32)
    one = norm_one[...].astype(jnp.float32)
    two = norm_two[...].astype(jnp.float32)
    loss = jnp.full((1, one.shape[1]), jnp.sum(loss_ref[...]), jnp.float32)
    for row, value in enumerate(
        (acc_one, acc_one * one, acc_two, acc_two * two, one, two, one * two)
    ):
        out_ref[row : row + 1, :] = jnp.sum(value, axis=0, keepdims=True)
    out_ref[7:8, :] = loss


def finish_kernel(
    samples, own_one, get_one, own_two, get_two, norm_one, norm_two, total_ref, stat_ref, *outs
):
    scale = 2.0 * off_weight / samples
    one = norm_one[...].astype(jnp.float32)
    two = norm_two[...].astype(jnp.float32)
    mixed = total_ref[6:7, :]
    corr = mixed / samples
    diag = (-2.0 * (1.0 - corr)).astype(jnp.bfloat16).astype(jnp.float32) - 2.0 * off_weight * corr
    for index, (own, get, mine, other, inv) in enumerate(
        ((own_one, get_one, one, two, 1), (own_two, get_two, two, one, 3))
    ):
        back = scale * (own[...] + get[...].astype(jnp.float32)) + other * diag
        sum_back = scale * total_ref[2 * index : 2 * index + 1, :]
        sum_back += total_ref[5 - index : 6 - index, :] * diag
        sum_prod = scale * total_ref[2 * index + 1 : 2 * index + 2, :] + mixed * diag
        grad = back - sum_back / samples - mine * (sum_prod / samples)
        outs[index][...] = (stat_ref[inv : inv + 1, :] * grad).astype(jnp.bfloat16)


def by_features(kernel, operands, heights, loss, out_heights, dtype, name):
    width = operands[0].shape[1]
    lanes = width // tiles
    place = lambda step: (0, step)
    in_specs = [pl.BlockSpec((height, lanes), place) for height in heights]
    if loss is not None:
        operands = (*operands, loss)
        in_specs.append(pl.BlockSpec(loss.shape, lambda step: (0, 0)))
    return pl.pallas_call(
        kernel,
        grid=(tiles,),
        in_specs=in_specs,
        out_specs=[pl.BlockSpec((height, lanes), place) for height in out_heights],
        out_shape=[jax.ShapeDtypeStruct((height, width), dtype) for height in out_heights],
        compiler_params=pltpu.CompilerParams(vmem_limit_bytes=vmem),
        cost_estimate=pl.CostEstimate(flops=width, bytes_accessed=width, transcendentals=0),
        name=name,
    )(*operands)


def ring_shards(view_one, view_two):
    rows, width = view_one.shape
    batches = lax.axis_size("batch")
    samples = rows * batches
    chips = batches // 2
    hops = chips // 2
    line = chips // 2
    order = [2 * r for r in range(line)] + [2 * r + 1 for r in reversed(range(line))]
    ahead = [
        (2 * order[r] + c, 2 * order[(r + 1) % chips] + c) for r in range(chips) for c in range(2)
    ]
    behind = [(there, here) for here, there in ahead]

    def swapped(value, bit):
        return lax.ppermute(value, "batch", [(i, i ^ bit) for i in range(batches)])

    values_one = view_one.astype(jnp.float32)
    values_two = view_two.astype(jnp.float32)
    sums = jnp.stack(
        [
            jnp.sum(values_one, axis=0),
            jnp.sum(values_one * values_one, axis=0),
            jnp.sum(values_two, axis=0),
            jnp.sum(values_two * values_two, axis=0),
        ]
    )
    sums = jnp.sum(lax.all_gather(sums, "batch", axis=0), axis=0) / samples
    mean_one, mean_two = sums[0], sums[2]
    inv_one = 1.0 / jnp.sqrt(sums[1] - mean_one * mean_one + 1e-05)
    inv_two = 1.0 / jnp.sqrt(sums[3] - mean_two * mean_two + 1e-05)
    stat = jnp.stack([mean_one, inv_one, mean_two, inv_two])

    def normed(view, mean, inv):
        both = jnp.concatenate([view, swapped(view, 1)], axis=0).astype(jnp.float32)
        return ((both - mean) * inv).astype(jnp.bfloat16)

    q_one = normed(view_one, mean_one, inv_one)
    q_two = normed(view_two, mean_two, inv_two)
    loss = jnp.zeros((8, 128), jnp.float32)
    acc = None
    ends = [[view_one, view_one], [view_two, view_two]]
    waiting = []
    for hop in range(hops):
        last = hop == hops - 1
        if hop > 1:
            blocks = waiting.pop(0)
            loss, *acc = attend(q_one, q_two, stat, *blocks, loss, acc, False)
            ends[0][0], ends[0][1], ends[1][0], ends[1][1], loss = lax.optimization_barrier(
                (*ends[0], *ends[1], loss)
            )
            if waiting:
                waiting[0] = (list(ends[0]), list(ends[1]))
        for pair in ends:
            up, down = pair
            if last:
                up, down = up[: rows // 2], down[rows // 2 :]
            pair[0] = lax.ppermute(up, "batch", ahead)
            pair[1] = lax.ppermute(down, "batch", behind)
        waiting.append((list(ends[0]), list(ends[1])))
    while len(waiting) > 1:
        blocks = waiting.pop(0)
        loss, *acc = attend(q_one, q_two, stat, *blocks, loss, acc, False)
    blocks = ([view_one, *waiting[0][0]], [view_two, *waiting[0][1]])
    loss, own_one, send_one, own_two, send_two = attend(
        q_one, q_two, stat, *blocks, loss, acc, True
    )
    get_one, get_two = swapped(send_one, 1), swapped(send_two, 1)
    parts = (own_one, get_one, own_two, get_two, q_one, q_two)
    heights = (rows,) * 6
    (total,) = by_features(totals_kernel, parts, heights, loss, (8,), jnp.float32, "totals")
    size = 1
    while size < batches:
        if size * 4 <= batches:
            near, far, both = (swapped(total, size * step) for step in (1, 2, 3))
            total = (total + near) + (far + both)
            size *= 4
        else:
            total = total + swapped(total, size)
            size *= 2
    grad_one, grad_two = by_features(
        functools.partial(finish_kernel, samples),
        (*parts, total, stat),
        (*heights, 8, 4),
        None,
        (rows, rows),
        jnp.bfloat16,
        "finish",
    )
    corr = total[6] / samples
    squares = total[7, 0] / (samples * samples)
    loss = jnp.sum((1.0 - corr) ** 2 - off_weight * corr * corr) + off_weight * squares
    return (grad_one, grad_two, jnp.reshape(loss / width, (1,)))


def solution(mesh):
    placed = (P(("groups", "batch"), "feat"), P(("groups", "batch"), "feat"))
    batches = mesh.shape["batch"]
    ringed = mesh.shape["feat"] == 1 and batches >= 8 and batches & (batches - 1) == 0
    return jax.shard_map(
        ring_shards if ringed else shards,
        mesh=mesh,
        in_specs=placed,
        out_specs=(P(("groups", "batch"), "feat"), P(("groups", "batch"), "feat"), P("groups")),
        check_vma=False,
    )
```

```python
import functools

import jax
import jax.numpy as jnp
from jax import lax
from jax.experimental import pallas as pl
from jax.experimental.pallas import tpu as pltpu
from jax.sharding import PartitionSpec as P

off_weight = 0.0051
tiles = 4
vmem = 56 * 1024 * 1024


def local_term(columns, full_two):
    return lax.dot_general(
        columns, full_two, (((0,), (0,)), ((), ())), preferred_element_type=jnp.float32
    )


def tile_grad(summed, row_base, samples):
    corr = summed / samples
    row_ids = row_base + lax.broadcasted_iota(jnp.int32, corr.shape, 0)
    col_ids = lax.broadcasted_iota(jnp.int32, corr.shape, 1)
    diag = row_ids == col_ids
    grad = jnp.where(diag, -2.0 * (1.0 - corr), 2.0 * off_weight * corr).astype(jnp.bfloat16)
    part_loss = jnp.sum(jnp.where(diag, (1.0 - corr) ** 2, off_weight * corr * corr))
    return (grad, part_loss)


def fold_step(columns, full_two, piece):
    contrib = lax.dot_general(
        full_two, piece, (((1,), (1,)), ((), ())), preferred_element_type=jnp.float32
    )
    back_mix = jnp.dot(columns, piece, preferred_element_type=jnp.float32)
    return (contrib, back_mix)


def finish(back, normed, inv, sum_back, sum_prod, samples):
    normal_f = normed.astype(jnp.float32)
    return (inv * (back - sum_back / samples - normal_f * sum_prod / samples)).astype(jnp.bfloat16)


def shards(view_one, view_two):
    rows, half_feat = view_one.shape
    batches = lax.axis_size("batch")
    samples = rows * batches
    values_one = view_one.astype(jnp.float32)
    values_two = view_two.astype(jnp.float32)
    sums = lax.psum(
        (
            jnp.sum(values_one, axis=0),
            jnp.sum(values_one * values_one, axis=0),
            jnp.sum(values_two, axis=0),
            jnp.sum(values_two * values_two, axis=0),
        ),
        "batch",
    )
    mean_one = sums[0] / samples
    mean_two = sums[2] / samples
    inv_one = 1.0 / jnp.sqrt(sums[1] / samples - mean_one * mean_one + 1e-05)
    inv_two = 1.0 / jnp.sqrt(sums[3] / samples - mean_two * mean_two + 1e-05)
    norm_one = ((values_one - mean_one) * inv_one).astype(jnp.bfloat16)
    norm_two = ((values_two - mean_two) * inv_two).astype(jnp.bfloat16)
    full_two = lax.all_gather(norm_two, "feat", axis=1, tiled=True)
    width = full_two.shape[1]
    tile = half_feat // batches
    row_base = lax.axis_index("feat") * half_feat + lax.axis_index("batch") * tile
    summed = lax.psum_scatter(
        local_term(norm_one, full_two), "batch", scatter_dimension=0, tiled=True
    )
    grad, part_loss = tile_grad(summed, row_base, samples)
    back_one, back_mix = fold_step(
        norm_one, full_two, lax.all_gather(grad, "batch", axis=0, tiled=True)
    )
    back_two = lax.psum_scatter(back_mix, "feat", scatter_dimension=1, tiled=True)
    loss = lax.psum(part_loss, ("batch", "feat")) / width
    norm_one_f = norm_one.astype(jnp.float32)
    norm_two_f = norm_two.astype(jnp.float32)
    stats = (
        lax.psum(jnp.sum(back_one, axis=0).astype(jnp.bfloat16), "batch").astype(jnp.float32),
        lax.psum(jnp.sum(back_one * norm_one_f, axis=0).astype(jnp.bfloat16), "batch").astype(
            jnp.float32
        ),
        lax.psum(jnp.sum(back_two, axis=0).astype(jnp.bfloat16), "batch").astype(jnp.float32),
        lax.psum(jnp.sum(back_two * norm_two_f, axis=0).astype(jnp.bfloat16), "batch").astype(
            jnp.float32
        ),
    )
    grad_one = finish(back_one, norm_one, inv_one, stats[0], stats[1], samples)
    grad_two = finish(back_two, norm_two, inv_two, stats[2], stats[3], samples)
    return (grad_one, grad_two, jnp.reshape(loss, (1,)))


def eight_rows(sums, loss):
    lanes = sums[0].shape[1]
    row = lax.broadcasted_iota(jnp.int32, (8, lanes), 0)
    loss = jnp.zeros((1, lanes), jnp.float32) + loss
    values = list(sums)
    for _ in range(3):
        part = loss.astype(jnp.bfloat16).astype(jnp.float32)
        values.append(part)
        loss = loss - part
    out = jnp.zeros((8, lanes), jnp.float32)
    for index, value in enumerate(values):
        out = jnp.where(row == index, value, out)
    return out.astype(jnp.bfloat16)


def add_kernel(*refs):
    terms = [ref[...].astype(jnp.float32) for ref in refs[:-1]]
    while len(terms) > 1:
        terms = [terms[k] + terms[k + 1] for k in range(0, len(terms), 2)]
    total = terms[0]
    loss = (total[4:5] + total[5:6]) + total[6:7]
    refs[-1][...] = eight_rows([total[k : k + 1] for k in range(4)], loss)


def attend_kernel(count, begins, ends, *refs):
    q_one, q_two, stat_ref = refs[:3]
    blocks_one = refs[3 : 3 + count]
    blocks_two = refs[3 + count : 3 + 2 * count]
    rest = list(refs[3 + 2 * count :])
    loss_in = rest.pop(0)
    acc_in = None if begins else (rest.pop(0), rest.pop(0))
    late = (rest.pop(0), rest.pop(0)) if ends else None
    held_one, held_two, gram_one, gram_two, round_one, round_two = rest[-6:]
    loss_out, *outs = rest[:-6]
    step = pl.program_id(0)
    tile = lax.rem(step, tiles)

    @pl.when(step == 0)
    def _():
        gram_one[...] = jnp.zeros_like(gram_one)
        gram_two[...] = jnp.zeros_like(gram_two)

    @pl.when(step < tiles)
    def _():
        for blocks, held, mean in ((blocks_one, held_one, 0), (blocks_two, held_two, 2)):
            start = 0
            for block in blocks:
                size = block.shape[0]
                normal = (block[...].astype(jnp.float32) - stat_ref[mean : mean + 1, :]) * stat_ref[
                    mean + 1 : mean + 2, :
                ]
                held[tile, start : start + size, :] = normal.astype(jnp.bfloat16)
                start += size
        for gram, queries, held in ((gram_one, q_one, held_one), (gram_two, q_two, held_two)):
            gram[...] += lax.dot_general(
                queries[...], held[tile], (((1,), (1,)), ((), ())), preferred_element_type=jnp.float32
            )

    @pl.when(step == tiles)
    def _():
        both = gram_one[...] * gram_two[...]
        height, width = both.shape
        folded = jnp.sum(both.reshape(height // 8, 8, width), axis=0)
        loss_out[...] = loss_in[...] + jnp.sum(folded) * (1.0 / 1024)
        round_one[...] = gram_one[...].astype(jnp.bfloat16)
        round_two[...] = gram_two[...].astype(jnp.bfloat16)

    @pl.when(step >= tiles)
    def _():
        sums = []
        for index, (gram, held) in enumerate(((round_two, held_one), (round_one, held_two))):
            total = jnp.dot(gram[...], held[tile], preferred_element_type=jnp.float32)
            if not begins:
                total += acc_in[index][...]
            if ends:
                share = total.shape[0] // 2
                outs[2 * index][...] = total[:share]
                outs[2 * index + 1][...] = total[share:].astype(jnp.bfloat16)
                prod = total * late[index][...].astype(jnp.float32)
                sums.append(jnp.sum(total, axis=0, keepdims=True))
                sums.append(jnp.sum(prod, axis=0, keepdims=True))
            else:
                outs[index][...] = total
        if ends:
            outs[4][...] = eight_rows(sums, jnp.sum(loss_out[...]))


def attend(q_one, q_two, stat, blocks_one, blocks_two, loss, acc, ends):
    rows, width = q_one.shape
    lanes = width // tiles
    keys = sum(block.shape[0] for block in blocks_one)
    count = len(blocks_one)
    begins = acc is None
    early = lambda step: (0, jnp.minimum(step, tiles - 1))
    late = lambda step: (0, jnp.maximum(step - tiles, 0))
    fixed = pl.BlockSpec((8, 128), lambda step: (0, 0))
    operands = [q_one, q_two, stat, *blocks_one, *blocks_two, loss]
    in_specs = [pl.BlockSpec((rows, lanes), early)] * 2 + [pl.BlockSpec((4, lanes), early)]
    in_specs += [pl.BlockSpec((block.shape[0], lanes), early) for block in blocks_one] * 2
    in_specs.append(fixed)
    out_specs = [fixed]
    out_shape = [jax.ShapeDtypeStruct((8, 128), jnp.float32)]
    aliases = {3 + 2 * count: 0}
    if not begins:
        operands += list(acc)
        in_specs += [pl.BlockSpec((rows, lanes), late)] * 2
    if ends:
        operands += [q_one, q_two]
        in_specs += [pl.BlockSpec((rows, lanes), late)] * 2
        out_specs += [pl.BlockSpec((rows // 2, lanes), late)] * 4
        out_shape += [
            jax.ShapeDtypeStruct((rows // 2, width), jnp.float32),
            jax.ShapeDtypeStruct((rows // 2, width), jnp.bfloat16),
        ] * 2
        out_specs.append(pl.BlockSpec((8, lanes), late))
        out_shape.append(jax.ShapeDtypeStruct((8, width), jnp.bfloat16))
    else:
        if not begins:
            aliases.update({4 + 2 * count: 1, 5 + 2 * count: 2})
        out_specs += [pl.BlockSpec((rows, lanes), late)] * 2
        out_shape += [jax.ShapeDtypeStruct((rows, width), jnp.float32)] * 2
    return pl.pallas_call(
        functools.partial(attend_kernel, count, begins, ends),
        grid=(2 * tiles,),
        in_specs=in_specs,
        out_specs=out_specs,
        out_shape=out_shape,
        scratch_shapes=[pltpu.VMEM((tiles, keys, lanes), jnp.bfloat16)] * 2
        + [pltpu.VMEM((rows, keys), jnp.float32)] * 2
        + [pltpu.VMEM((rows, keys), jnp.bfloat16)] * 2,
        input_output_aliases=aliases,
        compiler_params=pltpu.CompilerParams(vmem_limit_bytes=vmem),
        cost_estimate=pl.CostEstimate(flops=width, bytes_accessed=width, transcendentals=0),
        name="attend",
    )(*operands)


def finish_kernel(
    samples, own_one, get_one, own_two, get_two, norm_one, norm_two, total_ref, norm_ref, stat_ref, *outs
):
    scale = 2.0 * off_weight / samples
    one = norm_one[...].astype(jnp.float32)
    two = norm_two[...].astype(jnp.float32)
    mixed = norm_ref[2:3, :]
    total = total_ref[...].astype(jnp.float32)
    corr = mixed / samples
    diag = (-2.0 * (1.0 - corr)).astype(jnp.bfloat16).astype(jnp.float32) - 2.0 * off_weight * corr
    for index, (own, get, mine, other, inv) in enumerate(
        ((own_one, get_one, one, two, 1), (own_two, get_two, two, one, 3))
    ):
        back = scale * (own[...] + get[...].astype(jnp.float32)) + other * diag
        sum_back = scale * total[2 * index : 2 * index + 1, :]
        sum_back += norm_ref[1 - index : 2 - index, :] * diag
        sum_prod = scale * total[2 * index + 1 : 2 * index + 2, :] + mixed * diag
        grad = back - sum_back / samples - mine * (sum_prod / samples)
        outs[index][...] = (stat_ref[inv : inv + 1, :] * grad).astype(jnp.bfloat16)


def by_features(kernel, operands, heights, out_heights, dtype, name):
    width = operands[0].shape[1]
    lanes = width // tiles
    place = lambda step: (0, step)
    in_specs = [pl.BlockSpec((height, lanes), place) for height in heights]
    return pl.pallas_call(
        kernel,
        grid=(tiles,),
        in_specs=in_specs,
        out_specs=[pl.BlockSpec((height, lanes), place) for height in out_heights],
        out_shape=[jax.ShapeDtypeStruct((height, width), dtype) for height in out_heights],
        compiler_params=pltpu.CompilerParams(vmem_limit_bytes=vmem),
        cost_estimate=pl.CostEstimate(flops=width, bytes_accessed=width, transcendentals=0),
        name=name,
    )(*operands)


def ring_shards(view_one, view_two):
    rows, width = view_one.shape
    batches = lax.axis_size("batch")
    samples = rows * batches
    chips = batches // 2
    hops = chips // 2
    line = chips // 2
    order = [2 * r for r in range(line)] + [2 * r + 1 for r in reversed(range(line))]
    ahead = [
        (2 * order[r] + c, 2 * order[(r + 1) % chips] + c) for r in range(chips) for c in range(2)
    ]
    behind = [(there, here) for here, there in ahead]

    def swapped(value, bit):
        return lax.ppermute(value, "batch", [(i, i ^ bit) for i in range(batches)])

    def summed(rows_of_sums):
        return jnp.sum(lax.all_gather(jnp.stack(rows_of_sums), "batch", axis=0), axis=0)

    far_one, far_two = swapped(view_one, 1), swapped(view_two, 1)
    here_one, here_two, far_one, far_two = lax.optimization_barrier(
        (view_one, view_two, far_one, far_two)
    )
    values_one = here_one.astype(jnp.float32)
    values_two = here_two.astype(jnp.float32)
    sums = summed(
        [
            jnp.sum(values_one, axis=0),
            jnp.sum(values_one * values_one, axis=0),
            jnp.sum(values_two, axis=0),
            jnp.sum(values_two * values_two, axis=0),
        ]
    )
    sums = sums / samples
    mean_one, mean_two = sums[0], sums[2]
    inv_one = 1.0 / jnp.sqrt(sums[1] - mean_one * mean_one + 1e-05)
    inv_two = 1.0 / jnp.sqrt(sums[3] - mean_two * mean_two + 1e-05)
    stat = jnp.stack([mean_one, inv_one, mean_two, inv_two])

    def normed(view, far, mean, inv):
        both = jnp.concatenate([view, far], axis=0).astype(jnp.float32)
        return ((both - mean) * inv).astype(jnp.bfloat16)

    q_one = normed(here_one, far_one, mean_one, inv_one)
    q_two = normed(here_two, far_two, mean_two, inv_two)
    loss = jnp.zeros((8, 128), jnp.float32)
    loss, *acc = attend(q_one, q_two, stat, [here_one], [here_two], loss, None, False)
    mine_one = q_one[:rows].astype(jnp.float32)
    mine_two = q_two[:rows].astype(jnp.float32)
    norm_sums = summed(
        [jnp.sum(mine_one, axis=0), jnp.sum(mine_two, axis=0), jnp.sum(mine_one * mine_two, axis=0)]
    )
    flows = [[view_one, view_one], [view_two, view_two]]
    arrived = []
    for hop in range(hops):
        if hop > 1:
            loss, *acc = attend(q_one, q_two, stat, *arrived[hop - 2], loss, acc, False)
        arrived.append([])
        for view, pair in enumerate(flows):
            if hop > 1 and view == 1:
                *pair, loss, norm_sums = lax.optimization_barrier((*pair, loss, norm_sums))
                arrived[hop - 1][1] = list(pair)
            up, down = pair
            if hop == hops - 1:
                up, down = up[: rows // 2], down[rows // 2 :]
            flows[view] = [lax.ppermute(up, "batch", ahead), lax.ppermute(down, "batch", behind)]
            arrived[hop].append(list(flows[view]))
    loss, *acc = attend(q_one, q_two, stat, *arrived[hops - 2], loss, acc, False)
    arrived[-1][1][0], loss = lax.optimization_barrier((arrived[-1][1][0], loss))
    loss, own_one, send_one, own_two, send_two, total = attend(
        q_one, q_two, stat, *arrived[hops - 1], loss, acc, True
    )
    get_one, get_two = swapped(send_one, 1), swapped(send_two, 1)
    size = 1
    while size < batches:
        steps = (1, 2, 3) if size * 4 <= batches else (1,)
        terms = (total, *(swapped(total, size * step) for step in steps))
        (total,) = by_features(
            add_kernel, terms, (8,) * len(terms), (8,), jnp.bfloat16, "add_totals"
        )
        size *= len(terms)
    grad_one, grad_two = by_features(
        functools.partial(finish_kernel, samples),
        (own_one, get_one, own_two, get_two, q_one, q_two, total, norm_sums, stat),
        (*((rows,) * 6), 8, 3, 4),
        (rows, rows),
        jnp.bfloat16,
        "finish",
    )
    corr = norm_sums[2] / samples
    squares = jnp.sum(total[4:7, 0].astype(jnp.float32)) / (samples * samples)
    loss = jnp.sum((1.0 - corr) ** 2 - off_weight * corr * corr) + off_weight * squares
    return (grad_one, grad_two, jnp.reshape(loss / width, (1,)))


def solution(mesh):
    placed = (P(("groups", "batch"), "feat"), P(("groups", "batch"), "feat"))
    batches = mesh.shape["batch"]
    ringed = mesh.shape["feat"] == 1 and batches >= 8 and batches & (batches - 1) == 0
    return jax.shard_map(
        ring_shards if ringed else shards,
        mesh=mesh,
        in_specs=placed,
        out_specs=(P(("groups", "batch"), "feat"), P(("groups", "batch"), "feat"), P("groups")),
        check_vma=False,
    )
```

```python
import functools

import jax
import jax.numpy as jnp
from jax import lax
from jax.experimental import pallas as pl
from jax.experimental.pallas import tpu as pltpu
from jax.sharding import PartitionSpec as P

off_weight = 0.0051
tiles = 4
vmem = 56 * 1024 * 1024


def local_term(columns, full_two):
    return lax.dot_general(
        columns, full_two, (((0,), (0,)), ((), ())), preferred_element_type=jnp.float32
    )


def tile_grad(summed, row_base, samples):
    corr = summed / samples
    row_ids = row_base + lax.broadcasted_iota(jnp.int32, corr.shape, 0)
    col_ids = lax.broadcasted_iota(jnp.int32, corr.shape, 1)
    diag = row_ids == col_ids
    grad = jnp.where(diag, -2.0 * (1.0 - corr), 2.0 * off_weight * corr).astype(jnp.bfloat16)
    part_loss = jnp.sum(jnp.where(diag, (1.0 - corr) ** 2, off_weight * corr * corr))
    return (grad, part_loss)


def fold_step(columns, full_two, piece):
    contrib = lax.dot_general(
        full_two, piece, (((1,), (1,)), ((), ())), preferred_element_type=jnp.float32
    )
    back_mix = jnp.dot(columns, piece, preferred_element_type=jnp.float32)
    return (contrib, back_mix)


def finish(back, normed, inv, sum_back, sum_prod, samples):
    normal_f = normed.astype(jnp.float32)
    return (inv * (back - sum_back / samples - normal_f * sum_prod / samples)).astype(jnp.bfloat16)


def shards(view_one, view_two):
    rows, half_feat = view_one.shape
    batches = lax.axis_size("batch")
    samples = rows * batches
    values_one = view_one.astype(jnp.float32)
    values_two = view_two.astype(jnp.float32)
    sums = lax.psum(
        (
            jnp.sum(values_one, axis=0),
            jnp.sum(values_one * values_one, axis=0),
            jnp.sum(values_two, axis=0),
            jnp.sum(values_two * values_two, axis=0),
        ),
        "batch",
    )
    mean_one = sums[0] / samples
    mean_two = sums[2] / samples
    inv_one = 1.0 / jnp.sqrt(sums[1] / samples - mean_one * mean_one + 1e-05)
    inv_two = 1.0 / jnp.sqrt(sums[3] / samples - mean_two * mean_two + 1e-05)
    norm_one = ((values_one - mean_one) * inv_one).astype(jnp.bfloat16)
    norm_two = ((values_two - mean_two) * inv_two).astype(jnp.bfloat16)
    full_two = lax.all_gather(norm_two, "feat", axis=1, tiled=True)
    width = full_two.shape[1]
    tile = half_feat // batches
    row_base = lax.axis_index("feat") * half_feat + lax.axis_index("batch") * tile
    summed = lax.psum_scatter(
        local_term(norm_one, full_two), "batch", scatter_dimension=0, tiled=True
    )
    grad, part_loss = tile_grad(summed, row_base, samples)
    back_one, back_mix = fold_step(
        norm_one, full_two, lax.all_gather(grad, "batch", axis=0, tiled=True)
    )
    back_two = lax.psum_scatter(back_mix, "feat", scatter_dimension=1, tiled=True)
    loss = lax.psum(part_loss, ("batch", "feat")) / width
    norm_one_f = norm_one.astype(jnp.float32)
    norm_two_f = norm_two.astype(jnp.float32)
    stats = (
        lax.psum(jnp.sum(back_one, axis=0).astype(jnp.bfloat16), "batch").astype(jnp.float32),
        lax.psum(jnp.sum(back_one * norm_one_f, axis=0).astype(jnp.bfloat16), "batch").astype(
            jnp.float32
        ),
        lax.psum(jnp.sum(back_two, axis=0).astype(jnp.bfloat16), "batch").astype(jnp.float32),
        lax.psum(jnp.sum(back_two * norm_two_f, axis=0).astype(jnp.bfloat16), "batch").astype(
            jnp.float32
        ),
    )
    grad_one = finish(back_one, norm_one, inv_one, stats[0], stats[1], samples)
    grad_two = finish(back_two, norm_two, inv_two, stats[2], stats[3], samples)
    return (grad_one, grad_two, jnp.reshape(loss, (1,)))


def eight_rows(sums, loss):
    lanes = sums[0].shape[1]
    row = lax.broadcasted_iota(jnp.int32, (8, lanes), 0)
    loss = jnp.zeros((1, lanes), jnp.float32) + loss
    values = list(sums)
    for _ in range(3):
        part = loss.astype(jnp.bfloat16).astype(jnp.float32)
        values.append(part)
        loss = loss - part
    out = jnp.zeros((8, lanes), jnp.float32)
    for index, value in enumerate(values):
        out = jnp.where(row == index, value, out)
    return out.astype(jnp.bfloat16)


def add_kernel(*refs):
    terms = [ref[...].astype(jnp.float32) for ref in refs[:-1]]
    while len(terms) > 1:
        terms = [terms[k] + terms[k + 1] for k in range(0, len(terms), 2)]
    total = terms[0]
    loss = (total[4:5] + total[5:6]) + total[6:7]
    refs[-1][...] = eight_rows([total[k : k + 1] for k in range(4)], loss)


def attend_kernel(count, begins, ends, *refs):
    q_one, q_two, stat_ref = refs[:3]
    blocks_one = refs[3 : 3 + count]
    blocks_two = refs[3 + count : 3 + 2 * count]
    rest = list(refs[3 + 2 * count :])
    loss_in = rest.pop(0)
    acc_in = None if begins else (rest.pop(0), rest.pop(0))
    late = (rest.pop(0), rest.pop(0)) if ends else None
    held_one, held_two, gram_one, gram_two, round_one, round_two = rest[-6:]
    loss_out, *outs = rest[:-6]
    step = pl.program_id(0)
    tile = lax.rem(step, tiles)

    @pl.when(step == 0)
    def _():
        gram_one[...] = jnp.zeros_like(gram_one)
        gram_two[...] = jnp.zeros_like(gram_two)

    @pl.when(step < tiles)
    def _():
        for blocks, held, mean in ((blocks_one, held_one, 0), (blocks_two, held_two, 2)):
            start = 0
            for block in blocks:
                size = block.shape[0]
                normal = (block[...].astype(jnp.float32) - stat_ref[mean : mean + 1, :]) * stat_ref[
                    mean + 1 : mean + 2, :
                ]
                held[tile, start : start + size, :] = normal.astype(jnp.bfloat16)
                start += size
        for gram, queries, held in ((gram_one, q_one, held_one), (gram_two, q_two, held_two)):
            gram[...] += lax.dot_general(
                queries[...], held[tile], (((1,), (1,)), ((), ())), preferred_element_type=jnp.float32
            )

    @pl.when(step == tiles)
    def _():
        both = gram_one[...] * gram_two[...]
        height, width = both.shape
        folded = jnp.sum(both.reshape(height // 8, 8, width), axis=0)
        loss_out[...] = loss_in[...] + jnp.sum(folded) * (1.0 / 1024)
        round_one[...] = gram_one[...].astype(jnp.bfloat16)
        round_two[...] = gram_two[...].astype(jnp.bfloat16)

    @pl.when(step >= tiles)
    def _():
        sums = []
        for index, (gram, held) in enumerate(((round_two, held_one), (round_one, held_two))):
            total = jnp.dot(gram[...], held[tile], preferred_element_type=jnp.float32)
            if not begins:
                total += acc_in[index][...]
            if ends:
                share = total.shape[0] // 2
                outs[2 * index][...] = total[:share].astype(jnp.bfloat16)
                outs[2 * index + 1][...] = total[share:].astype(jnp.bfloat16)
                prod = total * late[index][...].astype(jnp.float32)
                sums.append(jnp.sum(total, axis=0, keepdims=True))
                sums.append(jnp.sum(prod, axis=0, keepdims=True))
            else:
                outs[index][...] = total
        if ends:
            outs[4][...] = eight_rows(sums, jnp.sum(loss_out[...]))


def attend(q_one, q_two, stat, blocks_one, blocks_two, loss, acc, ends):
    rows, width = q_one.shape
    lanes = width // tiles
    keys = sum(block.shape[0] for block in blocks_one)
    count = len(blocks_one)
    begins = acc is None
    early = lambda step: (0, jnp.minimum(step, tiles - 1))
    late = lambda step: (0, jnp.maximum(step - tiles, 0))
    fixed = pl.BlockSpec((8, 128), lambda step: (0, 0))
    operands = [q_one, q_two, stat, *blocks_one, *blocks_two, loss]
    in_specs = [pl.BlockSpec((rows, lanes), early)] * 2 + [pl.BlockSpec((4, lanes), early)]
    in_specs += [pl.BlockSpec((block.shape[0], lanes), early) for block in blocks_one] * 2
    in_specs.append(fixed)
    out_specs = [fixed]
    out_shape = [jax.ShapeDtypeStruct((8, 128), jnp.float32)]
    aliases = {3 + 2 * count: 0}
    if not begins:
        operands += list(acc)
        in_specs += [pl.BlockSpec((rows, lanes), late)] * 2
    if ends:
        operands += [q_one, q_two]
        in_specs += [pl.BlockSpec((rows, lanes), late)] * 2
        out_specs += [pl.BlockSpec((rows // 2, lanes), late)] * 4
        out_shape += [
            jax.ShapeDtypeStruct((rows // 2, width), jnp.bfloat16),
            jax.ShapeDtypeStruct((rows // 2, width), jnp.bfloat16),
        ] * 2
        out_specs.append(pl.BlockSpec((8, lanes), late))
        out_shape.append(jax.ShapeDtypeStruct((8, width), jnp.bfloat16))
    else:
        if not begins:
            aliases.update({4 + 2 * count: 1, 5 + 2 * count: 2})
        out_specs += [pl.BlockSpec((rows, lanes), late)] * 2
        out_shape += [jax.ShapeDtypeStruct((rows, width), jnp.float32)] * 2
    return pl.pallas_call(
        functools.partial(attend_kernel, count, begins, ends),
        grid=(2 * tiles,),
        in_specs=in_specs,
        out_specs=out_specs,
        out_shape=out_shape,
        scratch_shapes=[pltpu.VMEM((tiles, keys, lanes), jnp.bfloat16)] * 2
        + [pltpu.VMEM((rows, keys), jnp.float32)] * 2
        + [pltpu.VMEM((rows, keys), jnp.bfloat16)] * 2,
        input_output_aliases=aliases,
        compiler_params=pltpu.CompilerParams(vmem_limit_bytes=vmem),
        cost_estimate=pl.CostEstimate(flops=width, bytes_accessed=width, transcendentals=0),
        name="attend",
    )(*operands)


def finish_kernel(
    samples, own_one, get_one, own_two, get_two, norm_one, norm_two, total_ref, norm_ref, stat_ref, *outs
):
    scale = 2.0 * off_weight / samples
    one = norm_one[...].astype(jnp.float32)
    two = norm_two[...].astype(jnp.float32)
    mixed = norm_ref[2:3, :]
    total = total_ref[...].astype(jnp.float32)
    corr = mixed / samples
    diag = (-2.0 * (1.0 - corr)).astype(jnp.bfloat16).astype(jnp.float32) - 2.0 * off_weight * corr
    for index, (own, get, mine, other, inv) in enumerate(
        ((own_one, get_one, one, two, 1), (own_two, get_two, two, one, 3))
    ):
        back = scale * (own[...].astype(jnp.float32) + get[...].astype(jnp.float32)) + other * diag
        sum_back = scale * total[2 * index : 2 * index + 1, :]
        sum_back += norm_ref[1 - index : 2 - index, :] * diag
        sum_prod = scale * total[2 * index + 1 : 2 * index + 2, :] + mixed * diag
        grad = back - sum_back / samples - mine * (sum_prod / samples)
        outs[index][...] = (stat_ref[inv : inv + 1, :] * grad).astype(jnp.bfloat16)


def add_totals(terms):
    return pl.pallas_call(
        add_kernel,
        out_shape=jax.ShapeDtypeStruct(terms[0].shape, jnp.bfloat16),
        cost_estimate=pl.CostEstimate(flops=1, bytes_accessed=1, transcendentals=0),
        name="add_totals",
    )(*terms)


def by_features(kernel, operands, heights, out_heights, dtype, name):
    width = operands[0].shape[1]
    lanes = width // tiles
    place = lambda step: (0, step)
    in_specs = [pl.BlockSpec((height, lanes), place) for height in heights]
    return pl.pallas_call(
        kernel,
        grid=(tiles,),
        in_specs=in_specs,
        out_specs=[pl.BlockSpec((height, lanes), place) for height in out_heights],
        out_shape=[jax.ShapeDtypeStruct((height, width), dtype) for height in out_heights],
        compiler_params=pltpu.CompilerParams(vmem_limit_bytes=vmem),
        cost_estimate=pl.CostEstimate(flops=width, bytes_accessed=width, transcendentals=0),
        name=name,
    )(*operands)


def ring_shards(view_one, view_two):
    rows, width = view_one.shape
    batches = lax.axis_size("batch")
    samples = rows * batches
    chips = batches // 2
    hops = chips // 2
    line = chips // 2
    order = [2 * r for r in range(line)] + [2 * r + 1 for r in reversed(range(line))]
    ahead = [
        (2 * order[r] + c, 2 * order[(r + 1) % chips] + c) for r in range(chips) for c in range(2)
    ]
    behind = [(there, here) for here, there in ahead]

    def swapped(value, bit):
        return lax.ppermute(value, "batch", [(i, i ^ bit) for i in range(batches)])

    def reduced(total, add):
        size = 1
        while size < batches:
            steps = (1, 2, 3) if size * 4 <= batches else (1,)
            total = add([total, *(swapped(total, size * step) for step in steps)])
            size *= len(steps) + 1
        return total

    def norm_totals(q_one, q_two):
        one, two = (q[:rows].astype(jnp.float32) for q in (q_one, q_two))
        return summed([jnp.sum(one, axis=0), jnp.sum(two, axis=0), jnp.sum(one * two, axis=0)])

    def summed(rows_of_sums):
        return jnp.sum(lax.all_gather(jnp.stack(rows_of_sums), "batch", axis=0), axis=0)

    far_one, far_two = swapped(view_one, 1), swapped(view_two, 1)
    here_one, here_two, far_one, far_two = lax.optimization_barrier(
        (view_one, view_two, far_one, far_two)
    )
    values_one = here_one.astype(jnp.float32)
    values_two = here_two.astype(jnp.float32)
    sums = summed(
        [
            jnp.sum(values_one, axis=0),
            jnp.sum(values_one * values_one, axis=0),
            jnp.sum(values_two, axis=0),
            jnp.sum(values_two * values_two, axis=0),
        ]
    )
    sums = sums / samples
    mean_one, mean_two = sums[0], sums[2]
    inv_one = 1.0 / jnp.sqrt(sums[1] - mean_one * mean_one + 1e-05)
    inv_two = 1.0 / jnp.sqrt(sums[3] - mean_two * mean_two + 1e-05)
    stat = jnp.stack([mean_one, inv_one, mean_two, inv_two])

    def normed(view, far, mean, inv):
        both = jnp.concatenate([view, far], axis=0).astype(jnp.float32)
        return ((both - mean) * inv).astype(jnp.bfloat16)

    q_one = normed(here_one, far_one, mean_one, inv_one)
    q_two = normed(here_two, far_two, mean_two, inv_two)
    loss = jnp.zeros((8, 128), jnp.float32)
    acc = None
    ends = [[view_one, view_one], [view_two, view_two]]
    arrived = []
    norm_sums = None
    for hop in range(hops):
        if hop > 1:
            if hop == 2:
                loss, *acc = attend(q_one, q_two, stat, [here_one], [here_two], loss, acc, False)
            loss, *acc = attend(q_one, q_two, stat, *arrived[hop - 2], loss, acc, False)
            tied = (q_one, q_two) if norm_sums is None else (q_one, q_two, norm_sums)
            *flat, loss = lax.optimization_barrier((*ends[0], *ends[1], *tied, loss))
            ends = [flat[:2], flat[2:4]]
            q_one, q_two, *rest = flat[4:]
            arrived[-1] = [list(pair) for pair in ends]
            norm_sums = rest[0] if rest else norm_totals(q_one, q_two)
        for view, (up, down) in enumerate(ends):
            if hop == hops - 1:
                up, down = up[: rows // 2], down[rows // 2 :]
            ends[view] = [lax.ppermute(up, "batch", ahead), lax.ppermute(down, "batch", behind)]
        arrived.append([list(pair) for pair in ends])
    loss, *acc = attend(q_one, q_two, stat, *arrived[hops - 2], loss, acc, False)
    arrived[-1][1][0], loss = lax.optimization_barrier((arrived[-1][1][0], loss))
    loss, own_one, send_one, own_two, send_two, total = attend(
        q_one, q_two, stat, *arrived[hops - 1], loss, acc, True
    )
    get_one, get_two = swapped(send_one, 1), swapped(send_two, 1)
    total = reduced(total, add_totals)
    grad_one, grad_two = by_features(
        functools.partial(finish_kernel, samples),
        (own_one, get_one, own_two, get_two, q_one, q_two, total, norm_sums, stat),
        (*((rows,) * 6), 8, 3, 4),
        (rows, rows),
        jnp.bfloat16,
        "finish",
    )
    corr = norm_sums[2] / samples
    squares = jnp.sum(total[4:7, 0].astype(jnp.float32)) / (samples * samples)
    loss = jnp.sum((1.0 - corr) ** 2 - off_weight * corr * corr) + off_weight * squares
    return (grad_one, grad_two, jnp.reshape(loss / width, (1,)))


def solution(mesh):
    placed = (P(("groups", "batch"), "feat"), P(("groups", "batch"), "feat"))
    batches = mesh.shape["batch"]
    ringed = mesh.shape["feat"] == 1 and batches >= 8 and batches & (batches - 1) == 0
    return jax.shard_map(
        ring_shards if ringed else shards,
        mesh=mesh,
        in_specs=placed,
        out_specs=(P(("groups", "batch"), "feat"), P(("groups", "batch"), "feat"), P("groups")),
        check_vma=False,
    )
```

```python
import functools

import jax
import jax.numpy as jnp
from jax import lax
from jax.experimental import pallas as pl
from jax.experimental.pallas import tpu as pltpu
from jax.sharding import PartitionSpec as P

off_weight = 0.0051
tiles = 4
vmem = 56 * 1024 * 1024


def local_term(columns, full_two):
    return lax.dot_general(
        columns, full_two, (((0,), (0,)), ((), ())), preferred_element_type=jnp.float32
    )


def tile_grad(summed, row_base, samples):
    corr = summed / samples
    row_ids = row_base + lax.broadcasted_iota(jnp.int32, corr.shape, 0)
    col_ids = lax.broadcasted_iota(jnp.int32, corr.shape, 1)
    diag = row_ids == col_ids
    grad = jnp.where(diag, -2.0 * (1.0 - corr), 2.0 * off_weight * corr).astype(jnp.bfloat16)
    part_loss = jnp.sum(jnp.where(diag, (1.0 - corr) ** 2, off_weight * corr * corr))
    return (grad, part_loss)


def fold_step(columns, full_two, piece):
    contrib = lax.dot_general(
        full_two, piece, (((1,), (1,)), ((), ())), preferred_element_type=jnp.float32
    )
    back_mix = jnp.dot(columns, piece, preferred_element_type=jnp.float32)
    return (contrib, back_mix)


def finish(back, normed, inv, sum_back, sum_prod, samples):
    normal_f = normed.astype(jnp.float32)
    return (inv * (back - sum_back / samples - normal_f * sum_prod / samples)).astype(jnp.bfloat16)


def shards(view_one, view_two):
    rows, half_feat = view_one.shape
    batches = lax.axis_size("batch")
    samples = rows * batches
    values_one = view_one.astype(jnp.float32)
    values_two = view_two.astype(jnp.float32)
    sums = lax.psum(
        (
            jnp.sum(values_one, axis=0),
            jnp.sum(values_one * values_one, axis=0),
            jnp.sum(values_two, axis=0),
            jnp.sum(values_two * values_two, axis=0),
        ),
        "batch",
    )
    mean_one = sums[0] / samples
    mean_two = sums[2] / samples
    inv_one = 1.0 / jnp.sqrt(sums[1] / samples - mean_one * mean_one + 1e-05)
    inv_two = 1.0 / jnp.sqrt(sums[3] / samples - mean_two * mean_two + 1e-05)
    norm_one = ((values_one - mean_one) * inv_one).astype(jnp.bfloat16)
    norm_two = ((values_two - mean_two) * inv_two).astype(jnp.bfloat16)
    full_two = lax.all_gather(norm_two, "feat", axis=1, tiled=True)
    width = full_two.shape[1]
    tile = half_feat // batches
    row_base = lax.axis_index("feat") * half_feat + lax.axis_index("batch") * tile
    summed = lax.psum_scatter(
        local_term(norm_one, full_two), "batch", scatter_dimension=0, tiled=True
    )
    grad, part_loss = tile_grad(summed, row_base, samples)
    back_one, back_mix = fold_step(
        norm_one, full_two, lax.all_gather(grad, "batch", axis=0, tiled=True)
    )
    back_two = lax.psum_scatter(back_mix, "feat", scatter_dimension=1, tiled=True)
    loss = lax.psum(part_loss, ("batch", "feat")) / width
    norm_one_f = norm_one.astype(jnp.float32)
    norm_two_f = norm_two.astype(jnp.float32)
    stats = (
        lax.psum(jnp.sum(back_one, axis=0).astype(jnp.bfloat16), "batch").astype(jnp.float32),
        lax.psum(jnp.sum(back_one * norm_one_f, axis=0).astype(jnp.bfloat16), "batch").astype(
            jnp.float32
        ),
        lax.psum(jnp.sum(back_two, axis=0).astype(jnp.bfloat16), "batch").astype(jnp.float32),
        lax.psum(jnp.sum(back_two * norm_two_f, axis=0).astype(jnp.bfloat16), "batch").astype(
            jnp.float32
        ),
    )
    grad_one = finish(back_one, norm_one, inv_one, stats[0], stats[1], samples)
    grad_two = finish(back_two, norm_two, inv_two, stats[2], stats[3], samples)
    return (grad_one, grad_two, jnp.reshape(loss, (1,)))


def eight_rows(sums, loss):
    lanes = sums[0].shape[1]
    row = lax.broadcasted_iota(jnp.int32, (8, lanes), 0)
    loss = jnp.zeros((1, lanes), jnp.float32) + loss
    values = list(sums)
    for _ in range(3):
        part = loss.astype(jnp.bfloat16).astype(jnp.float32)
        values.append(part)
        loss = loss - part
    out = jnp.zeros((8, lanes), jnp.float32)
    for index, value in enumerate(values):
        out = jnp.where(row == index, value, out)
    return out.astype(jnp.bfloat16)


def add_kernel(*refs):
    terms = [ref[...].astype(jnp.float32) for ref in refs[:-1]]
    while len(terms) > 1:
        terms = [terms[k] + terms[k + 1] for k in range(0, len(terms), 2)]
    total = terms[0]
    loss = (total[4:5] + total[5:6]) + total[6:7]
    refs[-1][...] = eight_rows([total[k : k + 1] for k in range(4)], loss)


def attend_kernel(count, begins, ends, *refs):
    q_one, q_two, stat_ref = refs[:3]
    blocks_one = refs[3 : 3 + count]
    blocks_two = refs[3 + count : 3 + 2 * count]
    rest = list(refs[3 + 2 * count :])
    loss_in = rest.pop(0)
    acc_in = None if begins else (rest.pop(0), rest.pop(0))
    late = rest[-8:-6] if ends else ()
    held_one, held_two, gram_one, gram_two, round_one, round_two = rest[-6:]
    loss_out, *outs = rest[: -8 if ends else -6]
    step = pl.program_id(0)
    tile = lax.rem(step, tiles)

    @pl.when(step == 0)
    def _():
        gram_one[...] = jnp.zeros_like(gram_one)
        gram_two[...] = jnp.zeros_like(gram_two)

    @pl.when(step < tiles)
    def _():
        for kept, queries in zip(late, (q_one, q_two)):
            kept[tile] = queries[...]
        for blocks, held, mean in ((blocks_one, held_one, 0), (blocks_two, held_two, 2)):
            start = 0
            for block in blocks:
                size = block.shape[0]
                normal = (block[...].astype(jnp.float32) - stat_ref[mean : mean + 1, :]) * stat_ref[
                    mean + 1 : mean + 2, :
                ]
                held[tile, start : start + size, :] = normal.astype(jnp.bfloat16)
                start += size
        for gram, queries, held in ((gram_one, q_one, held_one), (gram_two, q_two, held_two)):
            gram[...] += lax.dot_general(
                queries[...], held[tile], (((1,), (1,)), ((), ())), preferred_element_type=jnp.float32
            )

    @pl.when(step == tiles)
    def _():
        both = gram_one[...] * gram_two[...]
        height, width = both.shape
        folded = jnp.sum(both.reshape(height // 8, 8, width), axis=0)
        loss_out[...] = loss_in[...] + jnp.sum(folded) * (1.0 / 1024)
        round_one[...] = gram_one[...].astype(jnp.bfloat16)
        round_two[...] = gram_two[...].astype(jnp.bfloat16)

    @pl.when(step >= tiles)
    def _():
        sums = []
        for index, (gram, held) in enumerate(((round_two, held_one), (round_one, held_two))):
            total = jnp.dot(gram[...], held[tile], preferred_element_type=jnp.float32)
            if not begins:
                total += acc_in[index][...].astype(jnp.float32)
            if ends:
                share = total.shape[0] // 2
                outs[2 * index][...] = total[:share].astype(jnp.bfloat16)
                outs[2 * index + 1][...] = total[share:].astype(jnp.bfloat16)
                prod = total * late[index][tile].astype(jnp.float32)
                sums.append(jnp.sum(total, axis=0, keepdims=True))
                sums.append(jnp.sum(prod, axis=0, keepdims=True))
            else:
                outs[index][...] = total.astype(outs[index].dtype)
        if ends:
            outs[4][...] = eight_rows(sums, jnp.sum(loss_out[...]))


def attend(
    q_one, q_two, stat, blocks_one, blocks_two, loss, acc, ends, dtype=jnp.float32
):
    rows, width = q_one.shape
    lanes = width // tiles
    keys = sum(block.shape[0] for block in blocks_one)
    count = len(blocks_one)
    begins = acc is None
    early = lambda step: (0, jnp.minimum(step, tiles - 1))
    late = lambda step: (0, jnp.maximum(step - tiles, 0))
    fixed = pl.BlockSpec((8, 128), lambda step: (0, 0))
    operands = [q_one, q_two, stat, *blocks_one, *blocks_two, loss]
    in_specs = [pl.BlockSpec((rows, lanes), early)] * 2 + [pl.BlockSpec((4, lanes), early)]
    in_specs += [pl.BlockSpec((block.shape[0], lanes), early) for block in blocks_one] * 2
    in_specs.append(fixed)
    out_specs = [fixed]
    out_shape = [jax.ShapeDtypeStruct((8, 128), jnp.float32)]
    aliases = {3 + 2 * count: 0}
    if not begins:
        operands += list(acc)
        in_specs += [pl.BlockSpec((rows, lanes), late)] * 2
    if ends:
        out_specs += [pl.BlockSpec((rows // 2, lanes), late)] * 4
        out_shape += [
            jax.ShapeDtypeStruct((rows // 2, width), jnp.bfloat16),
            jax.ShapeDtypeStruct((rows // 2, width), jnp.bfloat16),
        ] * 2
        out_specs.append(pl.BlockSpec((8, lanes), late))
        out_shape.append(jax.ShapeDtypeStruct((8, width), jnp.bfloat16))
    else:
        if not begins and dtype == jnp.float32:
            aliases.update({4 + 2 * count: 1, 5 + 2 * count: 2})
        out_specs += [pl.BlockSpec((rows, lanes), late)] * 2
        out_shape += [jax.ShapeDtypeStruct((rows, width), dtype)] * 2
    return pl.pallas_call(
        functools.partial(attend_kernel, count, begins, ends),
        grid=(2 * tiles,),
        in_specs=in_specs,
        out_specs=out_specs,
        out_shape=out_shape,
        scratch_shapes=[pltpu.VMEM((tiles, rows, lanes), jnp.bfloat16)] * (2 if ends else 0)
        + [pltpu.VMEM((tiles, keys, lanes), jnp.bfloat16)] * 2
        + [pltpu.VMEM((rows, keys), jnp.float32)] * 2
        + [pltpu.VMEM((rows, keys), jnp.bfloat16)] * 2,
        input_output_aliases=aliases,
        compiler_params=pltpu.CompilerParams(vmem_limit_bytes=vmem),
        cost_estimate=pl.CostEstimate(flops=width, bytes_accessed=width, transcendentals=0),
        name="attend",
    )(*operands)


def finish_kernel(
    samples, own_one, get_one, own_two, get_two, norm_one, norm_two, total_ref, norm_ref, stat_ref, *outs
):
    scale = 2.0 * off_weight / samples
    one = norm_one[...].astype(jnp.float32)
    two = norm_two[...].astype(jnp.float32)
    mixed = norm_ref[2:3, :]
    total = total_ref[...].astype(jnp.float32)
    corr = mixed / samples
    diag = (-2.0 * (1.0 - corr)).astype(jnp.bfloat16).astype(jnp.float32) - 2.0 * off_weight * corr
    squares = (total[4:5, :1] + total[5:6, :1]) + total[6:7, :1]
    part = jnp.sum((1.0 - corr) ** 2 - off_weight * corr * corr)

    @pl.when(pl.program_id(0) == 0)
    def _():
        outs[2][...] = jnp.zeros_like(outs[2]) + squares * (off_weight / (samples * samples))

    outs[2][...] += part
    for index, (own, get, mine, other, inv) in enumerate(
        ((own_one, get_one, one, two, 1), (own_two, get_two, two, one, 3))
    ):
        back = scale * (own[...].astype(jnp.float32) + get[...].astype(jnp.float32)) + other * diag
        sum_back = scale * total[2 * index : 2 * index + 1, :]
        sum_back += norm_ref[1 - index : 2 - index, :] * diag
        sum_prod = scale * total[2 * index + 1 : 2 * index + 2, :] + mixed * diag
        grad = back - sum_back / samples - mine * (sum_prod / samples)
        outs[index][...] = (stat_ref[inv : inv + 1, :] * grad).astype(jnp.bfloat16)


def add_totals(terms):
    return pl.pallas_call(
        add_kernel,
        out_shape=jax.ShapeDtypeStruct(terms[0].shape, jnp.bfloat16),
        cost_estimate=pl.CostEstimate(flops=1, bytes_accessed=1, transcendentals=0),
        name="add_totals",
    )(*terms)


def finish_grads(samples, operands, rows):
    width = operands[0].shape[1]
    lanes = width // tiles
    heights = (*((rows,) * 6), 8, 4, 4)
    place = lambda step: (0, step)
    return pl.pallas_call(
        functools.partial(finish_kernel, samples),
        grid=(tiles,),
        in_specs=[pl.BlockSpec((height, lanes), place) for height in heights],
        out_specs=[pl.BlockSpec((rows, lanes), place)] * 2
        + [pl.BlockSpec((8, 128), lambda step: (0, 0))],
        out_shape=[jax.ShapeDtypeStruct((rows, width), jnp.bfloat16)] * 2
        + [jax.ShapeDtypeStruct((8, 128), jnp.float32)],
        compiler_params=pltpu.CompilerParams(vmem_limit_bytes=vmem),
        cost_estimate=pl.CostEstimate(flops=width, bytes_accessed=width, transcendentals=0),
        name="finish",
    )(*operands)


def ring_shards(view_one, view_two):
    rows, width = view_one.shape
    batches = lax.axis_size("batch")
    samples = rows * batches
    chips = batches // 2
    hops = chips // 2
    line = chips // 2
    order = [2 * r for r in range(line)] + [2 * r + 1 for r in reversed(range(line))]
    ahead = [
        (2 * order[r] + c, 2 * order[(r + 1) % chips] + c) for r in range(chips) for c in range(2)
    ]
    behind = [(there, here) for here, there in ahead]

    def swapped(value, bit):
        return lax.ppermute(value, "batch", [(i, i ^ bit) for i in range(batches)])

    def reduced(total, add):
        size = 1
        while size < batches:
            steps = (1, 2, 3) if size * 4 <= batches else (1,)
            total = add([total, *(swapped(total, size * step) for step in steps)])
            size *= len(steps) + 1
        return total

    def norm_totals(q_one, q_two):
        one, two = (q[:rows].astype(jnp.float32) for q in (q_one, q_two))
        sums = [jnp.sum(one, axis=0), jnp.sum(two, axis=0), jnp.sum(one * two, axis=0)]
        return summed([*sums, jnp.zeros_like(sums[0])])

    def summed(rows_of_sums):
        return jnp.sum(lax.all_gather(jnp.stack(rows_of_sums), "batch", axis=0), axis=0)

    def statistics(one, two):
        one, two = one.astype(jnp.float32), two.astype(jnp.float32)
        sums = summed(
            [
                jnp.sum(one, axis=0),
                jnp.sum(one * one, axis=0),
                jnp.sum(two, axis=0),
                jnp.sum(two * two, axis=0),
            ]
        )
        sums = sums / samples
        inv_one = 1.0 / jnp.sqrt(sums[1] - sums[0] * sums[0] + 1e-05)
        inv_two = 1.0 / jnp.sqrt(sums[3] - sums[2] * sums[2] + 1e-05)
        return jnp.stack([sums[0], inv_one, sums[2], inv_two])

    def normed(view, far, mean, inv):
        both = jnp.concatenate([view, far], axis=0).astype(jnp.float32)
        return ((both - mean) * inv).astype(jnp.bfloat16)

    here_one, here_two = view_one, view_two
    far_one, far_two = swapped(view_one, 1), swapped(view_two, 1)
    ends = [[view_one, view_one], [view_two, view_two]]
    arrived = []
    acc = None
    loss = jnp.zeros((8, 128), jnp.float32)
    for hop in range(hops):
        if hop == 1:
            *ends[0], here_one, here_two, far_one, far_two = lax.optimization_barrier(
                (*ends[0], here_one, here_two, far_one, far_two)
            )
            arrived[0][0] = list(ends[0])
            stat = statistics(here_one, here_two)
        if hop == 2:
            *flat, stat = lax.optimization_barrier((*ends[0], *ends[1], stat))
            ends = [flat[:2], flat[2:]]
            arrived[1] = [list(pair) for pair in ends]
            q_one = normed(here_one, far_one, stat[0], stat[1])
            q_two = normed(here_two, far_two, stat[2], stat[3])
            norm_sums = norm_totals(q_one, q_two)
            loss, *acc = attend(q_one, q_two, stat, [here_one], [here_two], loss, acc, False)
            loss, *acc = attend(q_one, q_two, stat, *arrived[0], loss, acc, False)
        if hop > 2:
            loss, *acc = attend(q_one, q_two, stat, *arrived[hop - 2], loss, acc, False)
            *flat, norm_sums, loss = lax.optimization_barrier((*ends[0], *ends[1], norm_sums, loss))
            ends = [flat[:2], flat[2:]]
            arrived[-1] = [list(pair) for pair in ends]
        for view, (up, down) in enumerate(ends):
            if hop == hops - 1:
                up, down = up[: rows // 2], down[rows // 2 :]
            ends[view] = [lax.ppermute(up, "batch", ahead), lax.ppermute(down, "batch", behind)]
        arrived.append([list(pair) for pair in ends])
    loss, *acc = attend(
        q_one, q_two, stat, *arrived[hops - 2], loss, acc, False, dtype=jnp.bfloat16
    )
    arrived[-1][1][0], loss = lax.optimization_barrier((arrived[-1][1][0], loss))
    loss, own_one, send_one, own_two, send_two, total = attend(
        q_one, q_two, stat, *arrived[hops - 1], loss, acc, True
    )
    get_one, get_two = swapped(send_one, 1), swapped(send_two, 1)
    total = reduced(total, add_totals)
    grad_one, grad_two, loss = finish_grads(
        samples, (own_one, get_one, own_two, get_two, q_one, q_two, total, norm_sums, stat), rows
    )
    return (grad_one, grad_two, jnp.reshape(loss[0, :1] / width, (1,)))


def solution(mesh):
    placed = (P(("groups", "batch"), "feat"), P(("groups", "batch"), "feat"))
    batches = mesh.shape["batch"]
    ringed = mesh.shape["feat"] == 1 and batches >= 8 and batches & (batches - 1) == 0
    return jax.shard_map(
        ring_shards if ringed else shards,
        mesh=mesh,
        in_specs=placed,
        out_specs=(P(("groups", "batch"), "feat"), P(("groups", "batch"), "feat"), P("groups")),
        check_vma=False,
    )
```

```python
import functools

import jax
import jax.numpy as jnp
from jax import lax
from jax.experimental import pallas as pl
from jax.experimental.pallas import tpu as pltpu
from jax.sharding import PartitionSpec as P

off_weight = 0.0051
tiles = 4
vmem = 56 * 1024 * 1024


def local_term(columns, full_two):
    return lax.dot_general(
        columns, full_two, (((0,), (0,)), ((), ())), preferred_element_type=jnp.float32
    )


def tile_grad(summed, row_base, samples):
    corr = summed / samples
    row_ids = row_base + lax.broadcasted_iota(jnp.int32, corr.shape, 0)
    col_ids = lax.broadcasted_iota(jnp.int32, corr.shape, 1)
    diag = row_ids == col_ids
    grad = jnp.where(diag, -2.0 * (1.0 - corr), 2.0 * off_weight * corr).astype(jnp.bfloat16)
    part_loss = jnp.sum(jnp.where(diag, (1.0 - corr) ** 2, off_weight * corr * corr))
    return (grad, part_loss)


def fold_step(columns, full_two, piece):
    contrib = lax.dot_general(
        full_two, piece, (((1,), (1,)), ((), ())), preferred_element_type=jnp.float32
    )
    back_mix = jnp.dot(columns, piece, preferred_element_type=jnp.float32)
    return (contrib, back_mix)


def finish(back, normed, inv, sum_back, sum_prod, samples):
    normal_f = normed.astype(jnp.float32)
    return (inv * (back - sum_back / samples - normal_f * sum_prod / samples)).astype(jnp.bfloat16)


def shards(view_one, view_two):
    rows, half_feat = view_one.shape
    batches = lax.axis_size("batch")
    samples = rows * batches
    values_one = view_one.astype(jnp.float32)
    values_two = view_two.astype(jnp.float32)
    sums = lax.psum(
        (
            jnp.sum(values_one, axis=0),
            jnp.sum(values_one * values_one, axis=0),
            jnp.sum(values_two, axis=0),
            jnp.sum(values_two * values_two, axis=0),
        ),
        "batch",
    )
    mean_one = sums[0] / samples
    mean_two = sums[2] / samples
    inv_one = 1.0 / jnp.sqrt(sums[1] / samples - mean_one * mean_one + 1e-05)
    inv_two = 1.0 / jnp.sqrt(sums[3] / samples - mean_two * mean_two + 1e-05)
    norm_one = ((values_one - mean_one) * inv_one).astype(jnp.bfloat16)
    norm_two = ((values_two - mean_two) * inv_two).astype(jnp.bfloat16)
    full_two = lax.all_gather(norm_two, "feat", axis=1, tiled=True)
    width = full_two.shape[1]
    tile = half_feat // batches
    row_base = lax.axis_index("feat") * half_feat + lax.axis_index("batch") * tile
    summed = lax.psum_scatter(
        local_term(norm_one, full_two), "batch", scatter_dimension=0, tiled=True
    )
    grad, part_loss = tile_grad(summed, row_base, samples)
    back_one, back_mix = fold_step(
        norm_one, full_two, lax.all_gather(grad, "batch", axis=0, tiled=True)
    )
    back_two = lax.psum_scatter(back_mix, "feat", scatter_dimension=1, tiled=True)
    loss = lax.psum(part_loss, ("batch", "feat")) / width
    norm_one_f = norm_one.astype(jnp.float32)
    norm_two_f = norm_two.astype(jnp.float32)
    stats = (
        lax.psum(jnp.sum(back_one, axis=0).astype(jnp.bfloat16), "batch").astype(jnp.float32),
        lax.psum(jnp.sum(back_one * norm_one_f, axis=0).astype(jnp.bfloat16), "batch").astype(
            jnp.float32
        ),
        lax.psum(jnp.sum(back_two, axis=0).astype(jnp.bfloat16), "batch").astype(jnp.float32),
        lax.psum(jnp.sum(back_two * norm_two_f, axis=0).astype(jnp.bfloat16), "batch").astype(
            jnp.float32
        ),
    )
    grad_one = finish(back_one, norm_one, inv_one, stats[0], stats[1], samples)
    grad_two = finish(back_two, norm_two, inv_two, stats[2], stats[3], samples)
    return (grad_one, grad_two, jnp.reshape(loss, (1,)))


def eight_rows(sums, loss):
    lanes = sums[0].shape[1]
    row = lax.broadcasted_iota(jnp.int32, (8, lanes), 0)
    loss = jnp.zeros((1, lanes), jnp.float32) + loss
    values = list(sums)
    for _ in range(3):
        part = loss.astype(jnp.bfloat16).astype(jnp.float32)
        values.append(part)
        loss = loss - part
    out = jnp.zeros((8, lanes), jnp.float32)
    for index, value in enumerate(values):
        out = jnp.where(row == index, value, out)
    return out.astype(jnp.bfloat16)


def added(refs):
    terms = [ref[...].astype(jnp.float32) for ref in refs]
    while len(terms) > 1:
        terms = [terms[k] + terms[k + 1] for k in range(0, len(terms), 2)]
    return terms[0]


def sums_kernel(one_ref, two_ref, out_ref):
    for index, ref in enumerate((one_ref, two_ref)):
        values = ref[...].astype(jnp.float32)
        out_ref[2 * index : 2 * index + 1, :] = jnp.sum(values, axis=0, keepdims=True)
        out_ref[2 * index + 1 : 2 * index + 2, :] = jnp.sum(values * values, axis=0, keepdims=True)


def first_sums(one, two):
    rows, width = one.shape
    lanes = width // tiles
    place = lambda step: (0, step)
    return pl.pallas_call(
        sums_kernel,
        grid=(tiles,),
        in_specs=[pl.BlockSpec((rows, lanes), place)] * 2,
        out_specs=pl.BlockSpec((4, lanes), place),
        out_shape=jax.ShapeDtypeStruct((4, width), jnp.float32),
        cost_estimate=pl.CostEstimate(flops=width, bytes_accessed=width, transcendentals=0),
        name="first_sums",
    )(one, two)


def add_kernel(*refs):
    total = added(refs[:-1])
    loss = (total[4:5] + total[5:6]) + total[6:7]
    refs[-1][...] = eight_rows([total[k : k + 1] for k in range(4)], loss)


def attend_kernel(count, begins, ends, *refs):
    q_one, q_two, stat_ref = refs[:3]
    blocks_one = refs[3 : 3 + count]
    blocks_two = refs[3 + count : 3 + 2 * count]
    rest = list(refs[3 + 2 * count :])
    loss_in = rest.pop(0)
    acc_in = None if begins else (rest.pop(0), rest.pop(0))
    late = rest[-8:-6] if ends else ()
    held_one, held_two, gram_one, gram_two, round_one, round_two = rest[-6:]
    loss_out, *outs = rest[: -8 if ends else -6]
    step = pl.program_id(0)
    tile = lax.rem(step, tiles)

    @pl.when(step == 0)
    def _():
        gram_one[...] = jnp.zeros_like(gram_one)
        gram_two[...] = jnp.zeros_like(gram_two)

    @pl.when(step < tiles)
    def _():
        for kept, queries in zip(late, (q_one, q_two)):
            kept[tile] = queries[...]
        for blocks, held, mean in ((blocks_one, held_one, 0), (blocks_two, held_two, 2)):
            start = 0
            for block in blocks:
                size = block.shape[0]
                normal = (block[...].astype(jnp.float32) - stat_ref[mean : mean + 1, :]) * stat_ref[
                    mean + 1 : mean + 2, :
                ]
                held[tile, start : start + size, :] = normal.astype(jnp.bfloat16)
                start += size
        for gram, queries, held in ((gram_one, q_one, held_one), (gram_two, q_two, held_two)):
            gram[...] += lax.dot_general(
                queries[...], held[tile], (((1,), (1,)), ((), ())), preferred_element_type=jnp.float32
            )

    @pl.when(step == tiles)
    def _():
        both = gram_one[...] * gram_two[...]
        height, width = both.shape
        folded = jnp.sum(both.reshape(height // 8, 8, width), axis=0)
        loss_out[...] = loss_in[...] + jnp.sum(folded) * (1.0 / 1024)
        round_one[...] = gram_one[...].astype(jnp.bfloat16)
        round_two[...] = gram_two[...].astype(jnp.bfloat16)

    @pl.when(step >= tiles)
    def _():
        sums = []
        for index, (gram, held) in enumerate(((round_two, held_one), (round_one, held_two))):
            total = jnp.dot(gram[...], held[tile], preferred_element_type=jnp.float32)
            if not begins:
                total += acc_in[index][...].astype(jnp.float32)
            if ends:
                share = total.shape[0] // 2
                outs[2 * index][...] = total[:share].astype(jnp.bfloat16)
                outs[2 * index + 1][...] = total[share:].astype(jnp.bfloat16)
                prod = total * late[index][tile].astype(jnp.float32)
                sums.append(jnp.sum(total, axis=0, keepdims=True))
                sums.append(jnp.sum(prod, axis=0, keepdims=True))
            else:
                outs[index][...] = total.astype(outs[index].dtype)
        if ends:
            outs[4][...] = eight_rows(sums, jnp.sum(loss_out[...]))


def attend(
    q_one, q_two, stat, blocks_one, blocks_two, loss, acc, ends, dtype=jnp.float32
):
    rows, width = q_one.shape
    lanes = width // tiles
    keys = sum(block.shape[0] for block in blocks_one)
    count = len(blocks_one)
    begins = acc is None
    early = lambda step: (0, jnp.minimum(step, tiles - 1))
    late = lambda step: (0, jnp.maximum(step - tiles, 0))
    fixed = pl.BlockSpec((8, 128), lambda step: (0, 0))
    operands = [q_one, q_two, stat, *blocks_one, *blocks_two, loss]
    in_specs = [pl.BlockSpec((rows, lanes), early)] * 2 + [pl.BlockSpec((4, lanes), early)]
    in_specs += [pl.BlockSpec((block.shape[0], lanes), early) for block in blocks_one] * 2
    in_specs.append(fixed)
    out_specs = [fixed]
    out_shape = [jax.ShapeDtypeStruct((8, 128), jnp.float32)]
    aliases = {3 + 2 * count: 0}
    if not begins:
        operands += list(acc)
        in_specs += [pl.BlockSpec((rows, lanes), late)] * 2
    if ends:
        out_specs += [pl.BlockSpec((rows // 2, lanes), late)] * 4
        out_shape += [
            jax.ShapeDtypeStruct((rows // 2, width), jnp.bfloat16),
            jax.ShapeDtypeStruct((rows // 2, width), jnp.bfloat16),
        ] * 2
        out_specs.append(pl.BlockSpec((8, lanes), late))
        out_shape.append(jax.ShapeDtypeStruct((8, width), jnp.bfloat16))
    else:
        if not begins and dtype == jnp.float32:
            aliases.update({4 + 2 * count: 1, 5 + 2 * count: 2})
        out_specs += [pl.BlockSpec((rows, lanes), late)] * 2
        out_shape += [jax.ShapeDtypeStruct((rows, width), dtype)] * 2
    return pl.pallas_call(
        functools.partial(attend_kernel, count, begins, ends),
        grid=(2 * tiles,),
        in_specs=in_specs,
        out_specs=out_specs,
        out_shape=out_shape,
        scratch_shapes=[pltpu.VMEM((tiles, rows, lanes), jnp.bfloat16)] * (2 if ends else 0)
        + [pltpu.VMEM((tiles, keys, lanes), jnp.bfloat16)] * 2
        + [pltpu.VMEM((rows, keys), jnp.float32)] * 2
        + [pltpu.VMEM((rows, keys), jnp.bfloat16)] * 2,
        input_output_aliases=aliases,
        compiler_params=pltpu.CompilerParams(vmem_limit_bytes=vmem),
        cost_estimate=pl.CostEstimate(flops=width, bytes_accessed=width, transcendentals=0),
        name="attend",
    )(*operands)


def finish_kernel(
    samples, full, own_one, get_one, own_two, get_two, norm_one, norm_two, norm_ref, stat_ref, *rest
):
    outs = rest[-3:]
    scale = 2.0 * off_weight / samples
    one = norm_one[...].astype(jnp.float32)
    two = norm_two[...].astype(jnp.float32)
    mixed = norm_ref[2:3, :]
    total = added(rest[:-3])
    corr = mixed / samples
    diag = (-2.0 * (1.0 - corr)).astype(jnp.bfloat16).astype(jnp.float32) - 2.0 * off_weight * corr
    squares = jnp.max((total[4:5, :128] + total[5:6, :128]) + total[6:7, :128])
    part = jnp.sum((1.0 - corr) ** 2 - off_weight * corr * corr)

    @pl.when(pl.program_id(0) == 0)
    def _():
        outs[2][0] = squares * (off_weight / (samples * samples * full))

    outs[2][0] += part / full
    for index, (own, get, mine, other, inv) in enumerate(
        ((own_one, get_one, one, two, 1), (own_two, get_two, two, one, 3))
    ):
        back = scale * (own[...].astype(jnp.float32) + get[...].astype(jnp.float32)) + other * diag
        sum_back = scale * total[2 * index : 2 * index + 1, :]
        sum_back += norm_ref[1 - index : 2 - index, :] * diag
        sum_prod = scale * total[2 * index + 1 : 2 * index + 2, :] + mixed * diag
        grad = back - sum_back / samples - mine * (sum_prod / samples)
        outs[index][...] = (stat_ref[inv : inv + 1, :] * grad).astype(jnp.bfloat16)


def add_totals(terms):
    return pl.pallas_call(
        add_kernel,
        out_shape=jax.ShapeDtypeStruct(terms[0].shape, jnp.bfloat16),
        cost_estimate=pl.CostEstimate(flops=1, bytes_accessed=1, transcendentals=0),
        name="add_totals",
    )(*terms)


def finish_grads(samples, operands, rows):
    width = operands[0].shape[1]
    lanes = width // tiles
    heights = (*((rows,) * 6), 4, 4) + (8,) * (len(operands) - 8)
    place = lambda step: (0, step)
    return pl.pallas_call(
        functools.partial(finish_kernel, samples, width),
        grid=(tiles,),
        in_specs=[pl.BlockSpec((height, lanes), place) for height in heights],
        out_specs=[pl.BlockSpec((rows, lanes), place)] * 2
        + [pl.BlockSpec(memory_space=pltpu.SMEM)],
        out_shape=[jax.ShapeDtypeStruct((rows, width), jnp.bfloat16)] * 2
        + [jax.ShapeDtypeStruct((1,), jnp.float32)],
        compiler_params=pltpu.CompilerParams(vmem_limit_bytes=vmem),
        cost_estimate=pl.CostEstimate(flops=width, bytes_accessed=width, transcendentals=0),
        name="finish",
    )(*operands)


def ring_shards(view_one, view_two):
    rows, width = view_one.shape
    batches = lax.axis_size("batch")
    samples = rows * batches
    chips = batches // 2
    hops = chips // 2
    line = chips // 2
    order = [2 * r for r in range(line)] + [2 * r + 1 for r in reversed(range(line))]
    ahead = [
        (2 * order[r] + c, 2 * order[(r + 1) % chips] + c) for r in range(chips) for c in range(2)
    ]
    behind = [(there, here) for here, there in ahead]

    def swapped(value, bit):
        return lax.ppermute(value, "batch", [(i, i ^ bit) for i in range(batches)])

    def reduced(total, add):
        size = 1
        while size < batches:
            steps = (1, 2, 3) if size * 4 <= batches else (1,)
            terms = [total, *(swapped(total, size * step) for step in steps)]
            size *= len(steps) + 1
            total = add(terms) if size < batches else None
        return terms

    def norm_totals(q_one, q_two):
        one, two = (q[:rows].astype(jnp.float32) for q in (q_one, q_two))
        sums = [jnp.sum(one, axis=0), jnp.sum(two, axis=0), jnp.sum(one * two, axis=0)]
        return summed([*sums, jnp.zeros_like(sums[0])])

    def summed(rows_of_sums):
        return jnp.sum(lax.all_gather(jnp.stack(rows_of_sums), "batch", axis=0), axis=0)

    def statistics(one, two):
        sums = first_sums(one, two)
        sums = jnp.sum(lax.all_gather(sums, "batch", axis=0), axis=0) / samples
        inv_one = 1.0 / jnp.sqrt(sums[1] - sums[0] * sums[0] + 1e-05)
        inv_two = 1.0 / jnp.sqrt(sums[3] - sums[2] * sums[2] + 1e-05)
        return jnp.stack([sums[0], inv_one, sums[2], inv_two])

    def normed(view, far, mean, inv):
        both = jnp.concatenate([view, far], axis=0).astype(jnp.float32)
        return ((both - mean) * inv).astype(jnp.bfloat16)

    stat = statistics(view_one, view_two)
    far_one, far_two = swapped(view_one, 1), swapped(view_two, 1)
    q_one = normed(view_one, far_one, stat[0], stat[1])
    q_two = normed(view_two, far_two, stat[2], stat[3])
    ends = [[view_one, view_one], [view_two, view_two]]
    arrived = []
    loss = jnp.zeros((8, 128), jnp.float32)
    loss, *acc = attend(q_one, q_two, stat, [view_one], [view_two], loss, None, False)
    for hop in range(hops):
        if hop > 1:
            loss, *acc = attend(q_one, q_two, stat, *arrived[hop - 2], loss, acc, False)
            tied = (q_one, q_two) if hop == 2 else (norm_sums,)
            *flat, loss = lax.optimization_barrier((*ends[0], *ends[1], *tied, loss))
            ends = [flat[:2], flat[2:4]]
            arrived[-1] = [list(pair) for pair in ends]
            if hop == 2:
                q_one, q_two = flat[4:]
                norm_sums = norm_totals(q_one, q_two)
            else:
                norm_sums = flat[4]
        if hop < hops - 1:
            ends = [
                [lax.ppermute(up, "batch", ahead), lax.ppermute(down, "batch", behind)]
                for up, down in ends
            ]
            arrived.append([list(pair) for pair in ends])
        else:
            last_one = lax.ppermute(ends[0][0], "batch", ahead)
            last_two = lax.ppermute(ends[1][1], "batch", behind)
    loss, *acc = attend(
        q_one, q_two, stat, *arrived[hops - 2], loss, acc, False, dtype=jnp.bfloat16
    )
    last_one, last_two, loss = lax.optimization_barrier((last_one, last_two, loss))
    loss, own_one, send_one, own_two, send_two, total = attend(
        q_one, q_two, stat, [last_one], [last_two], loss, acc, True
    )
    get_one, get_two = swapped(send_one, 1), swapped(send_two, 1)
    terms = reduced(total, add_totals)
    grad_one, grad_two, loss = finish_grads(
        samples, (own_one, get_one, own_two, get_two, q_one, q_two, norm_sums, stat, *terms), rows
    )
    return (grad_one, grad_two, loss)


def solution(mesh):
    placed = (P(("groups", "batch"), "feat"), P(("groups", "batch"), "feat"))
    batches = mesh.shape["batch"]
    ringed = mesh.shape["feat"] == 1 and batches >= 8 and batches & (batches - 1) == 0
    return jax.shard_map(
        ring_shards if ringed else shards,
        mesh=mesh,
        in_specs=placed,
        out_specs=(P(("groups", "batch"), "feat"), P(("groups", "batch"), "feat"), P("groups")),
        check_vma=False,
    )
```

```python
import functools

import jax
import jax.numpy as jnp
from jax import lax
from jax.experimental import pallas as pl
from jax.experimental.pallas import tpu as pltpu
from jax.sharding import PartitionSpec as P

off_weight = 0.0051
tiles = 4
vmem = 36 * 1024 * 1024


def local_term(columns, full_two):
    return lax.dot_general(
        columns, full_two, (((0,), (0,)), ((), ())), preferred_element_type=jnp.float32
    )


def tile_grad(summed, row_base, samples):
    corr = summed / samples
    row_ids = row_base + lax.broadcasted_iota(jnp.int32, corr.shape, 0)
    col_ids = lax.broadcasted_iota(jnp.int32, corr.shape, 1)
    diag = row_ids == col_ids
    grad = jnp.where(diag, -2.0 * (1.0 - corr), 2.0 * off_weight * corr).astype(jnp.bfloat16)
    part_loss = jnp.sum(jnp.where(diag, (1.0 - corr) ** 2, off_weight * corr * corr))
    return (grad, part_loss)


def fold_step(columns, full_two, piece):
    contrib = lax.dot_general(
        full_two, piece, (((1,), (1,)), ((), ())), preferred_element_type=jnp.float32
    )
    back_mix = jnp.dot(columns, piece, preferred_element_type=jnp.float32)
    return (contrib, back_mix)


def finish(back, normed, inv, sum_back, sum_prod, samples):
    normal_f = normed.astype(jnp.float32)
    return (inv * (back - sum_back / samples - normal_f * sum_prod / samples)).astype(jnp.bfloat16)


def shards(view_one, view_two):
    rows, half_feat = view_one.shape
    batches = lax.axis_size("batch")
    samples = rows * batches
    values_one = view_one.astype(jnp.float32)
    values_two = view_two.astype(jnp.float32)
    sums = lax.psum(
        (
            jnp.sum(values_one, axis=0),
            jnp.sum(values_one * values_one, axis=0),
            jnp.sum(values_two, axis=0),
            jnp.sum(values_two * values_two, axis=0),
        ),
        "batch",
    )
    mean_one = sums[0] / samples
    mean_two = sums[2] / samples
    inv_one = 1.0 / jnp.sqrt(sums[1] / samples - mean_one * mean_one + 1e-05)
    inv_two = 1.0 / jnp.sqrt(sums[3] / samples - mean_two * mean_two + 1e-05)
    norm_one = ((values_one - mean_one) * inv_one).astype(jnp.bfloat16)
    norm_two = ((values_two - mean_two) * inv_two).astype(jnp.bfloat16)
    full_two = lax.all_gather(norm_two, "feat", axis=1, tiled=True)
    width = full_two.shape[1]
    tile = half_feat // batches
    row_base = lax.axis_index("feat") * half_feat + lax.axis_index("batch") * tile
    summed = lax.psum_scatter(
        local_term(norm_one, full_two), "batch", scatter_dimension=0, tiled=True
    )
    grad, part_loss = tile_grad(summed, row_base, samples)
    back_one, back_mix = fold_step(
        norm_one, full_two, lax.all_gather(grad, "batch", axis=0, tiled=True)
    )
    back_two = lax.psum_scatter(back_mix, "feat", scatter_dimension=1, tiled=True)
    loss = lax.psum(part_loss, ("batch", "feat")) / width
    norm_one_f = norm_one.astype(jnp.float32)
    norm_two_f = norm_two.astype(jnp.float32)
    stats = (
        lax.psum(jnp.sum(back_one, axis=0).astype(jnp.bfloat16), "batch").astype(jnp.float32),
        lax.psum(jnp.sum(back_one * norm_one_f, axis=0).astype(jnp.bfloat16), "batch").astype(
            jnp.float32
        ),
        lax.psum(jnp.sum(back_two, axis=0).astype(jnp.bfloat16), "batch").astype(jnp.float32),
        lax.psum(jnp.sum(back_two * norm_two_f, axis=0).astype(jnp.bfloat16), "batch").astype(
            jnp.float32
        ),
    )
    grad_one = finish(back_one, norm_one, inv_one, stats[0], stats[1], samples)
    grad_two = finish(back_two, norm_two, inv_two, stats[2], stats[3], samples)
    return (grad_one, grad_two, jnp.reshape(loss, (1,)))


def eight_rows(sums, loss):
    lanes = sums[0].shape[1]
    row = lax.broadcasted_iota(jnp.int32, (8, lanes), 0)
    loss = jnp.zeros((1, lanes), jnp.float32) + loss
    values = list(sums)
    for _ in range(3):
        part = loss.astype(jnp.bfloat16).astype(jnp.float32)
        values.append(part)
        loss = loss - part
    out = jnp.zeros((8, lanes), jnp.float32)
    for index, value in enumerate(values):
        out = jnp.where(row == index, value, out)
    return out.astype(jnp.bfloat16)


def added(refs):
    terms = [ref[...].astype(jnp.float32) for ref in refs]
    while len(terms) > 1:
        terms = [terms[k] + terms[k + 1] for k in range(0, len(terms), 2)]
    return terms[0]


def sums_kernel(one_ref, two_ref, out_ref):
    for index, ref in enumerate((one_ref, two_ref)):
        values = ref[...].astype(jnp.float32)
        out_ref[2 * index : 2 * index + 1, :] = jnp.sum(values, axis=0, keepdims=True)
        out_ref[2 * index + 1 : 2 * index + 2, :] = jnp.sum(values * values, axis=0, keepdims=True)


def first_sums(one, two):
    width = one.shape[1]
    return pl.pallas_call(
        sums_kernel,
        out_shape=jax.ShapeDtypeStruct((4, width), jnp.float32),
        cost_estimate=pl.CostEstimate(flops=width, bytes_accessed=width, transcendentals=0),
        name="first_sums",
    )(one, two)


def add_kernel(*refs):
    total = added(refs[:-1])
    loss = (total[4:5] + total[5:6]) + total[6:7]
    refs[-1][...] = eight_rows([total[k : k + 1] for k in range(4)], loss)


def attend_kernel(count, begins, ends, *refs):
    q_one, q_two, stat_ref = refs[:3]
    blocks_one = refs[3 : 3 + count]
    blocks_two = refs[3 + count : 3 + 2 * count]
    rest = list(refs[3 + 2 * count :])
    loss_in = rest.pop(0)
    acc_in = None if begins else (rest.pop(0), rest.pop(0))
    late = rest[-8:-6] if ends else ()
    held_one, held_two, gram_one, gram_two, round_one, round_two = rest[-6:]
    loss_out, *outs = rest[: -8 if ends else -6]
    step = pl.program_id(0)
    tile = lax.rem(step, tiles)

    @pl.when(step == 0)
    def _():
        gram_one[...] = jnp.zeros_like(gram_one)
        gram_two[...] = jnp.zeros_like(gram_two)

    @pl.when(step < tiles)
    def _():
        for kept, queries in zip(late, (q_one, q_two)):
            kept[tile] = queries[...]
        for blocks, held, mean in ((blocks_one, held_one, 0), (blocks_two, held_two, 2)):
            start = 0
            for block in blocks:
                size = block.shape[0]
                normal = (block[...].astype(jnp.float32) - stat_ref[mean : mean + 1, :]) * stat_ref[
                    mean + 1 : mean + 2, :
                ]
                held[tile, start : start + size, :] = normal.astype(jnp.bfloat16)
                start += size
        for gram, queries, held in ((gram_one, q_one, held_one), (gram_two, q_two, held_two)):
            gram[...] += lax.dot_general(
                queries[...], held[tile], (((1,), (1,)), ((), ())), preferred_element_type=jnp.float32
            )

    @pl.when(step == tiles)
    def _():
        both = gram_one[...] * gram_two[...]
        height, width = both.shape
        folded = jnp.sum(both.reshape(height // 8, 8, width), axis=0)
        loss_out[...] = loss_in[...] + jnp.sum(folded) * (1.0 / 1024)
        round_one[...] = gram_one[...].astype(jnp.bfloat16)
        round_two[...] = gram_two[...].astype(jnp.bfloat16)

    @pl.when(step >= tiles)
    def _():
        sums = []
        for index, (gram, held) in enumerate(((round_two, held_one), (round_one, held_two))):
            total = jnp.dot(gram[...], held[tile], preferred_element_type=jnp.float32)
            if not begins:
                total += acc_in[index][...].astype(jnp.float32)
            if ends:
                share = total.shape[0] // 2
                outs[2 * index][...] = total[:share].astype(jnp.bfloat16)
                outs[2 * index + 1][...] = total[share:].astype(jnp.bfloat16)
                prod = total * late[index][tile].astype(jnp.float32)
                sums.append(jnp.sum(total, axis=0, keepdims=True))
                sums.append(jnp.sum(prod, axis=0, keepdims=True))
            else:
                outs[index][...] = total.astype(outs[index].dtype)
        if ends:
            outs[4][...] = eight_rows(sums, jnp.sum(loss_out[...]))


def attend(
    q_one, q_two, stat, blocks_one, blocks_two, loss, acc, ends, dtype=jnp.float32
):
    rows, width = q_one.shape
    lanes = width // tiles
    keys = sum(block.shape[0] for block in blocks_one)
    count = len(blocks_one)
    begins = acc is None
    early = lambda step: (0, jnp.minimum(step, tiles - 1))
    late = lambda step: (0, jnp.maximum(step - tiles, 0))
    fixed = pl.BlockSpec((8, 128), lambda step: (0, 0))
    operands = [q_one, q_two, stat, *blocks_one, *blocks_two, loss]
    in_specs = [pl.BlockSpec((rows, lanes), early)] * 2 + [pl.BlockSpec((4, lanes), early)]
    in_specs += [pl.BlockSpec((block.shape[0], lanes), early) for block in blocks_one] * 2
    in_specs.append(fixed)
    out_specs = [fixed]
    out_shape = [jax.ShapeDtypeStruct((8, 128), jnp.float32)]
    aliases = {3 + 2 * count: 0}
    if not begins:
        operands += list(acc)
        in_specs += [pl.BlockSpec((rows, lanes), late)] * 2
    if ends:
        out_specs += [pl.BlockSpec((rows // 2, lanes), late)] * 4
        out_shape += [
            jax.ShapeDtypeStruct((rows // 2, width), jnp.bfloat16),
            jax.ShapeDtypeStruct((rows // 2, width), jnp.bfloat16),
        ] * 2
        out_specs.append(pl.BlockSpec((8, lanes), late))
        out_shape.append(jax.ShapeDtypeStruct((8, width), jnp.bfloat16))
    else:
        if not begins and dtype == jnp.float32:
            aliases.update({4 + 2 * count: 1, 5 + 2 * count: 2})
        out_specs += [pl.BlockSpec((rows, lanes), late)] * 2
        out_shape += [jax.ShapeDtypeStruct((rows, width), dtype)] * 2
    return pl.pallas_call(
        functools.partial(attend_kernel, count, begins, ends),
        grid=(2 * tiles,),
        in_specs=in_specs,
        out_specs=out_specs,
        out_shape=out_shape,
        scratch_shapes=[pltpu.VMEM((tiles, rows, lanes), jnp.bfloat16)] * (2 if ends else 0)
        + [pltpu.VMEM((tiles, keys, lanes), jnp.bfloat16)] * 2
        + [pltpu.VMEM((rows, keys), jnp.float32)] * 2
        + [pltpu.VMEM((rows, keys), jnp.bfloat16)] * 2,
        input_output_aliases=aliases,
        compiler_params=pltpu.CompilerParams(vmem_limit_bytes=vmem),
        cost_estimate=pl.CostEstimate(flops=width, bytes_accessed=width, transcendentals=0),
        name="attend",
    )(*operands)


def finish_kernel(
    samples, full, own_one, get_one, own_two, get_two, norm_one, norm_two, norm_ref, stat_ref, *rest
):
    outs = rest[-3:]
    scale = 2.0 * off_weight / samples
    one = norm_one[...].astype(jnp.float32)
    two = norm_two[...].astype(jnp.float32)
    mixed = norm_ref[2:3, :]
    total = added(rest[:-3])
    corr = mixed / samples
    diag = (-2.0 * (1.0 - corr)).astype(jnp.bfloat16).astype(jnp.float32) - 2.0 * off_weight * corr
    squares = jnp.max((total[4:5, :128] + total[5:6, :128]) + total[6:7, :128])
    part = jnp.sum((1.0 - corr) ** 2 - off_weight * corr * corr)

    @pl.when(pl.program_id(0) == 0)
    def _():
        outs[2][0] = squares * (off_weight / (samples * samples * full))

    outs[2][0] += part / full
    for index, (own, get, mine, other, inv) in enumerate(
        ((own_one, get_one, one, two, 1), (own_two, get_two, two, one, 3))
    ):
        back = scale * (own[...].astype(jnp.float32) + get[...].astype(jnp.float32)) + other * diag
        sum_back = scale * total[2 * index : 2 * index + 1, :]
        sum_back += norm_ref[1 - index : 2 - index, :] * diag
        sum_prod = scale * total[2 * index + 1 : 2 * index + 2, :] + mixed * diag
        grad = back - sum_back / samples - mine * (sum_prod / samples)
        outs[index][...] = (stat_ref[inv : inv + 1, :] * grad).astype(jnp.bfloat16)


def add_totals(terms):
    return pl.pallas_call(
        add_kernel,
        out_shape=jax.ShapeDtypeStruct(terms[0].shape, jnp.bfloat16),
        cost_estimate=pl.CostEstimate(flops=1, bytes_accessed=1, transcendentals=0),
        name="add_totals",
    )(*terms)


def finish_grads(samples, operands, rows):
    width = operands[0].shape[1]
    lanes = width // tiles
    heights = (*((rows,) * 6), 4, 4) + (8,) * (len(operands) - 8)
    place = lambda step: (0, step)
    return pl.pallas_call(
        functools.partial(finish_kernel, samples, width),
        grid=(tiles,),
        in_specs=[pl.BlockSpec((height, lanes), place) for height in heights],
        out_specs=[pl.BlockSpec((rows, lanes), place)] * 2
        + [pl.BlockSpec(memory_space=pltpu.SMEM)],
        out_shape=[jax.ShapeDtypeStruct((rows, width), jnp.bfloat16)] * 2
        + [jax.ShapeDtypeStruct((1,), jnp.float32)],
        compiler_params=pltpu.CompilerParams(vmem_limit_bytes=vmem),
        cost_estimate=pl.CostEstimate(flops=width, bytes_accessed=width, transcendentals=0),
        name="finish",
    )(*operands)


def ring_shards(view_one, view_two):
    rows, width = view_one.shape
    batches = lax.axis_size("batch")
    samples = rows * batches
    chips = batches // 2
    hops = chips // 2
    line = chips // 2
    order = [2 * r for r in range(line)] + [2 * r + 1 for r in reversed(range(line))]
    ahead = [
        (2 * order[r] + c, 2 * order[(r + 1) % chips] + c) for r in range(chips) for c in range(2)
    ]
    behind = [(there, here) for here, there in ahead]

    def swapped(value, bit):
        return lax.ppermute(value, "batch", [(i, i ^ bit) for i in range(batches)])

    def reduced(total, add):
        size = 1
        while size < batches:
            steps = (1, 2, 3) if size * 4 <= batches else (1,)
            terms = [total, *(swapped(total, size * step) for step in steps)]
            size *= len(steps) + 1
            total = add(terms) if size < batches else None
        return terms

    def norm_totals(q_one, q_two):
        one, two = (q[:rows].astype(jnp.float32) for q in (q_one, q_two))
        sums = [jnp.sum(one, axis=0), jnp.sum(two, axis=0), jnp.sum(one * two, axis=0)]
        return summed([*sums, jnp.zeros_like(sums[0])])

    def summed(rows_of_sums):
        return jnp.sum(lax.all_gather(jnp.stack(rows_of_sums), "batch", axis=0), axis=0)

    def statistics(one, two):
        sums = first_sums(one, two)
        sums = jnp.sum(lax.all_gather(sums, "batch", axis=0), axis=0) / samples
        inv_one = 1.0 / jnp.sqrt(sums[1] - sums[0] * sums[0] + 1e-05)
        inv_two = 1.0 / jnp.sqrt(sums[3] - sums[2] * sums[2] + 1e-05)
        return jnp.stack([sums[0], inv_one, sums[2], inv_two])

    def normed(view, far, mean, inv):
        both = jnp.concatenate([view, far], axis=0).astype(jnp.float32)
        return ((both - mean) * inv).astype(jnp.bfloat16)

    stat = statistics(view_one, view_two)
    far_one, far_two = swapped(view_one, 1), swapped(view_two, 1)
    q_one = normed(view_one, far_one, stat[0], stat[1])
    q_two = normed(view_two, far_two, stat[2], stat[3])
    ends = [[view_one, view_one], [view_two, view_two]]
    arrived = []
    loss = jnp.zeros((8, 128), jnp.float32)
    loss, *acc = attend(q_one, q_two, stat, [view_one], [view_two], loss, None, False)
    for hop in range(hops):
        if hop > 1:
            loss, *acc = attend(q_one, q_two, stat, *arrived[hop - 2], loss, acc, False)
            tied = (q_one, q_two) if hop == 2 else (norm_sums,)
            *flat, loss = lax.optimization_barrier((*ends[0], *ends[1], *tied, loss))
            ends = [flat[:2], flat[2:4]]
            arrived[-1] = [list(pair) for pair in ends]
            if hop == 2:
                q_one, q_two = flat[4:]
                norm_sums = norm_totals(q_one, q_two)
            else:
                norm_sums = flat[4]
        if hop < hops - 1:
            ends = [
                [lax.ppermute(up, "batch", ahead), lax.ppermute(down, "batch", behind)]
                for up, down in ends
            ]
            arrived.append([list(pair) for pair in ends])
        else:
            last_one = lax.ppermute(ends[0][0], "batch", ahead)
            last_two = lax.ppermute(ends[1][1], "batch", behind)
    loss, *acc = attend(
        q_one, q_two, stat, *arrived[hops - 2], loss, acc, False, dtype=jnp.bfloat16
    )
    last_one, last_two, loss = lax.optimization_barrier((last_one, last_two, loss))
    loss, own_one, send_one, own_two, send_two, total = attend(
        q_one, q_two, stat, [last_one], [last_two], loss, acc, True
    )
    get_one, get_two = swapped(send_one, 1), swapped(send_two, 1)
    terms = reduced(total, add_totals)
    grad_one, grad_two, loss = finish_grads(
        samples, (own_one, get_one, own_two, get_two, q_one, q_two, norm_sums, stat, *terms), rows
    )
    return (grad_one, grad_two, loss)


def solution(mesh):
    placed = (P(("groups", "batch"), "feat"), P(("groups", "batch"), "feat"))
    batches = mesh.shape["batch"]
    ringed = mesh.shape["feat"] == 1 and batches >= 8 and batches & (batches - 1) == 0
    return jax.shard_map(
        ring_shards if ringed else shards,
        mesh=mesh,
        in_specs=placed,
        out_specs=(P(("groups", "batch"), "feat"), P(("groups", "batch"), "feat"), P("groups")),
        check_vma=False,
    )
```

```python
import functools

import jax
import jax.numpy as jnp
from jax import lax
from jax.experimental import pallas as pl
from jax.experimental.pallas import tpu as pltpu
from jax.sharding import PartitionSpec as P

off_weight = 0.0051
tiles = 4
vmem = 56 * 1024 * 1024
strip = 16


def local_term(columns, full_two):
    return lax.dot_general(
        columns, full_two, (((0,), (0,)), ((), ())), preferred_element_type=jnp.float32
    )


def tile_grad(summed, row_base, samples):
    corr = summed / samples
    row_ids = row_base + lax.broadcasted_iota(jnp.int32, corr.shape, 0)
    col_ids = lax.broadcasted_iota(jnp.int32, corr.shape, 1)
    diag = row_ids == col_ids
    grad = jnp.where(diag, -2.0 * (1.0 - corr), 2.0 * off_weight * corr).astype(jnp.bfloat16)
    part_loss = jnp.sum(jnp.where(diag, (1.0 - corr) ** 2, off_weight * corr * corr))
    return (grad, part_loss)


def fold_step(columns, full_two, piece):
    contrib = lax.dot_general(
        full_two, piece, (((1,), (1,)), ((), ())), preferred_element_type=jnp.float32
    )
    back_mix = jnp.dot(columns, piece, preferred_element_type=jnp.float32)
    return (contrib, back_mix)


def finish(back, normed, inv, sum_back, sum_prod, samples):
    normal_f = normed.astype(jnp.float32)
    return (inv * (back - sum_back / samples - normal_f * sum_prod / samples)).astype(jnp.bfloat16)


def shards(view_one, view_two):
    rows, half_feat = view_one.shape
    batches = lax.axis_size("batch")
    samples = rows * batches
    values_one = view_one.astype(jnp.float32)
    values_two = view_two.astype(jnp.float32)
    sums = lax.psum(
        (
            jnp.sum(values_one, axis=0),
            jnp.sum(values_one * values_one, axis=0),
            jnp.sum(values_two, axis=0),
            jnp.sum(values_two * values_two, axis=0),
        ),
        "batch",
    )
    mean_one = sums[0] / samples
    mean_two = sums[2] / samples
    inv_one = 1.0 / jnp.sqrt(sums[1] / samples - mean_one * mean_one + 1e-05)
    inv_two = 1.0 / jnp.sqrt(sums[3] / samples - mean_two * mean_two + 1e-05)
    norm_one = ((values_one - mean_one) * inv_one).astype(jnp.bfloat16)
    norm_two = ((values_two - mean_two) * inv_two).astype(jnp.bfloat16)
    full_two = lax.all_gather(norm_two, "feat", axis=1, tiled=True)
    width = full_two.shape[1]
    tile = half_feat // batches
    row_base = lax.axis_index("feat") * half_feat + lax.axis_index("batch") * tile
    summed = lax.psum_scatter(
        local_term(norm_one, full_two), "batch", scatter_dimension=0, tiled=True
    )
    grad, part_loss = tile_grad(summed, row_base, samples)
    back_one, back_mix = fold_step(
        norm_one, full_two, lax.all_gather(grad, "batch", axis=0, tiled=True)
    )
    back_two = lax.psum_scatter(back_mix, "feat", scatter_dimension=1, tiled=True)
    loss = lax.psum(part_loss, ("batch", "feat")) / width
    norm_one_f = norm_one.astype(jnp.float32)
    norm_two_f = norm_two.astype(jnp.float32)
    stats = (
        lax.psum(jnp.sum(back_one, axis=0).astype(jnp.bfloat16), "batch").astype(jnp.float32),
        lax.psum(jnp.sum(back_one * norm_one_f, axis=0).astype(jnp.bfloat16), "batch").astype(
            jnp.float32
        ),
        lax.psum(jnp.sum(back_two, axis=0).astype(jnp.bfloat16), "batch").astype(jnp.float32),
        lax.psum(jnp.sum(back_two * norm_two_f, axis=0).astype(jnp.bfloat16), "batch").astype(
            jnp.float32
        ),
    )
    grad_one = finish(back_one, norm_one, inv_one, stats[0], stats[1], samples)
    grad_two = finish(back_two, norm_two, inv_two, stats[2], stats[3], samples)
    return (grad_one, grad_two, jnp.reshape(loss, (1,)))


def eight_rows(sums, loss):
    lanes = sums[0].shape[1]
    row = lax.broadcasted_iota(jnp.int32, (8, lanes), 0)
    loss = jnp.zeros((1, lanes), jnp.float32) + loss
    values = list(sums)
    for _ in range(3):
        part = loss.astype(jnp.bfloat16).astype(jnp.float32)
        values.append(part)
        loss = loss - part
    out = jnp.zeros((8, lanes), jnp.float32)
    for index, value in enumerate(values):
        out = jnp.where(row == index, value, out)
    return out.astype(jnp.bfloat16)


def added(refs):
    terms = [ref[...].astype(jnp.float32) for ref in refs]
    while len(terms) > 1:
        terms = [terms[k] + terms[k + 1] for k in range(0, len(terms), 2)]
    return terms[0]


def sums_kernel(one_ref, two_ref, out_ref):
    for index, ref in enumerate((one_ref, two_ref)):
        values = ref[...].astype(jnp.float32)
        out_ref[2 * index : 2 * index + 1, :] = jnp.sum(values, axis=0, keepdims=True)
        out_ref[2 * index + 1 : 2 * index + 2, :] = jnp.sum(values * values, axis=0, keepdims=True)


def first_sums(one, two):
    width = one.shape[1]
    return pl.pallas_call(
        sums_kernel,
        out_shape=jax.ShapeDtypeStruct((4, width), jnp.float32),
        cost_estimate=pl.CostEstimate(flops=width, bytes_accessed=width, transcendentals=0),
        name="first_sums",
    )(one, two)


def add_kernel(*refs):
    total = added(refs[:-1])
    loss = (total[4:5] + total[5:6]) + total[6:7]
    refs[-1][...] = eight_rows([total[k : k + 1] for k in range(4)], loss)


def attend_kernel(count, begins, ends, *refs):
    q_one, q_two, stat_ref = refs[:3]
    blocks_one = refs[3 : 3 + count]
    blocks_two = refs[3 + count : 3 + 2 * count]
    rest = list(refs[3 + 2 * count :])
    loss_in = rest.pop(0)
    acc_in = None if begins else (rest.pop(0), rest.pop(0))
    late = rest[-8:-6] if ends else ()
    held_one, held_two, gram_one, gram_two, round_one, round_two = rest[-6:]
    fresh = rest[-9] if ends else None
    loss_out, *outs = rest[: -9 if ends else -6]
    step = pl.program_id(0)
    tile = lax.rem(step, tiles)

    @pl.when(step == 0)
    def _():
        gram_one[...] = jnp.zeros_like(gram_one)
        gram_two[...] = jnp.zeros_like(gram_two)

    @pl.when(step < tiles)
    def _():
        for kept, queries in zip(late, (q_one, q_two)):
            kept[tile] = queries[...]
        for blocks, held, mean in ((blocks_one, held_one, 0), (blocks_two, held_two, 2)):
            start = 0
            for block in blocks:
                size = block.shape[0]
                normal = (block[...].astype(jnp.float32) - stat_ref[mean : mean + 1, :]) * stat_ref[
                    mean + 1 : mean + 2, :
                ]
                held[tile, start : start + size, :] = normal.astype(jnp.bfloat16)
                start += size
        for gram, queries, held in ((gram_one, q_one, held_one), (gram_two, q_two, held_two)):
            gram[...] += lax.dot_general(
                queries[...], held[tile], (((1,), (1,)), ((), ())), preferred_element_type=jnp.float32
            )

    @pl.when(step == tiles)
    def _():
        both = gram_one[...] * gram_two[...]
        height, width = both.shape
        folded = jnp.sum(both.reshape(height // 8, 8, width), axis=0)
        loss_out[...] = loss_in[...] + jnp.sum(folded) * (1.0 / 1024)
        round_one[...] = gram_one[...].astype(jnp.bfloat16)
        round_two[...] = gram_two[...].astype(jnp.bfloat16)

    @pl.when(step >= tiles)
    def _():
        sums = []
        for index, (gram, held) in enumerate(((round_two, held_one), (round_one, held_two))):
            if not ends:
                total = jnp.dot(gram[...], held[tile], preferred_element_type=jnp.float32)
                if not begins:
                    total += acc_in[index][...].astype(jnp.float32)
                outs[index][...] = total.astype(outs[index].dtype)
                continue
            fresh[...] = jnp.dot(gram[...], held[tile], preferred_element_type=jnp.float32)
            height, lanes = fresh.shape
            share = height // 2
            plain = jnp.zeros((8, lanes), jnp.float32)
            prods = jnp.zeros((8, lanes), jnp.float32)
            for start in range(0, height, strip):
                rows = slice(start, start + strip)
                total = fresh[rows, :] + acc_in[index][rows, :].astype(jnp.float32)
                prod = total * late[index][tile, rows, :].astype(jnp.float32)
                plain += jnp.sum(total.reshape(strip // 8, 8, lanes), axis=0)
                prods += jnp.sum(prod.reshape(strip // 8, 8, lanes), axis=0)
                place = start % share
                out = outs[2 * index + start // share]
                out[place : place + strip, :] = total.astype(jnp.bfloat16)
            sums.append(jnp.sum(plain, axis=0, keepdims=True))
            sums.append(jnp.sum(prods, axis=0, keepdims=True))
        if ends:
            outs[4][...] = eight_rows(sums, jnp.sum(loss_out[...]))


def attend(
    q_one, q_two, stat, blocks_one, blocks_two, loss, acc, ends, dtype=jnp.float32
):
    rows, width = q_one.shape
    lanes = width // tiles
    keys = sum(block.shape[0] for block in blocks_one)
    count = len(blocks_one)
    begins = acc is None
    early = lambda step: (0, jnp.minimum(step, tiles - 1))
    late = lambda step: (0, jnp.maximum(step - tiles, 0))
    fixed = pl.BlockSpec((8, 128), lambda step: (0, 0))
    operands = [q_one, q_two, stat, *blocks_one, *blocks_two, loss]
    in_specs = [pl.BlockSpec((rows, lanes), early)] * 2 + [pl.BlockSpec((4, lanes), early)]
    in_specs += [pl.BlockSpec((block.shape[0], lanes), early) for block in blocks_one] * 2
    in_specs.append(fixed)
    out_specs = [fixed]
    out_shape = [jax.ShapeDtypeStruct((8, 128), jnp.float32)]
    aliases = {3 + 2 * count: 0}
    if not begins:
        operands += list(acc)
        in_specs += [pl.BlockSpec((rows, lanes), late)] * 2
    if ends:
        out_specs += [pl.BlockSpec((rows // 2, lanes), late)] * 4
        out_shape += [
            jax.ShapeDtypeStruct((rows // 2, width), jnp.bfloat16),
            jax.ShapeDtypeStruct((rows // 2, width), jnp.bfloat16),
        ] * 2
        out_specs.append(pl.BlockSpec((8, lanes), late))
        out_shape.append(jax.ShapeDtypeStruct((8, width), jnp.bfloat16))
    else:
        if not begins and dtype == jnp.float32:
            aliases.update({4 + 2 * count: 1, 5 + 2 * count: 2})
        out_specs += [pl.BlockSpec((rows, lanes), late)] * 2
        out_shape += [jax.ShapeDtypeStruct((rows, width), dtype)] * 2
    return pl.pallas_call(
        functools.partial(attend_kernel, count, begins, ends),
        grid=(2 * tiles,),
        in_specs=in_specs,
        out_specs=out_specs,
        out_shape=out_shape,
        scratch_shapes=[pltpu.VMEM((rows, lanes), jnp.float32)] * (1 if ends else 0)
        + [pltpu.VMEM((tiles, rows, lanes), jnp.bfloat16)] * (2 if ends else 0)
        + [pltpu.VMEM((tiles, keys, lanes), jnp.bfloat16)] * 2
        + [pltpu.VMEM((rows, keys), jnp.float32)] * 2
        + [pltpu.VMEM((rows, keys), jnp.bfloat16)] * 2,
        input_output_aliases=aliases,
        compiler_params=pltpu.CompilerParams(vmem_limit_bytes=vmem),
        cost_estimate=pl.CostEstimate(flops=width, bytes_accessed=width, transcendentals=0),
        name="attend",
    )(*operands)


def finish_kernel(
    samples, full, own_one, get_one, own_two, get_two, norm_one, norm_two, norm_ref, stat_ref, *rest
):
    outs = rest[-3:]
    scale = 2.0 * off_weight / samples
    mixed = norm_ref[2:3, :]
    total = added(rest[:-3])
    corr = mixed / samples
    diag = (-2.0 * (1.0 - corr)).astype(jnp.bfloat16).astype(jnp.float32) - 2.0 * off_weight * corr
    squares = jnp.max((total[4:5, :128] + total[5:6, :128]) + total[6:7, :128])
    part = jnp.sum((1.0 - corr) ** 2 - off_weight * corr * corr)

    @pl.when(pl.program_id(0) == 0)
    def _():
        outs[2][0] = squares * (off_weight / (samples * samples * full))

    outs[2][0] += part / full
    for index, (own, get, mine, other, inv_row) in enumerate(
        ((own_one, get_one, norm_one, norm_two, 1), (own_two, get_two, norm_two, norm_one, 3))
    ):
        inv = stat_ref[inv_row : inv_row + 1, :]
        sum_back = scale * total[2 * index : 2 * index + 1, :]
        sum_back += norm_ref[1 - index : 2 - index, :] * diag
        sum_prod = scale * total[2 * index + 1 : 2 * index + 2, :] + mixed * diag
        by_acc, by_other = inv * scale, inv * diag
        minus, by_mine = inv * sum_back / samples, inv * sum_prod / samples
        for start in range(0, own.shape[0], strip):
            rows = slice(start, start + strip)
            grad = by_acc * (own[rows, :].astype(jnp.float32) + get[rows, :].astype(jnp.float32))
            grad += by_other * other[rows, :].astype(jnp.float32) - minus
            grad -= by_mine * mine[rows, :].astype(jnp.float32)
            outs[index][rows, :] = grad.astype(jnp.bfloat16)


def add_totals(terms):
    return pl.pallas_call(
        add_kernel,
        out_shape=jax.ShapeDtypeStruct(terms[0].shape, jnp.bfloat16),
        cost_estimate=pl.CostEstimate(flops=1, bytes_accessed=1, transcendentals=0),
        name="add_totals",
    )(*terms)


def finish_grads(samples, operands, rows):
    width = operands[0].shape[1]
    lanes = width // tiles
    heights = (*((rows,) * 6), 4, 4) + (8,) * (len(operands) - 8)
    place = lambda step: (0, step)
    return pl.pallas_call(
        functools.partial(finish_kernel, samples, width),
        grid=(tiles,),
        in_specs=[pl.BlockSpec((height, lanes), place) for height in heights],
        out_specs=[pl.BlockSpec((rows, lanes), place)] * 2
        + [pl.BlockSpec(memory_space=pltpu.SMEM)],
        out_shape=[jax.ShapeDtypeStruct((rows, width), jnp.bfloat16)] * 2
        + [jax.ShapeDtypeStruct((1,), jnp.float32)],
        compiler_params=pltpu.CompilerParams(vmem_limit_bytes=vmem),
        cost_estimate=pl.CostEstimate(flops=width, bytes_accessed=width, transcendentals=0),
        name="finish",
    )(*operands)


def ring_shards(view_one, view_two):
    rows, width = view_one.shape
    batches = lax.axis_size("batch")
    samples = rows * batches
    chips = batches // 2
    hops = chips // 2
    line = chips // 2
    order = [2 * r for r in range(line)] + [2 * r + 1 for r in reversed(range(line))]
    ahead = [
        (2 * order[r] + c, 2 * order[(r + 1) % chips] + c) for r in range(chips) for c in range(2)
    ]
    behind = [(there, here) for here, there in ahead]

    def swapped(value, bit):
        return lax.ppermute(value, "batch", [(i, i ^ bit) for i in range(batches)])

    def reduced(total, add):
        size = 1
        while size < batches:
            steps = (1, 2, 3) if size * 4 <= batches else (1,)
            terms = [total, *(swapped(total, size * step) for step in steps)]
            size *= len(steps) + 1
            total = add(terms) if size < batches else None
        return terms

    def norm_totals(q_one, q_two):
        one, two = (q[:rows].astype(jnp.float32) for q in (q_one, q_two))
        sums = [jnp.sum(one, axis=0), jnp.sum(two, axis=0), jnp.sum(one * two, axis=0)]
        return summed([*sums, jnp.zeros_like(sums[0])])

    def summed(rows_of_sums):
        return jnp.sum(lax.all_gather(jnp.stack(rows_of_sums), "batch", axis=0), axis=0)

    def statistics(one, two):
        sums = first_sums(one, two)
        sums = jnp.sum(lax.all_gather(sums, "batch", axis=0), axis=0) / samples
        inv_one = 1.0 / jnp.sqrt(sums[1] - sums[0] * sums[0] + 1e-05)
        inv_two = 1.0 / jnp.sqrt(sums[3] - sums[2] * sums[2] + 1e-05)
        return jnp.stack([sums[0], inv_one, sums[2], inv_two])

    def normed(view, far, mean, inv):
        both = jnp.concatenate([view, far], axis=0).astype(jnp.float32)
        return ((both - mean) * inv).astype(jnp.bfloat16)

    stat = statistics(view_one, view_two)
    far_one, far_two = swapped(view_one, 1), swapped(view_two, 1)
    q_one = normed(view_one, far_one, stat[0], stat[1])
    q_two = normed(view_two, far_two, stat[2], stat[3])
    ends = [[view_one, view_one], [view_two, view_two]]
    arrived = []
    loss = jnp.zeros((8, 128), jnp.float32)
    loss, *acc = attend(q_one, q_two, stat, [view_one], [view_two], loss, None, False)
    for hop in range(hops):
        if hop > 1:
            loss, *acc = attend(q_one, q_two, stat, *arrived[hop - 2], loss, acc, False)
            tied = (q_one, q_two) if hop == 2 else (norm_sums,)
            *flat, loss = lax.optimization_barrier((*ends[0], *ends[1], *tied, loss))
            ends = [flat[:2], flat[2:4]]
            arrived[-1] = [list(pair) for pair in ends]
            if hop == 2:
                q_one, q_two = flat[4:]
                norm_sums = norm_totals(q_one, q_two)
            else:
                norm_sums = flat[4]
        if hop < hops - 1:
            ends = [
                [lax.ppermute(up, "batch", ahead), lax.ppermute(down, "batch", behind)]
                for up, down in ends
            ]
            arrived.append([list(pair) for pair in ends])
        else:
            last_one = lax.ppermute(ends[0][0], "batch", ahead)
            last_two = lax.ppermute(ends[1][1], "batch", behind)
    loss, *acc = attend(
        q_one, q_two, stat, *arrived[hops - 2], loss, acc, False, dtype=jnp.bfloat16
    )
    last_one, last_two, loss = lax.optimization_barrier((last_one, last_two, loss))
    loss, own_one, send_one, own_two, send_two, total = attend(
        q_one, q_two, stat, [last_one], [last_two], loss, acc, True
    )
    get_one, get_two = swapped(send_one, 1), swapped(send_two, 1)
    terms = reduced(total, add_totals)
    grad_one, grad_two, loss = finish_grads(
        samples, (own_one, get_one, own_two, get_two, q_one, q_two, norm_sums, stat, *terms), rows
    )
    return (grad_one, grad_two, loss)


def solution(mesh):
    placed = (P(("groups", "batch"), "feat"), P(("groups", "batch"), "feat"))
    batches = mesh.shape["batch"]
    ringed = mesh.shape["feat"] == 1 and batches >= 8 and batches & (batches - 1) == 0
    return jax.shard_map(
        ring_shards if ringed else shards,
        mesh=mesh,
        in_specs=placed,
        out_specs=(P(("groups", "batch"), "feat"), P(("groups", "batch"), "feat"), P("groups")),
        check_vma=False,
    )
```

```python
import functools

import jax
import jax.numpy as jnp
from jax import lax
from jax.experimental import pallas as pl
from jax.experimental.pallas import tpu as pltpu
from jax.sharding import PartitionSpec as P

off_weight = 0.0051
tiles = 4
vmem = 56 * 1024 * 1024
strip = 16


def local_term(columns, full_two):
    return lax.dot_general(
        columns, full_two, (((0,), (0,)), ((), ())), preferred_element_type=jnp.float32
    )


def tile_grad(summed, row_base, samples):
    corr = summed / samples
    row_ids = row_base + lax.broadcasted_iota(jnp.int32, corr.shape, 0)
    col_ids = lax.broadcasted_iota(jnp.int32, corr.shape, 1)
    diag = row_ids == col_ids
    grad = jnp.where(diag, -2.0 * (1.0 - corr), 2.0 * off_weight * corr).astype(jnp.bfloat16)
    part_loss = jnp.sum(jnp.where(diag, (1.0 - corr) ** 2, off_weight * corr * corr))
    return (grad, part_loss)


def fold_step(columns, full_two, piece):
    contrib = lax.dot_general(
        full_two, piece, (((1,), (1,)), ((), ())), preferred_element_type=jnp.float32
    )
    back_mix = jnp.dot(columns, piece, preferred_element_type=jnp.float32)
    return (contrib, back_mix)


def finish(back, normed, inv, sum_back, sum_prod, samples):
    normal_f = normed.astype(jnp.float32)
    return (inv * (back - sum_back / samples - normal_f * sum_prod / samples)).astype(jnp.bfloat16)


def shards(view_one, view_two):
    rows, half_feat = view_one.shape
    batches = lax.axis_size("batch")
    samples = rows * batches
    values_one = view_one.astype(jnp.float32)
    values_two = view_two.astype(jnp.float32)
    sums = lax.psum(
        (
            jnp.sum(values_one, axis=0),
            jnp.sum(values_one * values_one, axis=0),
            jnp.sum(values_two, axis=0),
            jnp.sum(values_two * values_two, axis=0),
        ),
        "batch",
    )
    mean_one = sums[0] / samples
    mean_two = sums[2] / samples
    inv_one = 1.0 / jnp.sqrt(sums[1] / samples - mean_one * mean_one + 1e-05)
    inv_two = 1.0 / jnp.sqrt(sums[3] / samples - mean_two * mean_two + 1e-05)
    norm_one = ((values_one - mean_one) * inv_one).astype(jnp.bfloat16)
    norm_two = ((values_two - mean_two) * inv_two).astype(jnp.bfloat16)
    full_two = lax.all_gather(norm_two, "feat", axis=1, tiled=True)
    width = full_two.shape[1]
    tile = half_feat // batches
    row_base = lax.axis_index("feat") * half_feat + lax.axis_index("batch") * tile
    summed = lax.psum_scatter(
        local_term(norm_one, full_two), "batch", scatter_dimension=0, tiled=True
    )
    grad, part_loss = tile_grad(summed, row_base, samples)
    back_one, back_mix = fold_step(
        norm_one, full_two, lax.all_gather(grad, "batch", axis=0, tiled=True)
    )
    back_two = lax.psum_scatter(back_mix, "feat", scatter_dimension=1, tiled=True)
    loss = lax.psum(part_loss, ("batch", "feat")) / width
    norm_one_f = norm_one.astype(jnp.float32)
    norm_two_f = norm_two.astype(jnp.float32)
    stats = (
        lax.psum(jnp.sum(back_one, axis=0).astype(jnp.bfloat16), "batch").astype(jnp.float32),
        lax.psum(jnp.sum(back_one * norm_one_f, axis=0).astype(jnp.bfloat16), "batch").astype(
            jnp.float32
        ),
        lax.psum(jnp.sum(back_two, axis=0).astype(jnp.bfloat16), "batch").astype(jnp.float32),
        lax.psum(jnp.sum(back_two * norm_two_f, axis=0).astype(jnp.bfloat16), "batch").astype(
            jnp.float32
        ),
    )
    grad_one = finish(back_one, norm_one, inv_one, stats[0], stats[1], samples)
    grad_two = finish(back_two, norm_two, inv_two, stats[2], stats[3], samples)
    return (grad_one, grad_two, jnp.reshape(loss, (1,)))


def eight_rows(sums, loss):
    lanes = sums[0].shape[1]
    row = lax.broadcasted_iota(jnp.int32, (8, lanes), 0)
    loss = jnp.zeros((1, lanes), jnp.float32) + loss
    values = list(sums)
    for _ in range(3):
        part = loss.astype(jnp.bfloat16).astype(jnp.float32)
        values.append(part)
        loss = loss - part
    out = jnp.zeros((8, lanes), jnp.float32)
    for index, value in enumerate(values):
        out = jnp.where(row == index, value, out)
    return out.astype(jnp.bfloat16)


def added(refs):
    terms = [ref[...].astype(jnp.float32) for ref in refs]
    while len(terms) > 1:
        terms = [terms[k] + terms[k + 1] for k in range(0, len(terms), 2)]
    return terms[0]


def sums_kernel(one_ref, two_ref, out_ref):
    height, width = one_ref.shape
    lanes = width // tiles
    for index, ref in enumerate((one_ref, two_ref)):
        for left in range(0, width, lanes):
            plain = jnp.zeros((8, lanes), jnp.float32)
            squares = jnp.zeros((8, lanes), jnp.float32)
            for start in range(0, height, strip):
                values = ref[start : start + strip, left : left + lanes].astype(jnp.float32)
                values = values.reshape(strip // 8, 8, lanes)
                plain += jnp.sum(values, axis=0)
                squares += jnp.sum(values * values, axis=0)
            for row, value in ((2 * index, plain), (2 * index + 1, squares)):
                out_ref[row : row + 1, left : left + lanes] = jnp.sum(value, axis=0, keepdims=True)


def first_sums(one, two):
    width = one.shape[1]
    return pl.pallas_call(
        sums_kernel,
        out_shape=jax.ShapeDtypeStruct((4, width), jnp.float32),
        cost_estimate=pl.CostEstimate(flops=width, bytes_accessed=width, transcendentals=0),
        name="first_sums",
    )(one, two)


def add_kernel(*refs):
    total = added(refs[:-1])
    loss = (total[4:5] + total[5:6]) + total[6:7]
    refs[-1][...] = eight_rows([total[k : k + 1] for k in range(4)], loss)


def attend_kernel(count, begins, ends, *refs):
    q_one, q_two, stat_ref = refs[:3]
    blocks_one = refs[3 : 3 + count]
    blocks_two = refs[3 + count : 3 + 2 * count]
    rest = list(refs[3 + 2 * count :])
    loss_in = rest.pop(0)
    acc_in = None if begins else (rest.pop(0), rest.pop(0))
    late = (rest.pop(0), rest.pop(0)) if ends else ()
    held_one, held_two, gram_one, gram_two, round_one, round_two = rest[-6:]
    fresh = rest[-7] if ends else None
    loss_out, *outs = rest[: -7 if ends else -6]
    step = pl.program_id(0)
    tile = lax.rem(step, tiles)

    @pl.when(step == 0)
    def _():
        gram_one[...] = jnp.zeros_like(gram_one)
        gram_two[...] = jnp.zeros_like(gram_two)

    @pl.when(step < tiles)
    def _():
        for blocks, held, mean in ((blocks_one, held_one, 0), (blocks_two, held_two, 2)):
            start = 0
            for block in blocks:
                for row in range(0, block.shape[0], strip):
                    normal = block[row : row + strip, :].astype(jnp.float32)
                    normal = (normal - stat_ref[mean : mean + 1, :]) * stat_ref[mean + 1 : mean + 2, :]
                    held[tile, start : start + strip, :] = normal.astype(jnp.bfloat16)
                    start += strip
        for gram, queries, held in ((gram_one, q_one, held_one), (gram_two, q_two, held_two)):
            gram[...] += lax.dot_general(
                queries[...], held[tile], (((1,), (1,)), ((), ())), preferred_element_type=jnp.float32
            )

    @pl.when(step == tiles)
    def _():
        both = gram_one[...] * gram_two[...]
        height, width = both.shape
        folded = jnp.sum(both.reshape(height // 8, 8, width), axis=0)
        loss_out[...] = loss_in[...] + jnp.sum(folded) * (1.0 / 1024)
        round_one[...] = gram_one[...].astype(jnp.bfloat16)
        round_two[...] = gram_two[...].astype(jnp.bfloat16)

    @pl.when(step >= tiles)
    def _():
        sums = []
        for index, (gram, held) in enumerate(((round_two, held_one), (round_one, held_two))):
            if not ends:
                total = jnp.dot(gram[...], held[tile], preferred_element_type=jnp.float32)
                if not begins:
                    total += acc_in[index][...].astype(jnp.float32)
                outs[index][...] = total.astype(outs[index].dtype)
                continue
            fresh[...] = jnp.dot(gram[...], held[tile], preferred_element_type=jnp.float32)
            height, lanes = fresh.shape
            share = height // 2
            plain = jnp.zeros((8, lanes), jnp.float32)
            prods = jnp.zeros((8, lanes), jnp.float32)
            for start in range(0, height, strip):
                rows = slice(start, start + strip)
                total = fresh[rows, :] + acc_in[index][rows, :].astype(jnp.float32)
                prod = total * late[index][rows, :].astype(jnp.float32)
                plain += jnp.sum(total.reshape(strip // 8, 8, lanes), axis=0)
                prods += jnp.sum(prod.reshape(strip // 8, 8, lanes), axis=0)
                place = start % share
                out = outs[2 * index + start // share]
                out[place : place + strip, :] = total.astype(jnp.bfloat16)
            sums.append(jnp.sum(plain, axis=0, keepdims=True))
            sums.append(jnp.sum(prods, axis=0, keepdims=True))
        if ends:
            outs[4][...] = eight_rows(sums, jnp.sum(loss_out[...]))


def attend(
    q_one, q_two, stat, blocks_one, blocks_two, loss, acc, ends, dtype=jnp.float32
):
    rows, width = q_one.shape
    lanes = width // tiles
    keys = sum(block.shape[0] for block in blocks_one)
    count = len(blocks_one)
    begins = acc is None
    early = lambda step: (0, jnp.minimum(step, tiles - 1))
    late = lambda step: (0, jnp.maximum(step - tiles, 0))
    fixed = pl.BlockSpec((8, 128), lambda step: (0, 0))
    operands = [q_one, q_two, stat, *blocks_one, *blocks_two, loss]
    in_specs = [pl.BlockSpec((rows, lanes), early)] * 2 + [pl.BlockSpec((4, lanes), early)]
    in_specs += [pl.BlockSpec((block.shape[0], lanes), early) for block in blocks_one] * 2
    in_specs.append(fixed)
    out_specs = [fixed]
    out_shape = [jax.ShapeDtypeStruct((8, 128), jnp.float32)]
    aliases = {3 + 2 * count: 0}
    if not begins:
        operands += list(acc)
        in_specs += [pl.BlockSpec((rows, lanes), late)] * 2
    if ends:
        operands += [q_one, q_two]
        in_specs += [pl.BlockSpec((rows, lanes), late)] * 2
        out_specs += [pl.BlockSpec((rows // 2, lanes), late)] * 4
        out_shape += [
            jax.ShapeDtypeStruct((rows // 2, width), jnp.bfloat16),
            jax.ShapeDtypeStruct((rows // 2, width), jnp.bfloat16),
        ] * 2
        out_specs.append(pl.BlockSpec((8, lanes), late))
        out_shape.append(jax.ShapeDtypeStruct((8, width), jnp.bfloat16))
    else:
        if not begins and dtype == jnp.float32:
            aliases.update({4 + 2 * count: 1, 5 + 2 * count: 2})
        out_specs += [pl.BlockSpec((rows, lanes), late)] * 2
        out_shape += [jax.ShapeDtypeStruct((rows, width), dtype)] * 2
    return pl.pallas_call(
        functools.partial(attend_kernel, count, begins, ends),
        grid=(2 * tiles,),
        in_specs=in_specs,
        out_specs=out_specs,
        out_shape=out_shape,
        scratch_shapes=[pltpu.VMEM((rows, lanes), jnp.float32)] * (1 if ends else 0)
        + [pltpu.VMEM((tiles, keys, lanes), jnp.bfloat16)] * 2
        + [pltpu.VMEM((rows, keys), jnp.float32)] * 2
        + [pltpu.VMEM((rows, keys), jnp.bfloat16)] * 2,
        input_output_aliases=aliases,
        compiler_params=pltpu.CompilerParams(vmem_limit_bytes=vmem),
        cost_estimate=pl.CostEstimate(flops=width, bytes_accessed=width, transcendentals=0),
        name="attend",
    )(*operands)


def finish_kernel(
    samples, full, own_one, get_one, own_two, get_two, norm_one, norm_two, norm_ref, stat_ref, *rest
):
    outs = rest[-3:]
    scale = 2.0 * off_weight / samples
    mixed = norm_ref[2:3, :]
    total = added(rest[:-3])
    corr = mixed / samples
    diag = (-2.0 * (1.0 - corr)).astype(jnp.bfloat16).astype(jnp.float32) - 2.0 * off_weight * corr
    squares = jnp.max((total[4:5, :128] + total[5:6, :128]) + total[6:7, :128])
    part = jnp.sum((1.0 - corr) ** 2 - off_weight * corr * corr)

    @pl.when(pl.program_id(0) == 0)
    def _():
        outs[2][0] = squares * (off_weight / (samples * samples * full))

    outs[2][0] += part / full
    for index, (own, get, mine, other, inv_row) in enumerate(
        ((own_one, get_one, norm_one, norm_two, 1), (own_two, get_two, norm_two, norm_one, 3))
    ):
        inv = stat_ref[inv_row : inv_row + 1, :]
        sum_back = scale * total[2 * index : 2 * index + 1, :]
        sum_back += norm_ref[1 - index : 2 - index, :] * diag
        sum_prod = scale * total[2 * index + 1 : 2 * index + 2, :] + mixed * diag
        by_acc, by_other = inv * scale, inv * diag
        minus, by_mine = inv * sum_back / samples, inv * sum_prod / samples
        for start in range(0, own.shape[0], strip):
            rows = slice(start, start + strip)
            grad = by_acc * (own[rows, :].astype(jnp.float32) + get[rows, :].astype(jnp.float32))
            grad += by_other * other[rows, :].astype(jnp.float32) - minus
            grad -= by_mine * mine[rows, :].astype(jnp.float32)
            outs[index][rows, :] = grad.astype(jnp.bfloat16)


def add_totals(terms):
    return pl.pallas_call(
        add_kernel,
        out_shape=jax.ShapeDtypeStruct(terms[0].shape, jnp.bfloat16),
        cost_estimate=pl.CostEstimate(flops=1, bytes_accessed=1, transcendentals=0),
        name="add_totals",
    )(*terms)


def finish_grads(samples, operands, rows):
    width = operands[0].shape[1]
    lanes = width // tiles
    heights = (*((rows,) * 6), 4, 4) + (8,) * (len(operands) - 8)
    place = lambda step: (0, step)
    return pl.pallas_call(
        functools.partial(finish_kernel, samples, width),
        grid=(tiles,),
        in_specs=[pl.BlockSpec((height, lanes), place) for height in heights],
        out_specs=[pl.BlockSpec((rows, lanes), place)] * 2
        + [pl.BlockSpec(memory_space=pltpu.SMEM)],
        out_shape=[jax.ShapeDtypeStruct((rows, width), jnp.bfloat16)] * 2
        + [jax.ShapeDtypeStruct((1,), jnp.float32)],
        compiler_params=pltpu.CompilerParams(vmem_limit_bytes=vmem),
        cost_estimate=pl.CostEstimate(flops=width, bytes_accessed=width, transcendentals=0),
        name="finish",
    )(*operands)


def ring_shards(view_one, view_two):
    rows, width = view_one.shape
    batches = lax.axis_size("batch")
    samples = rows * batches
    chips = batches // 2
    hops = chips // 2
    line = chips // 2
    order = [2 * r for r in range(line)] + [2 * r + 1 for r in reversed(range(line))]
    ahead = [
        (2 * order[r] + c, 2 * order[(r + 1) % chips] + c) for r in range(chips) for c in range(2)
    ]
    behind = [(there, here) for here, there in ahead]

    def swapped(value, bit):
        return lax.ppermute(value, "batch", [(i, i ^ bit) for i in range(batches)])

    def reduced(total, add):
        size = 1
        while size < batches:
            steps = (1, 2, 3) if size * 4 <= batches else (1,)
            terms = [total, *(swapped(total, size * step) for step in steps)]
            size *= len(steps) + 1
            total = add(terms) if size < batches else None
        return terms

    def norm_totals(q_one, q_two):
        one, two = (q[:rows].astype(jnp.float32) for q in (q_one, q_two))
        sums = [jnp.sum(one, axis=0), jnp.sum(two, axis=0), jnp.sum(one * two, axis=0)]
        return jnp.stack([*sums, jnp.zeros_like(sums[0])])

    def summed(sums):
        return jnp.sum(lax.all_gather(sums, "batch", axis=0), axis=0)

    def statistics(one, two):
        sums = first_sums(one, two)
        sums = summed(sums) / samples
        inv_one = 1.0 / jnp.sqrt(sums[1] - sums[0] * sums[0] + 1e-05)
        inv_two = 1.0 / jnp.sqrt(sums[3] - sums[2] * sums[2] + 1e-05)
        return jnp.stack([sums[0], inv_one, sums[2], inv_two])

    def normed(view, far, mean, inv):
        both = jnp.concatenate([view, far], axis=0).astype(jnp.float32)
        return ((both - mean) * inv).astype(jnp.bfloat16)

    stat = statistics(view_one, view_two)
    far_one, far_two = swapped(view_one, 1), swapped(view_two, 1)
    q_one = normed(view_one, far_one, stat[0], stat[1])
    q_two = normed(view_two, far_two, stat[2], stat[3])
    ends = [[view_one, view_one], [view_two, view_two]]
    arrived = []
    loss = jnp.zeros((8, 128), jnp.float32)
    loss, *acc = attend(q_one, q_two, stat, [view_one], [view_two], loss, None, False)
    for hop in range(hops):
        if hop > 1:
            loss, *acc = attend(q_one, q_two, stat, *arrived[hop - 2], loss, acc, False)
            tied = (q_one, q_two, norm_totals(q_one, q_two)) if hop == 2 else (norm_sums,)
            *flat, loss = lax.optimization_barrier((*ends[0], *ends[1], *tied, loss))
            ends = [flat[:2], flat[2:4]]
            arrived[-1] = [list(pair) for pair in ends]
            if hop == 2:
                q_one, q_two = flat[4:6]
                norm_sums = summed(flat[6])
            else:
                norm_sums = flat[4]
        if hop < hops - 1:
            ends = [
                [lax.ppermute(up, "batch", ahead), lax.ppermute(down, "batch", behind)]
                for up, down in ends
            ]
            arrived.append([list(pair) for pair in ends])
        else:
            last_one = lax.ppermute(ends[0][0], "batch", ahead)
            last_two = lax.ppermute(ends[1][1], "batch", behind)
    loss, *acc = attend(
        q_one, q_two, stat, *arrived[hops - 2], loss, acc, False, dtype=jnp.bfloat16
    )
    last_one, last_two, loss = lax.optimization_barrier((last_one, last_two, loss))
    loss, own_one, send_one, own_two, send_two, total = attend(
        q_one, q_two, stat, [last_one], [last_two], loss, acc, True
    )
    get_one, get_two = swapped(send_one, 1), swapped(send_two, 1)
    terms = reduced(total, add_totals)
    grad_one, grad_two, loss = finish_grads(
        samples, (own_one, get_one, own_two, get_two, q_one, q_two, norm_sums, stat, *terms), rows
    )
    return (grad_one, grad_two, loss)


def solution(mesh):
    placed = (P(("groups", "batch"), "feat"), P(("groups", "batch"), "feat"))
    batches = mesh.shape["batch"]
    ringed = mesh.shape["feat"] == 1 and batches >= 8 and batches & (batches - 1) == 0
    return jax.shard_map(
        ring_shards if ringed else shards,
        mesh=mesh,
        in_specs=placed,
        out_specs=(P(("groups", "batch"), "feat"), P(("groups", "batch"), "feat"), P("groups")),
        check_vma=False,
    )
```

```python
import functools

import jax
import jax.numpy as jnp
from jax import lax
from jax.experimental import pallas as pl
from jax.experimental.pallas import tpu as pltpu
from jax.sharding import PartitionSpec as P

off_weight = 0.0051
tiles = 4
vmem = 56 * 1024 * 1024
strip = 16


def local_term(columns, full_two):
    return lax.dot_general(
        columns, full_two, (((0,), (0,)), ((), ())), preferred_element_type=jnp.float32
    )


def tile_grad(summed, row_base, samples):
    corr = summed / samples
    row_ids = row_base + lax.broadcasted_iota(jnp.int32, corr.shape, 0)
    col_ids = lax.broadcasted_iota(jnp.int32, corr.shape, 1)
    diag = row_ids == col_ids
    grad = jnp.where(diag, -2.0 * (1.0 - corr), 2.0 * off_weight * corr).astype(jnp.bfloat16)
    part_loss = jnp.sum(jnp.where(diag, (1.0 - corr) ** 2, off_weight * corr * corr))
    return (grad, part_loss)


def fold_step(columns, full_two, piece):
    contrib = lax.dot_general(
        full_two, piece, (((1,), (1,)), ((), ())), preferred_element_type=jnp.float32
    )
    back_mix = jnp.dot(columns, piece, preferred_element_type=jnp.float32)
    return (contrib, back_mix)


def finish(back, normed, inv, sum_back, sum_prod, samples):
    normal_f = normed.astype(jnp.float32)
    return (inv * (back - sum_back / samples - normal_f * sum_prod / samples)).astype(jnp.bfloat16)


def shards(view_one, view_two):
    rows, half_feat = view_one.shape
    batches = lax.axis_size("batch")
    samples = rows * batches
    values_one = view_one.astype(jnp.float32)
    values_two = view_two.astype(jnp.float32)
    sums = lax.psum(
        (
            jnp.sum(values_one, axis=0),
            jnp.sum(values_one * values_one, axis=0),
            jnp.sum(values_two, axis=0),
            jnp.sum(values_two * values_two, axis=0),
        ),
        "batch",
    )
    mean_one = sums[0] / samples
    mean_two = sums[2] / samples
    inv_one = 1.0 / jnp.sqrt(sums[1] / samples - mean_one * mean_one + 1e-05)
    inv_two = 1.0 / jnp.sqrt(sums[3] / samples - mean_two * mean_two + 1e-05)
    norm_one = ((values_one - mean_one) * inv_one).astype(jnp.bfloat16)
    norm_two = ((values_two - mean_two) * inv_two).astype(jnp.bfloat16)
    full_two = lax.all_gather(norm_two, "feat", axis=1, tiled=True)
    width = full_two.shape[1]
    tile = half_feat // batches
    row_base = lax.axis_index("feat") * half_feat + lax.axis_index("batch") * tile
    summed = lax.psum_scatter(
        local_term(norm_one, full_two), "batch", scatter_dimension=0, tiled=True
    )
    grad, part_loss = tile_grad(summed, row_base, samples)
    back_one, back_mix = fold_step(
        norm_one, full_two, lax.all_gather(grad, "batch", axis=0, tiled=True)
    )
    back_two = lax.psum_scatter(back_mix, "feat", scatter_dimension=1, tiled=True)
    loss = lax.psum(part_loss, ("batch", "feat")) / width
    norm_one_f = norm_one.astype(jnp.float32)
    norm_two_f = norm_two.astype(jnp.float32)
    stats = (
        lax.psum(jnp.sum(back_one, axis=0).astype(jnp.bfloat16), "batch").astype(jnp.float32),
        lax.psum(jnp.sum(back_one * norm_one_f, axis=0).astype(jnp.bfloat16), "batch").astype(
            jnp.float32
        ),
        lax.psum(jnp.sum(back_two, axis=0).astype(jnp.bfloat16), "batch").astype(jnp.float32),
        lax.psum(jnp.sum(back_two * norm_two_f, axis=0).astype(jnp.bfloat16), "batch").astype(
            jnp.float32
        ),
    )
    grad_one = finish(back_one, norm_one, inv_one, stats[0], stats[1], samples)
    grad_two = finish(back_two, norm_two, inv_two, stats[2], stats[3], samples)
    return (grad_one, grad_two, jnp.reshape(loss, (1,)))


def eight_rows(sums, loss):
    lanes = sums[0].shape[1]
    row = lax.broadcasted_iota(jnp.int32, (8, lanes), 0)
    loss = jnp.zeros((1, lanes), jnp.float32) + loss
    values = list(sums)
    for _ in range(3):
        part = loss.astype(jnp.bfloat16).astype(jnp.float32)
        values.append(part)
        loss = loss - part
    out = jnp.zeros((8, lanes), jnp.float32)
    for index, value in enumerate(values):
        out = jnp.where(row == index, value, out)
    return out.astype(jnp.bfloat16)


def added(refs):
    terms = [ref[...].astype(jnp.float32) for ref in refs]
    while len(terms) > 1:
        terms = [terms[k] + terms[k + 1] for k in range(0, len(terms), 2)]
    return terms[0]


def sums_kernel(one_ref, two_ref, out_ref):
    for index, ref in enumerate((one_ref, two_ref)):
        values = ref[...].astype(jnp.float32)
        out_ref[2 * index : 2 * index + 1, :] = jnp.sum(values, axis=0, keepdims=True)
        out_ref[2 * index + 1 : 2 * index + 2, :] = jnp.sum(values * values, axis=0, keepdims=True)


def first_sums(one, two):
    width = one.shape[1]
    return pl.pallas_call(
        sums_kernel,
        out_shape=jax.ShapeDtypeStruct((4, width), jnp.float32),
        cost_estimate=pl.CostEstimate(flops=width, bytes_accessed=width, transcendentals=0),
        name="first_sums",
    )(one, two)


def add_kernel(*refs):
    total = added(refs[:-1])
    loss = (total[4:5] + total[5:6]) + total[6:7]
    refs[-1][...] = eight_rows([total[k : k + 1] for k in range(4)], loss)


def attend_kernel(count, begins, ends, *refs):
    q_one, q_two, stat_ref = refs[:3]
    blocks_one = refs[3 : 3 + count]
    blocks_two = refs[3 + count : 3 + 2 * count]
    rest = list(refs[3 + 2 * count :])
    loss_in = rest.pop(0)
    acc_in = None if begins else (rest.pop(0), rest.pop(0))
    late = rest[-8:-6] if ends else ()
    held_one, held_two, gram_one, gram_two, round_one, round_two = rest[-6:]
    fresh = rest[-9] if ends else None
    loss_out, *outs = rest[: -9 if ends else -6]
    step = pl.program_id(0)
    tile = lax.rem(step, tiles)

    @pl.when(step == 0)
    def _():
        gram_one[...] = jnp.zeros_like(gram_one)
        gram_two[...] = jnp.zeros_like(gram_two)

    @pl.when(step < tiles)
    def _():
        for kept, queries in zip(late, (q_one, q_two)):
            kept[tile] = queries[...]
        for blocks, held, mean in ((blocks_one, held_one, 0), (blocks_two, held_two, 2)):
            start = 0
            for block in blocks:
                size = block.shape[0]
                normal = (block[...].astype(jnp.float32) - stat_ref[mean : mean + 1, :]) * stat_ref[
                    mean + 1 : mean + 2, :
                ]
                held[tile, start : start + size, :] = normal.astype(jnp.bfloat16)
                start += size
        for gram, queries, held in ((gram_one, q_one, held_one), (gram_two, q_two, held_two)):
            gram[...] += lax.dot_general(
                queries[...], held[tile], (((1,), (1,)), ((), ())), preferred_element_type=jnp.float32
            )

    @pl.when(step == tiles)
    def _():
        both = gram_one[...] * gram_two[...]
        height, width = both.shape
        folded = jnp.sum(both.reshape(height // 8, 8, width), axis=0)
        loss_out[...] = loss_in[...] + jnp.sum(folded) * (1.0 / 1024)
        round_one[...] = gram_one[...].astype(jnp.bfloat16)
        round_two[...] = gram_two[...].astype(jnp.bfloat16)

    @pl.when(step >= tiles)
    def _():
        sums = []
        for index, (gram, held) in enumerate(((round_two, held_one), (round_one, held_two))):
            if not ends:
                total = jnp.dot(gram[...], held[tile], preferred_element_type=jnp.float32)
                if not begins:
                    total += acc_in[index][...].astype(jnp.float32)
                outs[index][...] = total.astype(outs[index].dtype)
                continue
            fresh[...] = jnp.dot(gram[...], held[tile], preferred_element_type=jnp.float32)
            height, lanes = fresh.shape
            share = height // 2
            plain = jnp.zeros((8, lanes), jnp.float32)
            prods = jnp.zeros((8, lanes), jnp.float32)
            for start in range(0, height, strip):
                rows = slice(start, start + strip)
                total = fresh[rows, :] + acc_in[index][rows, :].astype(jnp.float32)
                prod = total * late[index][tile, rows, :].astype(jnp.float32)
                plain += jnp.sum(total.reshape(strip // 8, 8, lanes), axis=0)
                prods += jnp.sum(prod.reshape(strip // 8, 8, lanes), axis=0)
                place = start % share
                out = outs[2 * index + start // share]
                out[place : place + strip, :] = total.astype(jnp.bfloat16)
            sums.append(jnp.sum(plain, axis=0, keepdims=True))
            sums.append(jnp.sum(prods, axis=0, keepdims=True))
        if ends:
            outs[4][...] = eight_rows(sums, jnp.sum(loss_out[...]))


def attend(
    q_one, q_two, stat, blocks_one, blocks_two, loss, acc, ends, dtype=jnp.float32
):
    rows, width = q_one.shape
    lanes = width // tiles
    keys = sum(block.shape[0] for block in blocks_one)
    count = len(blocks_one)
    begins = acc is None
    early = lambda step: (0, jnp.minimum(step, tiles - 1))
    late = lambda step: (0, jnp.maximum(step - tiles, 0))
    fixed = pl.BlockSpec((8, 128), lambda step: (0, 0))
    operands = [q_one, q_two, stat, *blocks_one, *blocks_two, loss]
    in_specs = [pl.BlockSpec((rows, lanes), early)] * 2 + [pl.BlockSpec((4, lanes), early)]
    in_specs += [pl.BlockSpec((block.shape[0], lanes), early) for block in blocks_one] * 2
    in_specs.append(fixed)
    out_specs = [fixed]
    out_shape = [jax.ShapeDtypeStruct((8, 128), jnp.float32)]
    aliases = {3 + 2 * count: 0}
    if not begins:
        operands += list(acc)
        in_specs += [pl.BlockSpec((rows, lanes), late)] * 2
    if ends:
        out_specs += [pl.BlockSpec((rows // 2, lanes), late)] * 4
        out_shape += [
            jax.ShapeDtypeStruct((rows // 2, width), jnp.bfloat16),
            jax.ShapeDtypeStruct((rows // 2, width), jnp.bfloat16),
        ] * 2
        out_specs.append(pl.BlockSpec((8, lanes), late))
        out_shape.append(jax.ShapeDtypeStruct((8, width), jnp.bfloat16))
    else:
        if not begins and dtype == jnp.float32:
            aliases.update({4 + 2 * count: 1, 5 + 2 * count: 2})
        out_specs += [pl.BlockSpec((rows, lanes), late)] * 2
        out_shape += [jax.ShapeDtypeStruct((rows, width), dtype)] * 2
    return pl.pallas_call(
        functools.partial(attend_kernel, count, begins, ends),
        grid=(2 * tiles,),
        in_specs=in_specs,
        out_specs=out_specs,
        out_shape=out_shape,
        scratch_shapes=[pltpu.VMEM((rows, lanes), jnp.float32)] * (1 if ends else 0)
        + [pltpu.VMEM((tiles, rows, lanes), jnp.bfloat16)] * (2 if ends else 0)
        + [pltpu.VMEM((tiles, keys, lanes), jnp.bfloat16)] * 2
        + [pltpu.VMEM((rows, keys), jnp.float32)] * 2
        + [pltpu.VMEM((rows, keys), jnp.bfloat16)] * 2,
        input_output_aliases=aliases,
        compiler_params=pltpu.CompilerParams(vmem_limit_bytes=vmem),
        cost_estimate=pl.CostEstimate(flops=width, bytes_accessed=width, transcendentals=0),
        name="attend",
    )(*operands)


def finish_kernel(
    samples, full, own_one, get_one, own_two, get_two, norm_one, norm_two, norm_ref, stat_ref, *rest
):
    outs = rest[-3:]
    scale = 2.0 * off_weight / samples
    mixed = norm_ref[2:3, :]
    total = added(rest[:-3])
    corr = mixed / samples
    diag = (-2.0 * (1.0 - corr)).astype(jnp.bfloat16).astype(jnp.float32) - 2.0 * off_weight * corr
    squares = jnp.max((total[4:5, :128] + total[5:6, :128]) + total[6:7, :128])
    part = jnp.sum((1.0 - corr) ** 2 - off_weight * corr * corr)

    @pl.when(pl.program_id(0) == 0)
    def _():
        outs[2][0] = squares * (off_weight / (samples * samples * full))

    outs[2][0] += part / full
    for index, (own, get, mine, other, inv_row) in enumerate(
        ((own_one, get_one, norm_one, norm_two, 1), (own_two, get_two, norm_two, norm_one, 3))
    ):
        inv = stat_ref[inv_row : inv_row + 1, :]
        sum_back = scale * total[2 * index : 2 * index + 1, :]
        sum_back += norm_ref[1 - index : 2 - index, :] * diag
        sum_prod = scale * total[2 * index + 1 : 2 * index + 2, :] + mixed * diag
        by_acc, by_other = inv * scale, inv * diag
        minus, by_mine = inv * sum_back / samples, inv * sum_prod / samples
        for start in range(0, own.shape[0], strip):
            rows = slice(start, start + strip)
            grad = by_acc * (own[rows, :].astype(jnp.float32) + get[rows, :].astype(jnp.float32))
            grad += by_other * other[rows, :].astype(jnp.float32) - minus
            grad -= by_mine * mine[rows, :].astype(jnp.float32)
            outs[index][rows, :] = grad.astype(jnp.bfloat16)


def add_totals(terms):
    return pl.pallas_call(
        add_kernel,
        out_shape=jax.ShapeDtypeStruct(terms[0].shape, jnp.bfloat16),
        cost_estimate=pl.CostEstimate(flops=1, bytes_accessed=1, transcendentals=0),
        name="add_totals",
    )(*terms)


def finish_grads(samples, operands, rows):
    width = operands[0].shape[1]
    lanes = width // tiles
    heights = (*((rows,) * 6), 4, 4) + (8,) * (len(operands) - 8)
    place = lambda step: (0, step)
    return pl.pallas_call(
        functools.partial(finish_kernel, samples, width),
        grid=(tiles,),
        in_specs=[pl.BlockSpec((height, lanes), place) for height in heights],
        out_specs=[pl.BlockSpec((rows, lanes), place)] * 2
        + [pl.BlockSpec(memory_space=pltpu.SMEM)],
        out_shape=[jax.ShapeDtypeStruct((rows, width), jnp.bfloat16)] * 2
        + [jax.ShapeDtypeStruct((1,), jnp.float32)],
        compiler_params=pltpu.CompilerParams(vmem_limit_bytes=vmem),
        cost_estimate=pl.CostEstimate(flops=width, bytes_accessed=width, transcendentals=0),
        name="finish",
    )(*operands)


def ring_shards(view_one, view_two):
    rows, width = view_one.shape
    batches = lax.axis_size("batch")
    samples = rows * batches
    chips = batches // 2
    hops = chips // 2
    line = chips // 2
    order = [2 * r for r in range(line)] + [2 * r + 1 for r in reversed(range(line))]
    ahead = [
        (2 * order[r] + c, 2 * order[(r + 1) % chips] + c) for r in range(chips) for c in range(2)
    ]
    behind = [(there, here) for here, there in ahead]

    def swapped(value, bit):
        return lax.ppermute(value, "batch", [(i, i ^ bit) for i in range(batches)])

    def reduced(total, add):
        size = 1
        while size < batches:
            steps = (1, 2, 3) if size * 4 <= batches else (1,)
            terms = [total, *(swapped(total, size * step) for step in steps)]
            size *= len(steps) + 1
            total = add(terms) if size < batches else None
        return terms

    def norm_totals(q_one, q_two):
        one, two = (q[:rows].astype(jnp.float32) for q in (q_one, q_two))
        sums = [jnp.sum(one, axis=0), jnp.sum(two, axis=0), jnp.sum(one * two, axis=0)]
        return jnp.stack([*sums, jnp.zeros_like(sums[0])])

    def summed(sums):
        return jnp.sum(lax.all_gather(sums, "batch", axis=0), axis=0)

    def statistics(gathered):
        sums = jnp.sum(gathered, axis=0) / samples
        inv_one = 1.0 / jnp.sqrt(sums[1] - sums[0] * sums[0] + 1e-05)
        inv_two = 1.0 / jnp.sqrt(sums[3] - sums[2] * sums[2] + 1e-05)
        return jnp.stack([sums[0], inv_one, sums[2], inv_two])

    def normed(view, far, mean, inv):
        both = jnp.concatenate([view, far], axis=0).astype(jnp.float32)
        return ((both - mean) * inv).astype(jnp.bfloat16)

    gathered = lax.all_gather(first_sums(view_one, view_two), "batch", axis=0)
    far_one, far_two = swapped(view_one, 1), swapped(view_two, 1)
    ends = [[view_one, view_one], [view_two, view_two]]
    arrived = []
    loss = jnp.zeros((8, 128), jnp.float32)
    for hop in range(hops):
        if hop == 1:
            *arrived[0][0], gathered = lax.optimization_barrier((*ends[0], gathered))
            stat = statistics(gathered)
            q_one = normed(view_one, far_one, stat[0], stat[1])
            q_two = normed(view_two, far_two, stat[2], stat[3])
            loss, *acc = attend(q_one, q_two, stat, [view_one], [view_two], loss, None, False)
        if hop > 1:
            loss, *acc = attend(q_one, q_two, stat, *arrived[hop - 2], loss, acc, False)
            tied = (q_one, q_two, norm_totals(q_one, q_two)) if hop == 2 else (norm_sums,)
            *ends[1], tied, loss = lax.optimization_barrier((*ends[1], tied, loss))
            arrived[-1] = [list(pair) for pair in ends]
            if hop == 2:
                q_one, q_two, sums = tied
                norm_sums = summed(sums)
            else:
                (norm_sums,) = tied
        if hop < hops - 1:
            ends = [
                [lax.ppermute(up, "batch", ahead), lax.ppermute(down, "batch", behind)]
                for up, down in ends
            ]
            arrived.append([list(pair) for pair in ends])
        else:
            last_one = lax.ppermute(ends[0][0], "batch", ahead)
            last_two = lax.ppermute(ends[1][1], "batch", behind)
    loss, *acc = attend(
        q_one, q_two, stat, *arrived[hops - 2], loss, acc, False, dtype=jnp.bfloat16
    )
    last_one, last_two, loss = lax.optimization_barrier((last_one, last_two, loss))
    loss, own_one, send_one, own_two, send_two, total = attend(
        q_one, q_two, stat, [last_one], [last_two], loss, acc, True
    )
    get_one, get_two = swapped(send_one, 1), swapped(send_two, 1)
    terms = reduced(total, add_totals)
    grad_one, grad_two, loss = finish_grads(
        samples, (own_one, get_one, own_two, get_two, q_one, q_two, norm_sums, stat, *terms), rows
    )
    return (grad_one, grad_two, loss)


def solution(mesh):
    placed = (P(("groups", "batch"), "feat"), P(("groups", "batch"), "feat"))
    batches = mesh.shape["batch"]
    ringed = mesh.shape["feat"] == 1 and batches >= 8 and batches & (batches - 1) == 0
    return jax.shard_map(
        ring_shards if ringed else shards,
        mesh=mesh,
        in_specs=placed,
        out_specs=(P(("groups", "batch"), "feat"), P(("groups", "batch"), "feat"), P("groups")),
        check_vma=False,
    )
```

```python
import functools

import jax
import jax.numpy as jnp
from jax import lax
from jax.experimental import pallas as pl
from jax.experimental.pallas import tpu as pltpu
from jax.sharding import PartitionSpec as P

off_weight = 0.0051
tiles = 4
vmem = 56 * 1024 * 1024
strip = 16


def local_term(columns, full_two):
    return lax.dot_general(
        columns, full_two, (((0,), (0,)), ((), ())), preferred_element_type=jnp.float32
    )


def tile_grad(summed, row_base, samples):
    corr = summed / samples
    row_ids = row_base + lax.broadcasted_iota(jnp.int32, corr.shape, 0)
    col_ids = lax.broadcasted_iota(jnp.int32, corr.shape, 1)
    diag = row_ids == col_ids
    grad = jnp.where(diag, -2.0 * (1.0 - corr), 2.0 * off_weight * corr).astype(jnp.bfloat16)
    part_loss = jnp.sum(jnp.where(diag, (1.0 - corr) ** 2, off_weight * corr * corr))
    return (grad, part_loss)


def fold_step(columns, full_two, piece):
    contrib = lax.dot_general(
        full_two, piece, (((1,), (1,)), ((), ())), preferred_element_type=jnp.float32
    )
    back_mix = jnp.dot(columns, piece, preferred_element_type=jnp.float32)
    return (contrib, back_mix)


def finish(back, normed, inv, sum_back, sum_prod, samples):
    normal_f = normed.astype(jnp.float32)
    return (inv * (back - sum_back / samples - normal_f * sum_prod / samples)).astype(jnp.bfloat16)


def shards(view_one, view_two):
    rows, half_feat = view_one.shape
    batches = lax.axis_size("batch")
    samples = rows * batches
    values_one = view_one.astype(jnp.float32)
    values_two = view_two.astype(jnp.float32)
    sums = lax.psum(
        (
            jnp.sum(values_one, axis=0),
            jnp.sum(values_one * values_one, axis=0),
            jnp.sum(values_two, axis=0),
            jnp.sum(values_two * values_two, axis=0),
        ),
        "batch",
    )
    mean_one = sums[0] / samples
    mean_two = sums[2] / samples
    inv_one = 1.0 / jnp.sqrt(sums[1] / samples - mean_one * mean_one + 1e-05)
    inv_two = 1.0 / jnp.sqrt(sums[3] / samples - mean_two * mean_two + 1e-05)
    norm_one = ((values_one - mean_one) * inv_one).astype(jnp.bfloat16)
    norm_two = ((values_two - mean_two) * inv_two).astype(jnp.bfloat16)
    full_two = lax.all_gather(norm_two, "feat", axis=1, tiled=True)
    width = full_two.shape[1]
    tile = half_feat // batches
    row_base = lax.axis_index("feat") * half_feat + lax.axis_index("batch") * tile
    summed = lax.psum_scatter(
        local_term(norm_one, full_two), "batch", scatter_dimension=0, tiled=True
    )
    grad, part_loss = tile_grad(summed, row_base, samples)
    back_one, back_mix = fold_step(
        norm_one, full_two, lax.all_gather(grad, "batch", axis=0, tiled=True)
    )
    back_two = lax.psum_scatter(back_mix, "feat", scatter_dimension=1, tiled=True)
    loss = lax.psum(part_loss, ("batch", "feat")) / width
    norm_one_f = norm_one.astype(jnp.float32)
    norm_two_f = norm_two.astype(jnp.float32)
    stats = (
        lax.psum(jnp.sum(back_one, axis=0).astype(jnp.bfloat16), "batch").astype(jnp.float32),
        lax.psum(jnp.sum(back_one * norm_one_f, axis=0).astype(jnp.bfloat16), "batch").astype(
            jnp.float32
        ),
        lax.psum(jnp.sum(back_two, axis=0).astype(jnp.bfloat16), "batch").astype(jnp.float32),
        lax.psum(jnp.sum(back_two * norm_two_f, axis=0).astype(jnp.bfloat16), "batch").astype(
            jnp.float32
        ),
    )
    grad_one = finish(back_one, norm_one, inv_one, stats[0], stats[1], samples)
    grad_two = finish(back_two, norm_two, inv_two, stats[2], stats[3], samples)
    return (grad_one, grad_two, jnp.reshape(loss, (1,)))


def eight_rows(sums, loss):
    lanes = sums[0].shape[1]
    row = lax.broadcasted_iota(jnp.int32, (8, lanes), 0)
    loss = jnp.zeros((1, lanes), jnp.float32) + loss
    values = list(sums)
    for _ in range(3):
        part = loss.astype(jnp.bfloat16).astype(jnp.float32)
        values.append(part)
        loss = loss - part
    out = jnp.zeros((8, lanes), jnp.float32)
    for index, value in enumerate(values):
        out = jnp.where(row == index, value, out)
    return out.astype(jnp.bfloat16)


def added(refs):
    terms = [ref[...].astype(jnp.float32) for ref in refs]
    while len(terms) > 1:
        terms = [terms[k] + terms[k + 1] for k in range(0, len(terms), 2)]
    return terms[0]


def sums_kernel(one_ref, two_ref, out_ref):
    for index, ref in enumerate((one_ref, two_ref)):
        values = ref[...].astype(jnp.float32)
        out_ref[2 * index : 2 * index + 1, :] = jnp.sum(values, axis=0, keepdims=True)
        out_ref[2 * index + 1 : 2 * index + 2, :] = jnp.sum(values * values, axis=0, keepdims=True)


def first_sums(one, two):
    width = one.shape[1]
    return pl.pallas_call(
        sums_kernel,
        out_shape=jax.ShapeDtypeStruct((4, width), jnp.float32),
        cost_estimate=pl.CostEstimate(flops=width, bytes_accessed=width, transcendentals=0),
        name="first_sums",
    )(one, two)


def add_kernel(*refs):
    total = added(refs[:-1])
    loss = (total[4:5] + total[5:6]) + total[6:7]
    refs[-1][...] = eight_rows([total[k : k + 1] for k in range(4)], loss)


def attend_kernel(count, begins, ends, *refs):
    q_one, q_two, stat_ref = refs[:3]
    blocks_one = refs[3 : 3 + count]
    blocks_two = refs[3 + count : 3 + 2 * count]
    rest = list(refs[3 + 2 * count :])
    loss_in = rest.pop(0)
    acc_in = None if begins else (rest.pop(0), rest.pop(0))
    late = rest[-8:-6] if ends else ()
    held_one, held_two, gram_one, gram_two, round_one, round_two = rest[-6:]
    fresh = rest[-9] if ends else None
    loss_out, *outs = rest[: -9 if ends else -6]
    step = pl.program_id(0)
    tile = lax.rem(step, tiles)

    @pl.when(step == 0)
    def _():
        gram_one[...] = jnp.zeros_like(gram_one)
        gram_two[...] = jnp.zeros_like(gram_two)

    @pl.when(step < tiles)
    def _():
        for kept, queries in zip(late, (q_one, q_two)):
            kept[tile] = queries[...]
        for blocks, held, mean in ((blocks_one, held_one, 0), (blocks_two, held_two, 2)):
            start = 0
            for block in blocks:
                size = block.shape[0]
                normal = (block[...].astype(jnp.float32) - stat_ref[mean : mean + 1, :]) * stat_ref[
                    mean + 1 : mean + 2, :
                ]
                held[tile, start : start + size, :] = normal.astype(jnp.bfloat16)
                start += size
        for gram, queries, held in ((gram_one, q_one, held_one), (gram_two, q_two, held_two)):
            gram[...] += lax.dot_general(
                queries[...], held[tile], (((1,), (1,)), ((), ())), preferred_element_type=jnp.float32
            )

    @pl.when(step == tiles)
    def _():
        both = gram_one[...] * gram_two[...]
        height, width = both.shape
        folded = jnp.sum(both.reshape(height // 8, 8, width), axis=0)
        loss_out[...] = loss_in[...] + jnp.sum(folded) * (1.0 / 1024)
        round_one[...] = gram_one[...].astype(jnp.bfloat16)
        round_two[...] = gram_two[...].astype(jnp.bfloat16)

    @pl.when(step >= tiles)
    def _():
        sums = []
        for index, (gram, held) in enumerate(((round_two, held_one), (round_one, held_two))):
            if not ends:
                total = jnp.dot(gram[...], held[tile], preferred_element_type=jnp.float32)
                if not begins:
                    total += acc_in[index][...].astype(jnp.float32)
                outs[index][...] = total.astype(outs[index].dtype)
                continue
            fresh[...] = jnp.dot(gram[...], held[tile], preferred_element_type=jnp.float32)
            height, lanes = fresh.shape
            share = height // 2
            plain = jnp.zeros((8, lanes), jnp.float32)
            prods = jnp.zeros((8, lanes), jnp.float32)
            for start in range(0, height, strip):
                rows = slice(start, start + strip)
                total = fresh[rows, :] + acc_in[index][rows, :].astype(jnp.float32)
                prod = total * late[index][tile, rows, :].astype(jnp.float32)
                plain += jnp.sum(total.reshape(strip // 8, 8, lanes), axis=0)
                prods += jnp.sum(prod.reshape(strip // 8, 8, lanes), axis=0)
                place = start % share
                out = outs[2 * index + start // share]
                out[place : place + strip, :] = total.astype(jnp.bfloat16)
            sums.append(jnp.sum(plain, axis=0, keepdims=True))
            sums.append(jnp.sum(prods, axis=0, keepdims=True))
        if ends:
            outs[4][...] = eight_rows(sums, jnp.sum(loss_out[...]))


def attend(
    q_one, q_two, stat, blocks_one, blocks_two, loss, acc, ends, dtype=jnp.float32
):
    rows, width = q_one.shape
    lanes = width // tiles
    keys = sum(block.shape[0] for block in blocks_one)
    count = len(blocks_one)
    begins = acc is None
    early = lambda step: (0, jnp.minimum(step, tiles - 1))
    late = lambda step: (0, jnp.maximum(step - tiles, 0))
    fixed = pl.BlockSpec((8, 128), lambda step: (0, 0))
    operands = [q_one, q_two, stat, *blocks_one, *blocks_two, loss]
    in_specs = [pl.BlockSpec((rows, lanes), early)] * 2 + [pl.BlockSpec((4, lanes), early)]
    in_specs += [pl.BlockSpec((block.shape[0], lanes), early) for block in blocks_one] * 2
    in_specs.append(fixed)
    out_specs = [fixed]
    out_shape = [jax.ShapeDtypeStruct((8, 128), jnp.float32)]
    aliases = {3 + 2 * count: 0}
    if not begins:
        operands += list(acc)
        in_specs += [pl.BlockSpec((rows, lanes), late)] * 2
    if ends:
        out_specs += [pl.BlockSpec((rows // 2, lanes), late)] * 4
        out_shape += [
            jax.ShapeDtypeStruct((rows // 2, width), jnp.bfloat16),
            jax.ShapeDtypeStruct((rows // 2, width), jnp.bfloat16),
        ] * 2
        out_specs.append(pl.BlockSpec((8, lanes), late))
        out_shape.append(jax.ShapeDtypeStruct((8, width), jnp.bfloat16))
    else:
        if not begins and dtype == jnp.float32:
            aliases.update({4 + 2 * count: 1, 5 + 2 * count: 2})
        out_specs += [pl.BlockSpec((rows, lanes), late)] * 2
        out_shape += [jax.ShapeDtypeStruct((rows, width), dtype)] * 2
    return pl.pallas_call(
        functools.partial(attend_kernel, count, begins, ends),
        grid=(2 * tiles,),
        in_specs=in_specs,
        out_specs=out_specs,
        out_shape=out_shape,
        scratch_shapes=[pltpu.VMEM((rows, lanes), jnp.float32)] * (1 if ends else 0)
        + [pltpu.VMEM((tiles, rows, lanes), jnp.bfloat16)] * (2 if ends else 0)
        + [pltpu.VMEM((tiles, keys, lanes), jnp.bfloat16)] * 2
        + [pltpu.VMEM((rows, keys), jnp.float32)] * 2
        + [pltpu.VMEM((rows, keys), jnp.bfloat16)] * 2,
        input_output_aliases=aliases,
        compiler_params=pltpu.CompilerParams(vmem_limit_bytes=vmem),
        cost_estimate=pl.CostEstimate(flops=width, bytes_accessed=width, transcendentals=0),
        name="attend",
    )(*operands)


def finish_kernel(
    samples, full, own_one, get_one, own_two, get_two, norm_one, norm_two, norm_ref, stat_ref, *rest
):
    outs = rest[-3:]
    scale = 2.0 * off_weight / samples
    mixed = norm_ref[2:3, :]
    total = added(rest[:-3])
    corr = mixed / samples
    diag = (-2.0 * (1.0 - corr)).astype(jnp.bfloat16).astype(jnp.float32) - 2.0 * off_weight * corr
    squares = jnp.max((total[4:5, :128] + total[5:6, :128]) + total[6:7, :128])
    part = jnp.sum((1.0 - corr) ** 2 - off_weight * corr * corr)

    @pl.when(pl.program_id(0) == 0)
    def _():
        outs[2][0] = squares * (off_weight / (samples * samples * full))

    outs[2][0] += part / full
    for index, (own, get, mine, other, inv_row) in enumerate(
        ((own_one, get_one, norm_one, norm_two, 1), (own_two, get_two, norm_two, norm_one, 3))
    ):
        inv = stat_ref[inv_row : inv_row + 1, :]
        sum_back = scale * total[2 * index : 2 * index + 1, :]
        sum_back += norm_ref[1 - index : 2 - index, :] * diag
        sum_prod = scale * total[2 * index + 1 : 2 * index + 2, :] + mixed * diag
        by_acc, by_other = inv * scale, inv * diag
        minus, by_mine = inv * sum_back / samples, inv * sum_prod / samples
        for start in range(0, own.shape[0], strip):
            rows = slice(start, start + strip)
            grad = by_acc * (own[rows, :].astype(jnp.float32) + get[rows, :].astype(jnp.float32))
            grad += by_other * other[rows, :].astype(jnp.float32) - minus
            grad -= by_mine * mine[rows, :].astype(jnp.float32)
            outs[index][rows, :] = grad.astype(jnp.bfloat16)


def add_totals(terms):
    return pl.pallas_call(
        add_kernel,
        out_shape=jax.ShapeDtypeStruct(terms[0].shape, jnp.bfloat16),
        cost_estimate=pl.CostEstimate(flops=1, bytes_accessed=1, transcendentals=0),
        name="add_totals",
    )(*terms)


def finish_grads(samples, operands, rows):
    width = operands[0].shape[1]
    lanes = width // tiles
    heights = (*((rows,) * 6), 4, 4) + (8,) * (len(operands) - 8)
    place = lambda step: (0, step)
    return pl.pallas_call(
        functools.partial(finish_kernel, samples, width),
        grid=(tiles,),
        in_specs=[pl.BlockSpec((height, lanes), place) for height in heights],
        out_specs=[pl.BlockSpec((rows, lanes), place)] * 2
        + [pl.BlockSpec(memory_space=pltpu.SMEM)],
        out_shape=[jax.ShapeDtypeStruct((rows, width), jnp.bfloat16)] * 2
        + [jax.ShapeDtypeStruct((1,), jnp.float32)],
        compiler_params=pltpu.CompilerParams(vmem_limit_bytes=vmem),
        cost_estimate=pl.CostEstimate(flops=width, bytes_accessed=width, transcendentals=0),
        name="finish",
    )(*operands)


def ring_shards(view_one, view_two):
    rows, width = view_one.shape
    batches = lax.axis_size("batch")
    samples = rows * batches
    chips = batches // 2
    hops = chips // 2
    line = chips // 2
    order = [2 * r for r in range(line)] + [2 * r + 1 for r in reversed(range(line))]
    ahead = [
        (2 * order[r] + c, 2 * order[(r + 1) % chips] + c) for r in range(chips) for c in range(2)
    ]
    behind = [(there, here) for here, there in ahead]

    def swapped(value, bit):
        return lax.ppermute(value, "batch", [(i, i ^ bit) for i in range(batches)])

    def reduced(total, add):
        size = 1
        while size < batches:
            steps = (1, 2, 3) if size * 4 <= batches else (1,)
            terms = [total, *(swapped(total, size * step) for step in steps)]
            size *= len(steps) + 1
            total = add(terms) if size < batches else None
        return terms

    def norm_totals(q_one, q_two):
        one, two = (q[:rows].astype(jnp.float32) for q in (q_one, q_two))
        sums = [jnp.sum(one, axis=0), jnp.sum(two, axis=0), jnp.sum(one * two, axis=0)]
        return jnp.stack([*sums, jnp.zeros_like(sums[0])])

    def statistics(sums):
        sums = [value / samples for value in sums]
        inv_one = 1.0 / jnp.sqrt(sums[1] - sums[0] * sums[0] + 1e-05)
        inv_two = 1.0 / jnp.sqrt(sums[3] - sums[2] * sums[2] + 1e-05)
        return jnp.stack([sums[0], inv_one, sums[2], inv_two])

    def normed(view, far, mean, inv):
        both = jnp.concatenate([view, far], axis=0).astype(jnp.float32)
        return ((both - mean) * inv).astype(jnp.bfloat16)

    sums = first_sums(view_one, view_two)
    sums = lax.psum(tuple(sums[row] for row in range(4)), "batch")
    far_one, far_two = swapped(view_one, 1), swapped(view_two, 1)
    ends = [[view_one, view_one], [view_two, view_two]]
    arrived = []
    loss = jnp.zeros((8, 128), jnp.float32)
    for hop in range(hops):
        if hop == 2:
            ends[0][0], *sums = lax.optimization_barrier((ends[0][0], *sums))
            stat = statistics(sums)
            q_one = normed(view_one, far_one, stat[0], stat[1])
            q_two = normed(view_two, far_two, stat[2], stat[3])
            *flat, q_one, q_two, norm_sums = lax.optimization_barrier(
                (*ends[0], *ends[1], q_one, q_two, norm_totals(q_one, q_two))
            )
            ends = [flat[:2], flat[2:]]
            arrived[-1] = [list(pair) for pair in ends]
            norm_sums = jnp.sum(lax.all_gather(norm_sums, "batch", axis=0), axis=0)
            loss, *acc = attend(q_one, q_two, stat, [view_one], [view_two], loss, None, False)
        if hop > 2:
            for blocks in arrived[:2] if hop == 3 else arrived[hop - 2 : hop - 1]:
                loss, *acc = attend(q_one, q_two, stat, *blocks, loss, acc, False)
            *flat, norm_sums, loss = lax.optimization_barrier((*ends[0], *ends[1], norm_sums, loss))
            ends = [flat[:2], flat[2:]]
            arrived[-1] = [list(pair) for pair in ends]
        if hop < hops - 1:
            ends = [
                [lax.ppermute(up, "batch", ahead), lax.ppermute(down, "batch", behind)]
                for up, down in ends
            ]
            arrived.append([list(pair) for pair in ends])
        else:
            last_one = lax.ppermute(ends[0][0], "batch", ahead)
            last_two = lax.ppermute(ends[1][1], "batch", behind)
    loss, *acc = attend(
        q_one, q_two, stat, *arrived[hops - 2], loss, acc, False, dtype=jnp.bfloat16
    )
    last_one, last_two, loss = lax.optimization_barrier((last_one, last_two, loss))
    loss, own_one, send_one, own_two, send_two, total = attend(
        q_one, q_two, stat, [last_one], [last_two], loss, acc, True
    )
    get_one, get_two = swapped(send_one, 1), swapped(send_two, 1)
    terms = reduced(total, add_totals)
    grad_one, grad_two, loss = finish_grads(
        samples, (own_one, get_one, own_two, get_two, q_one, q_two, norm_sums, stat, *terms), rows
    )
    return (grad_one, grad_two, loss)


def solution(mesh):
    placed = (P(("groups", "batch"), "feat"), P(("groups", "batch"), "feat"))
    batches = mesh.shape["batch"]
    ringed = mesh.shape["feat"] == 1 and batches >= 16 and batches & (batches - 1) == 0
    return jax.shard_map(
        ring_shards if ringed else shards,
        mesh=mesh,
        in_specs=placed,
        out_specs=(P(("groups", "batch"), "feat"), P(("groups", "batch"), "feat"), P("groups")),
        check_vma=False,
    )
```

```python
import functools

import jax
import jax.numpy as jnp
from jax import lax
from jax.experimental import pallas as pl
from jax.experimental.pallas import tpu as pltpu
from jax.sharding import PartitionSpec as P

off_weight = 0.0051
tiles = 4
vmem = 56 * 1024 * 1024
strip = 16


def local_term(columns, full_two):
    return lax.dot_general(
        columns, full_two, (((0,), (0,)), ((), ())), preferred_element_type=jnp.float32
    )


def tile_grad(summed, row_base, samples):
    corr = summed / samples
    row_ids = row_base + lax.broadcasted_iota(jnp.int32, corr.shape, 0)
    col_ids = lax.broadcasted_iota(jnp.int32, corr.shape, 1)
    diag = row_ids == col_ids
    grad = jnp.where(diag, -2.0 * (1.0 - corr), 2.0 * off_weight * corr).astype(jnp.bfloat16)
    part_loss = jnp.sum(jnp.where(diag, (1.0 - corr) ** 2, off_weight * corr * corr))
    return (grad, part_loss)


def fold_step(columns, full_two, piece):
    contrib = lax.dot_general(
        full_two, piece, (((1,), (1,)), ((), ())), preferred_element_type=jnp.float32
    )
    back_mix = jnp.dot(columns, piece, preferred_element_type=jnp.float32)
    return (contrib, back_mix)


def finish(back, normed, inv, sum_back, sum_prod, samples):
    normal_f = normed.astype(jnp.float32)
    return (inv * (back - sum_back / samples - normal_f * sum_prod / samples)).astype(jnp.bfloat16)


def shards(view_one, view_two):
    rows, half_feat = view_one.shape
    batches = lax.axis_size("batch")
    samples = rows * batches
    values_one = view_one.astype(jnp.float32)
    values_two = view_two.astype(jnp.float32)
    sums = lax.psum(
        (
            jnp.sum(values_one, axis=0),
            jnp.sum(values_one * values_one, axis=0),
            jnp.sum(values_two, axis=0),
            jnp.sum(values_two * values_two, axis=0),
        ),
        "batch",
    )
    mean_one = sums[0] / samples
    mean_two = sums[2] / samples
    inv_one = 1.0 / jnp.sqrt(sums[1] / samples - mean_one * mean_one + 1e-05)
    inv_two = 1.0 / jnp.sqrt(sums[3] / samples - mean_two * mean_two + 1e-05)
    norm_one = ((values_one - mean_one) * inv_one).astype(jnp.bfloat16)
    norm_two = ((values_two - mean_two) * inv_two).astype(jnp.bfloat16)
    full_two = lax.all_gather(norm_two, "feat", axis=1, tiled=True)
    width = full_two.shape[1]
    tile = half_feat // batches
    row_base = lax.axis_index("feat") * half_feat + lax.axis_index("batch") * tile
    summed = lax.psum_scatter(
        local_term(norm_one, full_two), "batch", scatter_dimension=0, tiled=True
    )
    grad, part_loss = tile_grad(summed, row_base, samples)
    back_one, back_mix = fold_step(
        norm_one, full_two, lax.all_gather(grad, "batch", axis=0, tiled=True)
    )
    back_two = lax.psum_scatter(back_mix, "feat", scatter_dimension=1, tiled=True)
    loss = lax.psum(part_loss, ("batch", "feat")) / width
    norm_one_f = norm_one.astype(jnp.float32)
    norm_two_f = norm_two.astype(jnp.float32)
    stats = (
        lax.psum(jnp.sum(back_one, axis=0).astype(jnp.bfloat16), "batch").astype(jnp.float32),
        lax.psum(jnp.sum(back_one * norm_one_f, axis=0).astype(jnp.bfloat16), "batch").astype(
            jnp.float32
        ),
        lax.psum(jnp.sum(back_two, axis=0).astype(jnp.bfloat16), "batch").astype(jnp.float32),
        lax.psum(jnp.sum(back_two * norm_two_f, axis=0).astype(jnp.bfloat16), "batch").astype(
            jnp.float32
        ),
    )
    grad_one = finish(back_one, norm_one, inv_one, stats[0], stats[1], samples)
    grad_two = finish(back_two, norm_two, inv_two, stats[2], stats[3], samples)
    return (grad_one, grad_two, jnp.reshape(loss, (1,)))


def added(refs):
    terms = [ref[...].astype(jnp.float32) for ref in refs]
    while len(terms) > 1:
        terms = [terms[k] + terms[k + 1] for k in range(0, len(terms), 2)]
    return terms[0]


def sums_kernel(one_ref, two_ref, out_ref):
    for index, ref in enumerate((one_ref, two_ref)):
        values = ref[...].astype(jnp.float32)
        out_ref[2 * index : 2 * index + 1, :] = jnp.sum(values, axis=0, keepdims=True)
        out_ref[2 * index + 1 : 2 * index + 2, :] = jnp.sum(values * values, axis=0, keepdims=True)


def first_sums(one, two):
    width = one.shape[1]
    return pl.pallas_call(
        sums_kernel,
        out_shape=jax.ShapeDtypeStruct((4, width), jnp.float32),
        cost_estimate=pl.CostEstimate(flops=width, bytes_accessed=width, transcendentals=0),
        name="first_sums",
    )(one, two)


def three_rows(value):
    rows = []
    for _ in range(3):
        part = value.astype(jnp.bfloat16).astype(jnp.float32)
        rows.append(part)
        value = value - part
    row = lax.broadcasted_iota(jnp.int32, (4, 128), 0)
    out = jnp.where(row == 0, rows[0], jnp.where(row == 1, rows[1], 0.0))
    return jnp.where(row == 2, rows[2], out).astype(jnp.bfloat16)


def loss_of(total):
    return (total[0:1] + total[1:2]) + total[2:3]


def add_kernel(*refs):
    total = added(refs[:-1])
    width = total.shape[1] - 128
    refs[-1][:, :width] = total[:, :width].astype(jnp.bfloat16)
    refs[-1][:, width:] = three_rows(loss_of(total[:, width:]))


def attend_kernel(count, begins, ends, *refs):
    q_one, q_two, stat_ref = refs[:3]
    blocks_one = refs[3 : 3 + count]
    blocks_two = refs[3 + count : 3 + 2 * count]
    rest = list(refs[3 + 2 * count :])
    loss_in = rest.pop(0)
    acc_in = None if begins else (rest.pop(0), rest.pop(0))
    late = rest[-8:-6] if ends else ()
    held_one, held_two, gram_one, gram_two, round_one, round_two = rest[-6:]
    fresh = rest[-9] if ends else None
    loss_out, *outs = rest[: -9 if ends else -6]
    step = pl.program_id(0)
    tile = lax.rem(step, tiles)

    @pl.when(step == 0)
    def _():
        gram_one[...] = jnp.zeros_like(gram_one)
        gram_two[...] = jnp.zeros_like(gram_two)

    @pl.when(step < tiles)
    def _():
        for kept, queries in zip(late, (q_one, q_two)):
            kept[tile] = queries[...]
        for blocks, held, mean in ((blocks_one, held_one, 0), (blocks_two, held_two, 2)):
            start = 0
            for block in blocks:
                size = block.shape[0]
                normal = (block[...].astype(jnp.float32) - stat_ref[mean : mean + 1, :]) * stat_ref[
                    mean + 1 : mean + 2, :
                ]
                held[tile, start : start + size, :] = normal.astype(jnp.bfloat16)
                start += size
        for gram, queries, held in ((gram_one, q_one, held_one), (gram_two, q_two, held_two)):
            gram[...] += lax.dot_general(
                queries[...], held[tile], (((1,), (1,)), ((), ())), preferred_element_type=jnp.float32
            )

    @pl.when(step == tiles)
    def _():
        both = gram_one[...] * gram_two[...]
        height, width = both.shape
        folded = jnp.sum(both.reshape(height // 8, 8, width), axis=0)
        loss_out[...] = loss_in[...] + jnp.sum(folded) * (1.0 / 1024)
        round_one[...] = gram_one[...].astype(jnp.bfloat16)
        round_two[...] = gram_two[...].astype(jnp.bfloat16)

    @pl.when(step >= tiles)
    def _():
        sums = []
        for index, (gram, held) in enumerate(((round_two, held_one), (round_one, held_two))):
            if not ends:
                total = jnp.dot(gram[...], held[tile], preferred_element_type=jnp.float32)
                if not begins:
                    total += acc_in[index][...].astype(jnp.float32)
                outs[index][...] = total.astype(outs[index].dtype)
                continue
            fresh[...] = jnp.dot(gram[...], held[tile], preferred_element_type=jnp.float32)
            height, lanes = fresh.shape
            share = height // 2
            plain = jnp.zeros((8, lanes), jnp.float32)
            prods = jnp.zeros((8, lanes), jnp.float32)
            for start in range(0, height, strip):
                rows = slice(start, start + strip)
                total = fresh[rows, :] + acc_in[index][rows, :].astype(jnp.float32)
                prod = total * late[index][tile, rows, :].astype(jnp.float32)
                plain += jnp.sum(total.reshape(strip // 8, 8, lanes), axis=0)
                prods += jnp.sum(prod.reshape(strip // 8, 8, lanes), axis=0)
                place = start % share
                out = outs[2 * index + start // share]
                out[place : place + strip, :] = total.astype(jnp.bfloat16)
            sums.append(jnp.sum(plain, axis=0, keepdims=True))
            sums.append(jnp.sum(prods, axis=0, keepdims=True))
        if ends:
            for index, value in enumerate(sums):
                outs[4][index : index + 1, :] = value.astype(jnp.bfloat16)
            outs[5][...] = three_rows(jnp.zeros((1, 128), jnp.float32) + jnp.sum(loss_out[...]))


def attend(
    q_one, q_two, stat, blocks_one, blocks_two, loss, acc, ends, dtype=jnp.float32
):
    rows, width = q_one.shape
    lanes = width // tiles
    keys = sum(block.shape[0] for block in blocks_one)
    count = len(blocks_one)
    begins = acc is None
    early = lambda step: (0, jnp.minimum(step, tiles - 1))
    late = lambda step: (0, jnp.maximum(step - tiles, 0))
    fixed = pl.BlockSpec((8, 128), lambda step: (0, 0))
    operands = [q_one, q_two, stat, *blocks_one, *blocks_two, loss]
    in_specs = [pl.BlockSpec((rows, lanes), early)] * 2 + [pl.BlockSpec((4, lanes), early)]
    in_specs += [pl.BlockSpec((block.shape[0], lanes), early) for block in blocks_one] * 2
    in_specs.append(fixed)
    out_specs = [fixed]
    out_shape = [jax.ShapeDtypeStruct((8, 128), jnp.float32)]
    aliases = {3 + 2 * count: 0}
    if not begins:
        operands += list(acc)
        in_specs += [pl.BlockSpec((rows, lanes), late)] * 2
    if ends:
        out_specs += [pl.BlockSpec((rows // 2, lanes), late)] * 4
        out_shape += [
            jax.ShapeDtypeStruct((rows // 2, width), jnp.bfloat16),
            jax.ShapeDtypeStruct((rows // 2, width), jnp.bfloat16),
        ] * 2
        out_specs += [pl.BlockSpec((4, lanes), late), pl.BlockSpec((4, 128), lambda step: (0, 0))]
        out_shape += [jax.ShapeDtypeStruct((4, size), jnp.bfloat16) for size in (width, 128)]
    else:
        if not begins and dtype == jnp.float32:
            aliases.update({4 + 2 * count: 1, 5 + 2 * count: 2})
        out_specs += [pl.BlockSpec((rows, lanes), late)] * 2
        out_shape += [jax.ShapeDtypeStruct((rows, width), dtype)] * 2
    return pl.pallas_call(
        functools.partial(attend_kernel, count, begins, ends),
        grid=(2 * tiles,),
        in_specs=in_specs,
        out_specs=out_specs,
        out_shape=out_shape,
        scratch_shapes=[pltpu.VMEM((rows, lanes), jnp.float32)] * (1 if ends else 0)
        + [pltpu.VMEM((tiles, rows, lanes), jnp.bfloat16)] * (2 if ends else 0)
        + [pltpu.VMEM((tiles, keys, lanes), jnp.bfloat16)] * 2
        + [pltpu.VMEM((rows, keys), jnp.float32)] * 2
        + [pltpu.VMEM((rows, keys), jnp.bfloat16)] * 2,
        input_output_aliases=aliases,
        compiler_params=pltpu.CompilerParams(vmem_limit_bytes=vmem),
        cost_estimate=pl.CostEstimate(flops=width, bytes_accessed=width, transcendentals=0),
        name="attend",
    )(*operands)


def finish_kernel(
    samples, full, own_one, get_one, own_two, get_two, norm_one, norm_two, norm_ref, stat_ref, *rest
):
    outs = rest[-3:]
    count = (len(rest) - 3) // 2
    scale = 2.0 * off_weight / samples
    mixed = norm_ref[2:3, :]
    total = added(rest[:count])
    corr = mixed / samples
    diag = (-2.0 * (1.0 - corr)).astype(jnp.bfloat16).astype(jnp.float32) - 2.0 * off_weight * corr
    squares = jnp.max(loss_of(added(rest[count:-3])))
    part = jnp.sum((1.0 - corr) ** 2 - off_weight * corr * corr)

    @pl.when(pl.program_id(0) == 0)
    def _():
        outs[2][0] = squares * (off_weight / (samples * samples * full))

    outs[2][0] += part / full
    for index, (own, get, mine, other, inv_row) in enumerate(
        ((own_one, get_one, norm_one, norm_two, 1), (own_two, get_two, norm_two, norm_one, 3))
    ):
        inv = stat_ref[inv_row : inv_row + 1, :]
        sum_back = scale * total[2 * index : 2 * index + 1, :]
        sum_back += norm_ref[1 - index : 2 - index, :] * diag
        sum_prod = scale * total[2 * index + 1 : 2 * index + 2, :] + mixed * diag
        by_acc, by_other = inv * scale, inv * diag
        minus, by_mine = inv * sum_back / samples, inv * sum_prod / samples
        for start in range(0, own.shape[0], strip):
            rows = slice(start, start + strip)
            grad = by_acc * (own[rows, :].astype(jnp.float32) + get[rows, :].astype(jnp.float32))
            grad += by_other * other[rows, :].astype(jnp.float32) - minus
            grad -= by_mine * mine[rows, :].astype(jnp.float32)
            outs[index][rows, :] = grad.astype(jnp.bfloat16)


def add_totals(terms):
    return pl.pallas_call(
        add_kernel,
        out_shape=jax.ShapeDtypeStruct(terms[0].shape, jnp.bfloat16),
        cost_estimate=pl.CostEstimate(flops=1, bytes_accessed=1, transcendentals=0),
        name="add_totals",
    )(*terms)


def finish_grads(samples, operands, rows):
    width = operands[0].shape[1]
    lanes = width // tiles
    count = (len(operands) - 8) // 2
    heights = (*((rows,) * 6), 4, 4) + (4,) * count
    place = lambda step: (0, step)
    return pl.pallas_call(
        functools.partial(finish_kernel, samples, width),
        grid=(tiles,),
        in_specs=[pl.BlockSpec((height, lanes), place) for height in heights]
        + [pl.BlockSpec((4, 128), lambda step: (0, width // 128))] * count,
        out_specs=[pl.BlockSpec((rows, lanes), place)] * 2
        + [pl.BlockSpec(memory_space=pltpu.SMEM)],
        out_shape=[jax.ShapeDtypeStruct((rows, width), jnp.bfloat16)] * 2
        + [jax.ShapeDtypeStruct((1,), jnp.float32)],
        compiler_params=pltpu.CompilerParams(vmem_limit_bytes=vmem),
        cost_estimate=pl.CostEstimate(flops=width, bytes_accessed=width, transcendentals=0),
        name="finish",
    )(*operands)


def ring_shards(view_one, view_two):
    rows, width = view_one.shape
    batches = lax.axis_size("batch")
    samples = rows * batches
    chips = batches // 2
    hops = chips // 2
    line = chips // 2
    order = [2 * r for r in range(line)] + [2 * r + 1 for r in reversed(range(line))]
    ahead = [
        (2 * order[r] + c, 2 * order[(r + 1) % chips] + c) for r in range(chips) for c in range(2)
    ]
    behind = [(there, here) for here, there in ahead]

    def swapped(value, bit):
        return lax.ppermute(value, "batch", [(i, i ^ bit) for i in range(batches)])

    def norm_totals(q_one, q_two):
        one, two = (q[:rows].astype(jnp.float32) for q in (q_one, q_two))
        sums = [jnp.sum(one, axis=0), jnp.sum(two, axis=0), jnp.sum(one * two, axis=0)]
        return jnp.stack([*sums, jnp.zeros_like(sums[0])])

    def statistics(sums):
        sums = [value / samples for value in sums]
        inv_one = 1.0 / jnp.sqrt(sums[1] - sums[0] * sums[0] + 1e-05)
        inv_two = 1.0 / jnp.sqrt(sums[3] - sums[2] * sums[2] + 1e-05)
        return jnp.stack([sums[0], inv_one, sums[2], inv_two])

    def normed(view, far, mean, inv):
        both = jnp.concatenate([view, far], axis=0).astype(jnp.float32)
        return ((both - mean) * inv).astype(jnp.bfloat16)

    sums = first_sums(view_one, view_two)
    sums = lax.psum(tuple(sums[row] for row in range(4)), "batch")
    far_one, far_two = swapped(view_one, 1), swapped(view_two, 1)
    ends = [[view_one, view_one], [view_two, view_two]]
    arrived = []
    loss = jnp.zeros((8, 128), jnp.float32)
    for hop in range(hops):
        if hop == 2:
            ends[0][0], *sums = lax.optimization_barrier((ends[0][0], *sums))
            stat = statistics(sums)
            q_one = normed(view_one, far_one, stat[0], stat[1])
            q_two = normed(view_two, far_two, stat[2], stat[3])
            *flat, q_one, q_two, norm_sums = lax.optimization_barrier(
                (*ends[0], *ends[1], q_one, q_two, norm_totals(q_one, q_two))
            )
            ends = [flat[:2], flat[2:]]
            arrived[-1] = [list(pair) for pair in ends]
            norm_sums = jnp.sum(lax.all_gather(norm_sums, "batch", axis=0), axis=0)
            loss, *acc = attend(q_one, q_two, stat, [view_one], [view_two], loss, None, False)
        if hop > 2:
            for blocks in arrived[:2] if hop == 3 else arrived[hop - 2 : hop - 1]:
                loss, *acc = attend(q_one, q_two, stat, *blocks, loss, acc, False)
            *flat, norm_sums, loss = lax.optimization_barrier((*ends[0], *ends[1], norm_sums, loss))
            ends = [flat[:2], flat[2:]]
            arrived[-1] = [list(pair) for pair in ends]
        if hop < hops - 1:
            ends = [
                [lax.ppermute(up, "batch", ahead), lax.ppermute(down, "batch", behind)]
                for up, down in ends
            ]
            arrived.append([list(pair) for pair in ends])
        else:
            last_one = lax.ppermute(ends[0][0], "batch", ahead)
            last_two = lax.ppermute(ends[1][1], "batch", behind)
    loss, *acc = attend(
        q_one, q_two, stat, *arrived[hops - 2], loss, acc, False, dtype=jnp.bfloat16
    )
    last_one, last_two, loss = lax.optimization_barrier((last_one, last_two, loss))
    loss, own_one, send_one, own_two, send_two, total, loss_rows = attend(
        q_one, q_two, stat, [last_one], [last_two], loss, acc, True
    )
    get_one, get_two = swapped(send_one, 1), swapped(send_two, 1)
    total = jnp.concatenate([total, loss_rows], axis=1)
    size = 1
    while size < batches:
        if size > 1:
            total = add_totals(terms)
        steps = (1, 2, 3) if size * 4 <= batches else (1,)
        terms = [total, *(swapped(total, size * step) for step in steps)]
        size *= len(terms)
    grad_one, grad_two, loss = finish_grads(
        samples, (own_one, get_one, own_two, get_two, q_one, q_two, norm_sums, stat, *terms, *terms), rows
    )
    return (grad_one, grad_two, loss)


def solution(mesh):
    placed = (P(("groups", "batch"), "feat"), P(("groups", "batch"), "feat"))
    batches = mesh.shape["batch"]
    ringed = mesh.shape["feat"] == 1 and batches >= 16 and batches & (batches - 1) == 0
    return jax.shard_map(
        ring_shards if ringed else shards,
        mesh=mesh,
        in_specs=placed,
        out_specs=(P(("groups", "batch"), "feat"), P(("groups", "batch"), "feat"), P("groups")),
        check_vma=False,
    )
```

```python
import functools

import jax
import jax.numpy as jnp
from jax import lax
from jax.experimental import pallas as pl
from jax.experimental.pallas import tpu as pltpu
from jax.sharding import PartitionSpec as P

off_weight = 0.0051
tiles = 4
vmem = 56 * 1024 * 1024
strip = 16


def local_term(columns, full_two):
    return lax.dot_general(
        columns, full_two, (((0,), (0,)), ((), ())), preferred_element_type=jnp.float32
    )


def tile_grad(summed, row_base, samples):
    corr = summed / samples
    row_ids = row_base + lax.broadcasted_iota(jnp.int32, corr.shape, 0)
    col_ids = lax.broadcasted_iota(jnp.int32, corr.shape, 1)
    diag = row_ids == col_ids
    grad = jnp.where(diag, -2.0 * (1.0 - corr), 2.0 * off_weight * corr).astype(jnp.bfloat16)
    part_loss = jnp.sum(jnp.where(diag, (1.0 - corr) ** 2, off_weight * corr * corr))
    return (grad, part_loss)


def fold_step(columns, full_two, piece):
    contrib = lax.dot_general(
        full_two, piece, (((1,), (1,)), ((), ())), preferred_element_type=jnp.float32
    )
    back_mix = jnp.dot(columns, piece, preferred_element_type=jnp.float32)
    return (contrib, back_mix)


def finish(back, normed, inv, sum_back, sum_prod, samples):
    normal_f = normed.astype(jnp.float32)
    return (inv * (back - sum_back / samples - normal_f * sum_prod / samples)).astype(jnp.bfloat16)


def shards(view_one, view_two):
    rows, half_feat = view_one.shape
    batches = lax.axis_size("batch")
    samples = rows * batches
    values_one = view_one.astype(jnp.float32)
    values_two = view_two.astype(jnp.float32)
    sums = lax.psum(
        (
            jnp.sum(values_one, axis=0),
            jnp.sum(values_one * values_one, axis=0),
            jnp.sum(values_two, axis=0),
            jnp.sum(values_two * values_two, axis=0),
        ),
        "batch",
    )
    mean_one = sums[0] / samples
    mean_two = sums[2] / samples
    inv_one = 1.0 / jnp.sqrt(sums[1] / samples - mean_one * mean_one + 1e-05)
    inv_two = 1.0 / jnp.sqrt(sums[3] / samples - mean_two * mean_two + 1e-05)
    norm_one = ((values_one - mean_one) * inv_one).astype(jnp.bfloat16)
    norm_two = ((values_two - mean_two) * inv_two).astype(jnp.bfloat16)
    full_two = lax.all_gather(norm_two, "feat", axis=1, tiled=True)
    width = full_two.shape[1]
    tile = half_feat // batches
    row_base = lax.axis_index("feat") * half_feat + lax.axis_index("batch") * tile
    summed = lax.psum_scatter(
        local_term(norm_one, full_two), "batch", scatter_dimension=0, tiled=True
    )
    grad, part_loss = tile_grad(summed, row_base, samples)
    back_one, back_mix = fold_step(
        norm_one, full_two, lax.all_gather(grad, "batch", axis=0, tiled=True)
    )
    back_two = lax.psum_scatter(back_mix, "feat", scatter_dimension=1, tiled=True)
    loss = lax.psum(part_loss, ("batch", "feat")) / width
    norm_one_f = norm_one.astype(jnp.float32)
    norm_two_f = norm_two.astype(jnp.float32)
    stats = (
        lax.psum(jnp.sum(back_one, axis=0).astype(jnp.bfloat16), "batch").astype(jnp.float32),
        lax.psum(jnp.sum(back_one * norm_one_f, axis=0).astype(jnp.bfloat16), "batch").astype(
            jnp.float32
        ),
        lax.psum(jnp.sum(back_two, axis=0).astype(jnp.bfloat16), "batch").astype(jnp.float32),
        lax.psum(jnp.sum(back_two * norm_two_f, axis=0).astype(jnp.bfloat16), "batch").astype(
            jnp.float32
        ),
    )
    grad_one = finish(back_one, norm_one, inv_one, stats[0], stats[1], samples)
    grad_two = finish(back_two, norm_two, inv_two, stats[2], stats[3], samples)
    return (grad_one, grad_two, jnp.reshape(loss, (1,)))


def added(refs):
    terms = [ref[...].astype(jnp.float32) for ref in refs]
    while len(terms) > 1:
        terms = [terms[k] + terms[k + 1] for k in range(0, len(terms), 2)]
    return terms[0]


def sums_kernel(one_ref, two_ref, out_ref):
    for index, ref in enumerate((one_ref, two_ref)):
        values = ref[...].astype(jnp.float32)
        out_ref[2 * index : 2 * index + 1, :] = jnp.sum(values, axis=0, keepdims=True)
        out_ref[2 * index + 1 : 2 * index + 2, :] = jnp.sum(values * values, axis=0, keepdims=True)


def first_sums(one, two):
    width = one.shape[1]
    return pl.pallas_call(
        sums_kernel,
        out_shape=jax.ShapeDtypeStruct((4, width), jnp.float32),
        cost_estimate=pl.CostEstimate(flops=width, bytes_accessed=width, transcendentals=0),
        name="first_sums",
    )(one, two)


def three_rows(value):
    rows = []
    for _ in range(3):
        part = value.astype(jnp.bfloat16).astype(jnp.float32)
        rows.append(part)
        value = value - part
    row = lax.broadcasted_iota(jnp.int32, (8, 128), 0)
    out = jnp.where(row == 0, rows[0], jnp.where(row == 1, rows[1], 0.0))
    return jnp.where(row == 2, rows[2], out).astype(jnp.bfloat16)


def loss_of(total):
    return (total[0:1] + total[1:2]) + total[2:3]


def halves(value):
    high = value.astype(jnp.bfloat16)
    return (high, (value - high.astype(jnp.float32)).astype(jnp.bfloat16))


def split_kernel(sums_ref, out_ref):
    out_ref[:2, :] = sums_ref[:2, :].astype(jnp.bfloat16)
    out_ref[2:3, :], out_ref[3:4, :] = halves(sums_ref[2:3, :])


def split_rows(sums):
    return pl.pallas_call(
        split_kernel, out_shape=jax.ShapeDtypeStruct(sums.shape, jnp.bfloat16), name="split_rows"
    )(sums)


def add_kernel(*refs):
    total = added(refs[:-1])
    width = total.shape[1] - 128
    out_ref = refs[-1]
    out_ref[:6, :width] = total[:6, :width].astype(jnp.bfloat16)
    out_ref[6:7, :width], out_ref[7:8, :width] = halves(total[6:7, :width] + total[7:8, :width])
    out_ref[:, width:] = three_rows(loss_of(total[:, width:]))


def attend_kernel(count, begins, ends, *refs):
    q_one, q_two, stat_ref = refs[:3]
    blocks_one = refs[3 : 3 + count]
    blocks_two = refs[3 + count : 3 + 2 * count]
    rest = list(refs[3 + 2 * count :])
    loss_in = rest.pop(0)
    acc_in = None if begins else (rest.pop(0), rest.pop(0))
    norm_rows = rest.pop(0) if ends else None
    late = rest[-8:-6] if ends else ()
    held_one, held_two, gram_one, gram_two, round_one, round_two = rest[-6:]
    fresh = rest[-9] if ends else None
    loss_out, *outs = rest[: -9 if ends else -6]
    step = pl.program_id(0)
    tile = lax.rem(step, tiles)

    @pl.when(step == 0)
    def _():
        gram_one[...] = jnp.zeros_like(gram_one)
        gram_two[...] = jnp.zeros_like(gram_two)

    @pl.when(step < tiles)
    def _():
        for kept, queries in zip(late, (q_one, q_two)):
            kept[tile] = queries[...]
        for blocks, held, mean in ((blocks_one, held_one, 0), (blocks_two, held_two, 2)):
            start = 0
            for block in blocks:
                size = block.shape[0]
                normal = (block[...].astype(jnp.float32) - stat_ref[mean : mean + 1, :]) * stat_ref[
                    mean + 1 : mean + 2, :
                ]
                held[tile, start : start + size, :] = normal.astype(jnp.bfloat16)
                start += size
        for gram, queries, held in ((gram_one, q_one, held_one), (gram_two, q_two, held_two)):
            gram[...] += lax.dot_general(
                queries[...], held[tile], (((1,), (1,)), ((), ())), preferred_element_type=jnp.float32
            )

    @pl.when(step == tiles)
    def _():
        both = gram_one[...] * gram_two[...]
        height, width = both.shape
        folded = jnp.sum(both.reshape(height // 8, 8, width), axis=0)
        loss_out[...] = loss_in[...] + jnp.sum(folded) * (1.0 / 1024)
        round_one[...] = gram_one[...].astype(jnp.bfloat16)
        round_two[...] = gram_two[...].astype(jnp.bfloat16)

    @pl.when(step >= tiles)
    def _():
        sums = []
        for index, (gram, held) in enumerate(((round_two, held_one), (round_one, held_two))):
            if not ends:
                total = jnp.dot(gram[...], held[tile], preferred_element_type=jnp.float32)
                if not begins:
                    total += acc_in[index][...].astype(jnp.float32)
                outs[index][...] = total.astype(outs[index].dtype)
                continue
            fresh[...] = jnp.dot(gram[...], held[tile], preferred_element_type=jnp.float32)
            height, lanes = fresh.shape
            share = height // 2
            plain = jnp.zeros((8, lanes), jnp.float32)
            prods = jnp.zeros((8, lanes), jnp.float32)
            for start in range(0, height, strip):
                rows = slice(start, start + strip)
                total = fresh[rows, :] + acc_in[index][rows, :].astype(jnp.float32)
                prod = total * late[index][tile, rows, :].astype(jnp.float32)
                plain += jnp.sum(total.reshape(strip // 8, 8, lanes), axis=0)
                prods += jnp.sum(prod.reshape(strip // 8, 8, lanes), axis=0)
                place = start % share
                out = outs[2 * index + start // share]
                out[place : place + strip, :] = total.astype(jnp.bfloat16)
            sums.append(jnp.sum(plain, axis=0, keepdims=True))
            sums.append(jnp.sum(prods, axis=0, keepdims=True))
        if ends:
            for index, value in enumerate(sums):
                outs[4][index : index + 1, :] = value.astype(jnp.bfloat16)
            outs[4][4:, :] = norm_rows[...]
            outs[5][...] = three_rows(jnp.zeros((1, 128), jnp.float32) + jnp.sum(loss_out[...]))


def attend(
    q_one, q_two, stat, blocks_one, blocks_two, loss, acc, ends, dtype=jnp.float32, norm_rows=None
):
    rows, width = q_one.shape
    lanes = width // tiles
    keys = sum(block.shape[0] for block in blocks_one)
    count = len(blocks_one)
    begins = acc is None
    early = lambda step: (0, jnp.minimum(step, tiles - 1))
    late = lambda step: (0, jnp.maximum(step - tiles, 0))
    fixed = pl.BlockSpec((8, 128), lambda step: (0, 0))
    operands = [q_one, q_two, stat, *blocks_one, *blocks_two, loss]
    in_specs = [pl.BlockSpec((rows, lanes), early)] * 2 + [pl.BlockSpec((4, lanes), early)]
    in_specs += [pl.BlockSpec((block.shape[0], lanes), early) for block in blocks_one] * 2
    in_specs.append(fixed)
    out_specs = [fixed]
    out_shape = [jax.ShapeDtypeStruct((8, 128), jnp.float32)]
    aliases = {3 + 2 * count: 0}
    if not begins:
        operands += list(acc)
        in_specs += [pl.BlockSpec((rows, lanes), late)] * 2
    if ends:
        operands.append(norm_rows)
        in_specs.append(pl.BlockSpec((4, lanes), late))
        out_specs += [pl.BlockSpec((rows // 2, lanes), late)] * 4
        out_shape += [
            jax.ShapeDtypeStruct((rows // 2, width), jnp.bfloat16),
            jax.ShapeDtypeStruct((rows // 2, width), jnp.bfloat16),
        ] * 2
        out_specs += [pl.BlockSpec((8, lanes), late), pl.BlockSpec((8, 128), lambda step: (0, 0))]
        out_shape += [jax.ShapeDtypeStruct((8, size), jnp.bfloat16) for size in (width, 128)]
    else:
        if not begins and dtype == jnp.float32:
            aliases.update({4 + 2 * count: 1, 5 + 2 * count: 2})
        out_specs += [pl.BlockSpec((rows, lanes), late)] * 2
        out_shape += [jax.ShapeDtypeStruct((rows, width), dtype)] * 2
    return pl.pallas_call(
        functools.partial(attend_kernel, count, begins, ends),
        grid=(2 * tiles,),
        in_specs=in_specs,
        out_specs=out_specs,
        out_shape=out_shape,
        scratch_shapes=[pltpu.VMEM((rows, lanes), jnp.float32)] * (1 if ends else 0)
        + [pltpu.VMEM((tiles, rows, lanes), jnp.bfloat16)] * (2 if ends else 0)
        + [pltpu.VMEM((tiles, keys, lanes), jnp.bfloat16)] * 2
        + [pltpu.VMEM((rows, keys), jnp.float32)] * 2
        + [pltpu.VMEM((rows, keys), jnp.bfloat16)] * 2,
        input_output_aliases=aliases,
        compiler_params=pltpu.CompilerParams(vmem_limit_bytes=vmem),
        cost_estimate=pl.CostEstimate(flops=width, bytes_accessed=width, transcendentals=0),
        name="attend",
    )(*operands)


def finish_kernel(
    samples, full, own_one, get_one, own_two, get_two, norm_one, norm_two, stat_ref, *rest
):
    outs = rest[-3:]
    count = (len(rest) - 3) // 2
    scale = 2.0 * off_weight / samples
    total = added(rest[:count])
    mixed = total[6:7] + total[7:8]
    corr = mixed / samples
    diag = (-2.0 * (1.0 - corr)).astype(jnp.bfloat16).astype(jnp.float32) - 2.0 * off_weight * corr
    squares = jnp.max(loss_of(added(rest[count:-3])))
    part = jnp.sum((1.0 - corr) ** 2 - off_weight * corr * corr)

    @pl.when(pl.program_id(0) == 0)
    def _():
        outs[2][0] = squares * (off_weight / (samples * samples * full))

    outs[2][0] += part / full
    for index, (own, get, mine, other, inv_row) in enumerate(
        ((own_one, get_one, norm_one, norm_two, 1), (own_two, get_two, norm_two, norm_one, 3))
    ):
        inv = stat_ref[inv_row : inv_row + 1, :]
        sum_back = scale * total[2 * index : 2 * index + 1, :]
        sum_back += total[5 - index : 6 - index, :] * diag
        sum_prod = scale * total[2 * index + 1 : 2 * index + 2, :] + mixed * diag
        by_acc, by_other = inv * scale, inv * diag
        minus, by_mine = inv * sum_back / samples, inv * sum_prod / samples
        for start in range(0, own.shape[0], strip):
            rows = slice(start, start + strip)
            grad = by_acc * (own[rows, :].astype(jnp.float32) + get[rows, :].astype(jnp.float32))
            grad += by_other * other[rows, :].astype(jnp.float32) - minus
            grad -= by_mine * mine[rows, :].astype(jnp.float32)
            outs[index][rows, :] = grad.astype(jnp.bfloat16)


def add_totals(terms):
    return pl.pallas_call(
        add_kernel,
        out_shape=jax.ShapeDtypeStruct(terms[0].shape, jnp.bfloat16),
        cost_estimate=pl.CostEstimate(flops=1, bytes_accessed=1, transcendentals=0),
        name="add_totals",
    )(*terms)


def finish_grads(samples, operands, rows):
    width = operands[0].shape[1]
    lanes = width // tiles
    count = (len(operands) - 7) // 2
    heights = (*((rows,) * 6), 4) + (8,) * count
    place = lambda step: (0, step)
    return pl.pallas_call(
        functools.partial(finish_kernel, samples, width),
        grid=(tiles,),
        in_specs=[pl.BlockSpec((height, lanes), place) for height in heights]
        + [pl.BlockSpec((8, 128), lambda step: (0, width // 128))] * count,
        out_specs=[pl.BlockSpec((rows, lanes), place)] * 2
        + [pl.BlockSpec(memory_space=pltpu.SMEM)],
        out_shape=[jax.ShapeDtypeStruct((rows, width), jnp.bfloat16)] * 2
        + [jax.ShapeDtypeStruct((1,), jnp.float32)],
        compiler_params=pltpu.CompilerParams(vmem_limit_bytes=vmem),
        cost_estimate=pl.CostEstimate(flops=width, bytes_accessed=width, transcendentals=0),
        name="finish",
    )(*operands)


def ring_shards(view_one, view_two):
    rows, width = view_one.shape
    batches = lax.axis_size("batch")
    samples = rows * batches
    chips = batches // 2
    hops = chips // 2
    line = chips // 2
    order = [2 * r for r in range(line)] + [2 * r + 1 for r in reversed(range(line))]
    ahead = [
        (2 * order[r] + c, 2 * order[(r + 1) % chips] + c) for r in range(chips) for c in range(2)
    ]
    behind = [(there, here) for here, there in ahead]

    def swapped(value, bit):
        return lax.ppermute(value, "batch", [(i, i ^ bit) for i in range(batches)])

    def norm_totals(q_one, q_two):
        one, two = (q[:rows].astype(jnp.float32) for q in (q_one, q_two))
        sums = [jnp.sum(one, axis=0), jnp.sum(two, axis=0), jnp.sum(one * two, axis=0)]
        return jnp.stack([*sums, jnp.zeros_like(sums[0])])

    def statistics(sums):
        sums = [value / samples for value in sums]
        inv_one = 1.0 / jnp.sqrt(sums[1] - sums[0] * sums[0] + 1e-05)
        inv_two = 1.0 / jnp.sqrt(sums[3] - sums[2] * sums[2] + 1e-05)
        return jnp.stack([sums[0], inv_one, sums[2], inv_two])

    def normed(view, far, mean, inv):
        both = jnp.concatenate([view, far], axis=0).astype(jnp.float32)
        return ((both - mean) * inv).astype(jnp.bfloat16)

    sums = first_sums(view_one, view_two)
    sums = lax.psum(tuple(sums[row] for row in range(4)), "batch")
    far_one, far_two = swapped(view_one, 1), swapped(view_two, 1)
    ends = [[view_one, view_one], [view_two, view_two]]
    arrived = []
    loss = jnp.zeros((8, 128), jnp.float32)
    for hop in range(hops):
        if hop == 2:
            ends[0][0], *sums = lax.optimization_barrier((ends[0][0], *sums))
            stat = statistics(sums)
            q_one = normed(view_one, far_one, stat[0], stat[1])
            q_two = normed(view_two, far_two, stat[2], stat[3])
            *flat, q_one, q_two, norm_sums = lax.optimization_barrier(
                (*ends[0], *ends[1], q_one, q_two, norm_totals(q_one, q_two))
            )
            ends = [flat[:2], flat[2:]]
            arrived[-1] = [list(pair) for pair in ends]
            norm_sums = split_rows(norm_sums)
            loss, *acc = attend(q_one, q_two, stat, [view_one], [view_two], loss, None, False)
        if hop > 2:
            for blocks in arrived[:2] if hop == 3 else arrived[hop - 2 : hop - 1]:
                loss, *acc = attend(q_one, q_two, stat, *blocks, loss, acc, False)
            *flat, norm_sums, loss = lax.optimization_barrier((*ends[0], *ends[1], norm_sums, loss))
            ends = [flat[:2], flat[2:]]
            arrived[-1] = [list(pair) for pair in ends]
        if hop < hops - 1:
            ends = [
                [lax.ppermute(up, "batch", ahead), lax.ppermute(down, "batch", behind)]
                for up, down in ends
            ]
            arrived.append([list(pair) for pair in ends])
        else:
            last_one = lax.ppermute(ends[0][0], "batch", ahead)
            last_two = lax.ppermute(ends[1][1], "batch", behind)
    loss, *acc = attend(
        q_one, q_two, stat, *arrived[hops - 2], loss, acc, False, dtype=jnp.bfloat16
    )
    last_one, last_two, loss = lax.optimization_barrier((last_one, last_two, loss))
    loss, own_one, send_one, own_two, send_two, total, loss_rows = attend(
        q_one, q_two, stat, [last_one], [last_two], loss, acc, True, norm_rows=norm_sums
    )
    get_one, get_two = swapped(send_one, 1), swapped(send_two, 1)
    total = jnp.concatenate([total, loss_rows], axis=1)
    size = 1
    while size < batches:
        if size > 1:
            total = add_totals(terms)
        steps = (1, 2, 3) if size * 4 <= batches else (1,)
        terms = [total, *(swapped(total, size * step) for step in steps)]
        size *= len(terms)
    grad_one, grad_two, loss = finish_grads(
        samples, (own_one, get_one, own_two, get_two, q_one, q_two, stat, *terms, *terms), rows
    )
    return (grad_one, grad_two, loss)


def solution(mesh):
    placed = (P(("groups", "batch"), "feat"), P(("groups", "batch"), "feat"))
    batches = mesh.shape["batch"]
    ringed = mesh.shape["feat"] == 1 and batches >= 16 and batches & (batches - 1) == 0
    return jax.shard_map(
        ring_shards if ringed else shards,
        mesh=mesh,
        in_specs=placed,
        out_specs=(P(("groups", "batch"), "feat"), P(("groups", "batch"), "feat"), P("groups")),
        check_vma=False,
    )
```

```python
import functools

import jax
import jax.numpy as jnp
from jax import lax
from jax.experimental import pallas as pl
from jax.experimental.pallas import tpu as pltpu
from jax.sharding import PartitionSpec as P

off_weight = 0.0051
tiles = 2
vmem = 56 * 1024 * 1024
strip = 16


def local_term(columns, full_two):
    return lax.dot_general(
        columns, full_two, (((0,), (0,)), ((), ())), preferred_element_type=jnp.float32
    )


def tile_grad(summed, row_base, samples):
    corr = summed / samples
    row_ids = row_base + lax.broadcasted_iota(jnp.int32, corr.shape, 0)
    col_ids = lax.broadcasted_iota(jnp.int32, corr.shape, 1)
    diag = row_ids == col_ids
    grad = jnp.where(diag, -2.0 * (1.0 - corr), 2.0 * off_weight * corr).astype(jnp.bfloat16)
    part_loss = jnp.sum(jnp.where(diag, (1.0 - corr) ** 2, off_weight * corr * corr))
    return (grad, part_loss)


def fold_step(columns, full_two, piece):
    contrib = lax.dot_general(
        full_two, piece, (((1,), (1,)), ((), ())), preferred_element_type=jnp.float32
    )
    back_mix = jnp.dot(columns, piece, preferred_element_type=jnp.float32)
    return (contrib, back_mix)


def finish(back, normed, inv, sum_back, sum_prod, samples):
    normal_f = normed.astype(jnp.float32)
    return (inv * (back - sum_back / samples - normal_f * sum_prod / samples)).astype(jnp.bfloat16)


def shards(view_one, view_two):
    rows, half_feat = view_one.shape
    batches = lax.axis_size("batch")
    samples = rows * batches
    values_one = view_one.astype(jnp.float32)
    values_two = view_two.astype(jnp.float32)
    sums = lax.psum(
        (
            jnp.sum(values_one, axis=0),
            jnp.sum(values_one * values_one, axis=0),
            jnp.sum(values_two, axis=0),
            jnp.sum(values_two * values_two, axis=0),
        ),
        "batch",
    )
    mean_one = sums[0] / samples
    mean_two = sums[2] / samples
    inv_one = 1.0 / jnp.sqrt(sums[1] / samples - mean_one * mean_one + 1e-05)
    inv_two = 1.0 / jnp.sqrt(sums[3] / samples - mean_two * mean_two + 1e-05)
    norm_one = ((values_one - mean_one) * inv_one).astype(jnp.bfloat16)
    norm_two = ((values_two - mean_two) * inv_two).astype(jnp.bfloat16)
    full_two = lax.all_gather(norm_two, "feat", axis=1, tiled=True)
    width = full_two.shape[1]
    tile = half_feat // batches
    row_base = lax.axis_index("feat") * half_feat + lax.axis_index("batch") * tile
    summed = lax.psum_scatter(
        local_term(norm_one, full_two), "batch", scatter_dimension=0, tiled=True
    )
    grad, part_loss = tile_grad(summed, row_base, samples)
    back_one, back_mix = fold_step(
        norm_one, full_two, lax.all_gather(grad, "batch", axis=0, tiled=True)
    )
    back_two = lax.psum_scatter(back_mix, "feat", scatter_dimension=1, tiled=True)
    loss = lax.psum(part_loss, ("batch", "feat")) / width
    norm_one_f = norm_one.astype(jnp.float32)
    norm_two_f = norm_two.astype(jnp.float32)
    stats = (
        lax.psum(jnp.sum(back_one, axis=0).astype(jnp.bfloat16), "batch").astype(jnp.float32),
        lax.psum(jnp.sum(back_one * norm_one_f, axis=0).astype(jnp.bfloat16), "batch").astype(
            jnp.float32
        ),
        lax.psum(jnp.sum(back_two, axis=0).astype(jnp.bfloat16), "batch").astype(jnp.float32),
        lax.psum(jnp.sum(back_two * norm_two_f, axis=0).astype(jnp.bfloat16), "batch").astype(
            jnp.float32
        ),
    )
    grad_one = finish(back_one, norm_one, inv_one, stats[0], stats[1], samples)
    grad_two = finish(back_two, norm_two, inv_two, stats[2], stats[3], samples)
    return (grad_one, grad_two, jnp.reshape(loss, (1,)))


def added(refs):
    terms = [ref[...].astype(jnp.float32) for ref in refs]
    while len(terms) > 1:
        terms = [terms[k] + terms[k + 1] for k in range(0, len(terms), 2)]
    return terms[0]


def sums_kernel(one_ref, two_ref, out_ref):
    for index, ref in enumerate((one_ref, two_ref)):
        values = ref[...].astype(jnp.float32)
        out_ref[2 * index : 2 * index + 1, :] = jnp.sum(values, axis=0, keepdims=True)
        out_ref[2 * index + 1 : 2 * index + 2, :] = jnp.sum(values * values, axis=0, keepdims=True)


def first_sums(one, two):
    width = one.shape[1]
    return pl.pallas_call(
        sums_kernel,
        out_shape=jax.ShapeDtypeStruct((4, width), jnp.float32),
        cost_estimate=pl.CostEstimate(flops=width, bytes_accessed=width, transcendentals=0),
        name="first_sums",
    )(one, two)


def three_rows(value):
    rows = []
    for _ in range(3):
        part = value.astype(jnp.bfloat16).astype(jnp.float32)
        rows.append(part)
        value = value - part
    row = lax.broadcasted_iota(jnp.int32, (8, 128), 0)
    out = jnp.where(row == 0, rows[0], jnp.where(row == 1, rows[1], 0.0))
    return jnp.where(row == 2, rows[2], out).astype(jnp.bfloat16)


def loss_of(total):
    return (total[0:1] + total[1:2]) + total[2:3]


def halves(value):
    high = value.astype(jnp.bfloat16)
    return (high, (value - high.astype(jnp.float32)).astype(jnp.bfloat16))


def split_kernel(sums_ref, out_ref):
    out_ref[:2, :] = sums_ref[:2, :].astype(jnp.bfloat16)
    out_ref[2:3, :], out_ref[3:4, :] = halves(sums_ref[2:3, :])


def split_rows(sums):
    return pl.pallas_call(
        split_kernel, out_shape=jax.ShapeDtypeStruct(sums.shape, jnp.bfloat16), name="split_rows"
    )(sums)


def add_kernel(*refs):
    total = added(refs[:-1])
    width = total.shape[1] - 128
    out_ref = refs[-1]
    out_ref[:6, :width] = total[:6, :width].astype(jnp.bfloat16)
    out_ref[6:7, :width], out_ref[7:8, :width] = halves(total[6:7, :width] + total[7:8, :width])
    out_ref[:, width:] = three_rows(loss_of(total[:, width:]))


def attend_kernel(count, begins, ends, *refs):
    q_one, q_two, stat_ref = refs[:3]
    blocks_one = refs[3 : 3 + count]
    blocks_two = refs[3 + count : 3 + 2 * count]
    rest = list(refs[3 + 2 * count :])
    loss_in = rest.pop(0)
    acc_in = None if begins else (rest.pop(0), rest.pop(0))
    norm_rows = rest.pop(0) if ends else None
    late = rest[-8:-6] if ends else ()
    held_one, held_two, gram_one, gram_two, round_one, round_two = rest[-6:]
    fresh = rest[-9] if ends else None
    loss_out, *outs = rest[: -9 if ends else -6]
    step = pl.program_id(0)
    tile = lax.rem(step, tiles)

    @pl.when(step == 0)
    def _():
        gram_one[...] = jnp.zeros_like(gram_one)
        gram_two[...] = jnp.zeros_like(gram_two)

    @pl.when(step < tiles)
    def _():
        for kept, queries in zip(late, (q_one, q_two)):
            kept[tile] = queries[...]
        for blocks, held, mean in ((blocks_one, held_one, 0), (blocks_two, held_two, 2)):
            start = 0
            for block in blocks:
                size = block.shape[0]
                normal = (block[...].astype(jnp.float32) - stat_ref[mean : mean + 1, :]) * stat_ref[
                    mean + 1 : mean + 2, :
                ]
                held[tile, start : start + size, :] = normal.astype(jnp.bfloat16)
                start += size
        for gram, queries, held in ((gram_one, q_one, held_one), (gram_two, q_two, held_two)):
            gram[...] += lax.dot_general(
                queries[...], held[tile], (((1,), (1,)), ((), ())), preferred_element_type=jnp.float32
            )

    @pl.when(step == tiles)
    def _():
        both = gram_one[...] * gram_two[...]
        height, width = both.shape
        folded = jnp.sum(both.reshape(height // 8, 8, width), axis=0)
        loss_out[...] = loss_in[...] + jnp.sum(folded) * (1.0 / 1024)
        round_one[...] = gram_one[...].astype(jnp.bfloat16)
        round_two[...] = gram_two[...].astype(jnp.bfloat16)

    @pl.when(step >= tiles)
    def _():
        sums = []
        for index, (gram, held) in enumerate(((round_two, held_one), (round_one, held_two))):
            if not ends:
                total = jnp.dot(gram[...], held[tile], preferred_element_type=jnp.float32)
                if not begins:
                    total += acc_in[index][...].astype(jnp.float32)
                outs[index][...] = total.astype(outs[index].dtype)
                continue
            fresh[...] = jnp.dot(gram[...], held[tile], preferred_element_type=jnp.float32)
            height, lanes = fresh.shape
            share = height // 2
            plain = jnp.zeros((8, lanes), jnp.float32)
            prods = jnp.zeros((8, lanes), jnp.float32)
            for start in range(0, height, strip):
                rows = slice(start, start + strip)
                total = fresh[rows, :] + acc_in[index][rows, :].astype(jnp.float32)
                prod = total * late[index][tile, rows, :].astype(jnp.float32)
                plain += jnp.sum(total.reshape(strip // 8, 8, lanes), axis=0)
                prods += jnp.sum(prod.reshape(strip // 8, 8, lanes), axis=0)
                place = start % share
                out = outs[2 * index + start // share]
                out[place : place + strip, :] = total.astype(jnp.bfloat16)
            sums.append(jnp.sum(plain, axis=0, keepdims=True))
            sums.append(jnp.sum(prods, axis=0, keepdims=True))
        if ends:
            for index, value in enumerate(sums):
                outs[4][index : index + 1, :] = value.astype(jnp.bfloat16)
            outs[4][4:, :] = norm_rows[...]
            outs[5][...] = three_rows(jnp.zeros((1, 128), jnp.float32) + jnp.sum(loss_out[...]))


def attend(
    q_one, q_two, stat, blocks_one, blocks_two, loss, acc, ends, dtype=jnp.float32, norm_rows=None
):
    rows, width = q_one.shape
    lanes = width // tiles
    keys = sum(block.shape[0] for block in blocks_one)
    count = len(blocks_one)
    begins = acc is None
    early = lambda step: (0, jnp.minimum(step, tiles - 1))
    late = lambda step: (0, jnp.maximum(step - tiles, 0))
    fixed = pl.BlockSpec((8, 128), lambda step: (0, 0))
    operands = [q_one, q_two, stat, *blocks_one, *blocks_two, loss]
    in_specs = [pl.BlockSpec((rows, lanes), early)] * 2 + [pl.BlockSpec((4, lanes), early)]
    in_specs += [pl.BlockSpec((block.shape[0], lanes), early) for block in blocks_one] * 2
    in_specs.append(fixed)
    out_specs = [fixed]
    out_shape = [jax.ShapeDtypeStruct((8, 128), jnp.float32)]
    aliases = {3 + 2 * count: 0}
    if not begins:
        operands += list(acc)
        in_specs += [pl.BlockSpec((rows, lanes), late)] * 2
    if ends:
        operands.append(norm_rows)
        in_specs.append(pl.BlockSpec((4, lanes), late))
        out_specs += [pl.BlockSpec((rows // 2, lanes), late)] * 4
        out_shape += [
            jax.ShapeDtypeStruct((rows // 2, width), jnp.bfloat16),
            jax.ShapeDtypeStruct((rows // 2, width), jnp.bfloat16),
        ] * 2
        out_specs += [pl.BlockSpec((8, lanes), late), pl.BlockSpec((8, 128), lambda step: (0, 0))]
        out_shape += [jax.ShapeDtypeStruct((8, size), jnp.bfloat16) for size in (width, 128)]
    else:
        if not begins and dtype == jnp.float32:
            aliases.update({4 + 2 * count: 1, 5 + 2 * count: 2})
        out_specs += [pl.BlockSpec((rows, lanes), late)] * 2
        out_shape += [jax.ShapeDtypeStruct((rows, width), dtype)] * 2
    return pl.pallas_call(
        functools.partial(attend_kernel, count, begins, ends),
        grid=(2 * tiles,),
        in_specs=in_specs,
        out_specs=out_specs,
        out_shape=out_shape,
        scratch_shapes=[pltpu.VMEM((rows, lanes), jnp.float32)] * (1 if ends else 0)
        + [pltpu.VMEM((tiles, rows, lanes), jnp.bfloat16)] * (2 if ends else 0)
        + [pltpu.VMEM((tiles, keys, lanes), jnp.bfloat16)] * 2
        + [pltpu.VMEM((rows, keys), jnp.float32)] * 2
        + [pltpu.VMEM((rows, keys), jnp.bfloat16)] * 2,
        input_output_aliases=aliases,
        compiler_params=pltpu.CompilerParams(vmem_limit_bytes=vmem),
        cost_estimate=pl.CostEstimate(flops=width, bytes_accessed=width, transcendentals=0),
        name="attend",
    )(*operands)


def finish_kernel(
    samples, full, own_one, get_one, own_two, get_two, norm_one, norm_two, stat_ref, *rest
):
    outs = rest[-3:]
    count = (len(rest) - 3) // 2
    scale = 2.0 * off_weight / samples
    total = added(rest[:count])
    mixed = total[6:7] + total[7:8]
    corr = mixed / samples
    diag = (-2.0 * (1.0 - corr)).astype(jnp.bfloat16).astype(jnp.float32) - 2.0 * off_weight * corr
    squares = jnp.max(loss_of(added(rest[count:-3])))
    part = jnp.sum((1.0 - corr) ** 2 - off_weight * corr * corr)

    @pl.when(pl.program_id(0) == 0)
    def _():
        outs[2][0] = squares * (off_weight / (samples * samples * full))

    outs[2][0] += part / full
    for index, (own, get, mine, other, inv_row) in enumerate(
        ((own_one, get_one, norm_one, norm_two, 1), (own_two, get_two, norm_two, norm_one, 3))
    ):
        inv = stat_ref[inv_row : inv_row + 1, :]
        sum_back = scale * total[2 * index : 2 * index + 1, :]
        sum_back += total[5 - index : 6 - index, :] * diag
        sum_prod = scale * total[2 * index + 1 : 2 * index + 2, :] + mixed * diag
        by_acc, by_other = inv * scale, inv * diag
        minus, by_mine = inv * sum_back / samples, inv * sum_prod / samples
        for start in range(0, own.shape[0], strip):
            rows = slice(start, start + strip)
            grad = by_acc * (own[rows, :].astype(jnp.float32) + get[rows, :].astype(jnp.float32))
            grad += by_other * other[rows, :].astype(jnp.float32) - minus
            grad -= by_mine * mine[rows, :].astype(jnp.float32)
            outs[index][rows, :] = grad.astype(jnp.bfloat16)


def add_totals(terms):
    return pl.pallas_call(
        add_kernel,
        out_shape=jax.ShapeDtypeStruct(terms[0].shape, jnp.bfloat16),
        cost_estimate=pl.CostEstimate(flops=1, bytes_accessed=1, transcendentals=0),
        name="add_totals",
    )(*terms)


def finish_grads(samples, operands, rows):
    width = operands[0].shape[1]
    lanes = width // tiles
    count = (len(operands) - 7) // 2
    heights = (*((rows,) * 6), 4) + (8,) * count
    place = lambda step: (0, step)
    return pl.pallas_call(
        functools.partial(finish_kernel, samples, width),
        grid=(tiles,),
        in_specs=[pl.BlockSpec((height, lanes), place) for height in heights]
        + [pl.BlockSpec((8, 128), lambda step: (0, width // 128))] * count,
        out_specs=[pl.BlockSpec((rows, lanes), place)] * 2
        + [pl.BlockSpec(memory_space=pltpu.SMEM)],
        out_shape=[jax.ShapeDtypeStruct((rows, width), jnp.bfloat16)] * 2
        + [jax.ShapeDtypeStruct((1,), jnp.float32)],
        compiler_params=pltpu.CompilerParams(vmem_limit_bytes=vmem),
        cost_estimate=pl.CostEstimate(flops=width, bytes_accessed=width, transcendentals=0),
        name="finish",
    )(*operands)


def ring_shards(view_one, view_two):
    rows, width = view_one.shape
    batches = lax.axis_size("batch")
    samples = rows * batches
    chips = batches // 2
    hops = chips // 2
    line = chips // 2
    order = [2 * r for r in range(line)] + [2 * r + 1 for r in reversed(range(line))]
    ahead = [
        (2 * order[r] + c, 2 * order[(r + 1) % chips] + c) for r in range(chips) for c in range(2)
    ]
    behind = [(there, here) for here, there in ahead]

    def swapped(value, bit):
        return lax.ppermute(value, "batch", [(i, i ^ bit) for i in range(batches)])

    def norm_totals(q_one, q_two):
        one, two = (q[:rows].astype(jnp.float32) for q in (q_one, q_two))
        sums = [jnp.sum(one, axis=0), jnp.sum(two, axis=0), jnp.sum(one * two, axis=0)]
        return jnp.stack([*sums, jnp.zeros_like(sums[0])])

    def statistics(sums):
        sums = [value / samples for value in sums]
        inv_one = 1.0 / jnp.sqrt(sums[1] - sums[0] * sums[0] + 1e-05)
        inv_two = 1.0 / jnp.sqrt(sums[3] - sums[2] * sums[2] + 1e-05)
        return jnp.stack([sums[0], inv_one, sums[2], inv_two])

    def normed(view, far, mean, inv):
        both = jnp.concatenate([view, far], axis=0).astype(jnp.float32)
        return ((both - mean) * inv).astype(jnp.bfloat16)

    sums = first_sums(view_one, view_two)
    sums = lax.psum(tuple(sums[row] for row in range(4)), "batch")
    far_one, far_two = swapped(view_one, 1), swapped(view_two, 1)
    ends = [[view_one, view_one], [view_two, view_two]]
    arrived = []
    loss = jnp.zeros((8, 128), jnp.float32)
    for hop in range(hops):
        if hop == 2:
            ends[0][0], *sums = lax.optimization_barrier((ends[0][0], *sums))
            stat = statistics(sums)
            q_one = normed(view_one, far_one, stat[0], stat[1])
            q_two = normed(view_two, far_two, stat[2], stat[3])
            *flat, q_one, q_two, norm_sums = lax.optimization_barrier(
                (*ends[0], *ends[1], q_one, q_two, norm_totals(q_one, q_two))
            )
            ends = [flat[:2], flat[2:]]
            arrived[-1] = [list(pair) for pair in ends]
            norm_sums = split_rows(norm_sums)
            loss, *acc = attend(q_one, q_two, stat, [view_one], [view_two], loss, None, False)
        if hop > 2:
            for blocks in arrived[:2] if hop == 3 else arrived[hop - 2 : hop - 1]:
                loss, *acc = attend(q_one, q_two, stat, *blocks, loss, acc, False)
            *flat, norm_sums, loss = lax.optimization_barrier((*ends[0], *ends[1], norm_sums, loss))
            ends = [flat[:2], flat[2:]]
            arrived[-1] = [list(pair) for pair in ends]
        if hop < hops - 1:
            ends = [
                [lax.ppermute(up, "batch", ahead), lax.ppermute(down, "batch", behind)]
                for up, down in ends
            ]
            arrived.append([list(pair) for pair in ends])
        else:
            last_one = lax.ppermute(ends[0][0], "batch", ahead)
            last_two = lax.ppermute(ends[1][1], "batch", behind)
    loss, *acc = attend(
        q_one, q_two, stat, *arrived[hops - 2], loss, acc, False, dtype=jnp.bfloat16
    )
    last_one, last_two, loss = lax.optimization_barrier((last_one, last_two, loss))
    loss, own_one, send_one, own_two, send_two, total, loss_rows = attend(
        q_one, q_two, stat, [last_one], [last_two], loss, acc, True, norm_rows=norm_sums
    )
    get_one, get_two = swapped(send_one, 1), swapped(send_two, 1)
    total = jnp.concatenate([total, loss_rows], axis=1)
    size = 1
    while size < batches:
        if size > 1:
            total = add_totals(terms)
        steps = (1, 2, 3) if size * 4 <= batches else (1,)
        terms = [total, *(swapped(total, size * step) for step in steps)]
        size *= len(terms)
    grad_one, grad_two, loss = finish_grads(
        samples, (own_one, get_one, own_two, get_two, q_one, q_two, stat, *terms, *terms), rows
    )
    return (grad_one, grad_two, loss)


def solution(mesh):
    placed = (P(("groups", "batch"), "feat"), P(("groups", "batch"), "feat"))
    batches = mesh.shape["batch"]
    ringed = mesh.shape["feat"] == 1 and batches >= 16 and batches & (batches - 1) == 0
    return jax.shard_map(
        ring_shards if ringed else shards,
        mesh=mesh,
        in_specs=placed,
        out_specs=(P(("groups", "batch"), "feat"), P(("groups", "batch"), "feat"), P("groups")),
        check_vma=False,
    )
```
